32 devices in a mesh: gx: 16 (over z, y, core), gy: 2 (over x).
Axes of the slice: x: 2, y: 2, z: 4, core: 2. Of those that a mesh axis runs over, the one named last changes fastest.
Arguments:
- velocity: float32 [3, 512, 256, 128], P(None, 'gx', 'gy'), may hold values from -6 to 6
- stress: float32 [6, 512, 256, 128], P(None, 'gx', 'gy'), may hold values from -6 to 6
- lame_lambda: bfloat16 [512, 256, 128], P('gx', 'gy'), may hold values from 0.5 to 1.5
- shear_modulus: bfloat16 [512, 256, 128], P('gx', 'gy'), may hold values from 0.29882812 to 1
- buoyancy: bfloat16 [512, 256, 128], P('gx', 'gy'), may hold values from 0.5 to 1.5
- source_p: bfloat16 [3, 512, 256, 128], P(None, 'gx', 'gy'), may hold values from -6 to 6
- source_s: bfloat16 [3, 512, 256, 128], P(None, 'gx', 'gy'), may hold values from -6 to 6
Outputs:
- image_p: float32 [512, 256, 128], P('gx', 'gy')
- image_s: float32 [512, 256, 128], P('gx', 'gy')
The draws below stay inside these ranges and needn't reach their ends.
All inputs are finite; a program needn't handle non-finite values.
Results may differ from the reference program's by a relative error of at most 0.0003.
Values sent between devices are 32-bit elements; how exact they have to be, the bound alone decides.
No kernel may reach another device: no remote copies, remote signals or barrier semaphores. Data moves between devices by JAX's collectives and lax.ppermute only.
A program may use at most 128 MiB of HBM per device.

```python
import jax
import jax.numpy as jnp
from jax import lax

NX = 512
NY = 256
NZ = 128
STEPS = 2


def draw_velocity(key, part):
    noise_key = jax.random.fold_in(jax.random.fold_in(key, 11), 0)
    rough = jax.random.normal(noise_key, (3, NX, NY, NZ), jnp.float32)
    return jnp.clip(rough, -6.0, 6.0)


def block_levels(own_key, shape, cuts, least, high):
    gain = 1.0
    for position, shards_of in cuts:
        heights = jax.random.uniform(jax.random.fold_in(jax.random.fold_in(own_key, 6), position), (shards_of,), jnp.float32, least / len(cuts), high / len(cuts))
        gain = gain * jnp.repeat(jnp.exp(heights), shape[position] // shards_of).reshape((-1,) + (1,) * (len(shape) - 1 - position))
    return gain


def centred(stream_key, dims, spread, most, pieces=(), kind=jnp.bfloat16):
    values = jax.random.normal(stream_key, dims, jnp.float32) * spread
    if len(pieces) > 0:
        values = block_levels(stream_key, dims, pieces, -0.22, 0.18) * values
    return jnp.clip(values, min=-most, max=most).astype(kind)


def setup_inputs(seed: int = 0) -> dict:
    key_list = jax.random.split(jax.random.key(seed), 8)
    velocity = draw_velocity(jax.random.fold_in(key_list[7], 71), 0)
    stress = centred(key_list[1], (6, NX, NY, NZ), 1.0, 6.0, ((1, 16), (2, 2)), jnp.float32)
    lame_lambda = jnp.clip(0.5 + 1.0 * jax.random.uniform(key_list[2], (NX, NY, NZ), jnp.float32) ** block_levels(key_list[2], (NX, NY, NZ), ((0, 16), (1, 2)), -0.2, 0.2), 0.5, 1.5).astype(jnp.bfloat16)
    shear_modulus = jnp.clip(0.29882812 + 0.7011719 * jax.random.uniform(key_list[3], (NX, NY, NZ), jnp.float32) ** block_levels(key_list[3], (NX, NY, NZ), ((0, 16), (1, 2)), -0.2, 0.2), 0.29882812, 1.0).astype(jnp.bfloat16)
    buoyancy = jnp.clip(0.5 + 1.0 * jax.random.uniform(key_list[4], (NX, NY, NZ), jnp.float32) ** block_levels(key_list[4], (NX, NY, NZ), ((0, 16), (1, 2)), -0.2, 0.2), 0.5, 1.5).astype(jnp.bfloat16)
    source_p = centred(key_list[5], (3, NX, NY, NZ), 1.0, 6.0, ((1, 16), (2, 2)))
    source_s = centred(key_list[6], (3, NX, NY, NZ), 1.0, 6.0, ((1, 16), (2, 2)))
    return {"velocity": velocity, "stress": stress, "lame_lambda": lame_lambda, "shear_modulus": shear_modulus, "buoyancy": buoyancy, "source_p": source_p, "source_s": source_s}


time_step = 0.2


def next_cell(field, which):
    length = field.shape[which]
    zero_rim = jnp.zeros_like(lax.slice_in_dim(field, 0, 1, axis=which))
    return jnp.concatenate([lax.slice_in_dim(field, 1, length, axis=which), zero_rim], axis=which)


def prior_cell(field, which):
    length = field.shape[which]
    zero_rim = jnp.zeros_like(lax.slice_in_dim(field, 0, 1, axis=which))
    return jnp.concatenate([zero_rim, lax.slice_in_dim(field, 0, length - 1, axis=which)], axis=which)


def stress_update(velocity, stress, lame_value, shear_value):
    x_speed, y_speed, z_speed = velocity[0], velocity[1], velocity[2]
    strain_x = x_speed - prior_cell(x_speed, 0)
    strain_y = y_speed - prior_cell(y_speed, 1)
    strain_z = z_speed - prior_cell(z_speed, 2)
    volume = strain_x + strain_y + strain_z
    normal_x = stress[0] + time_step * (lame_value * volume + 2.0 * shear_value * strain_x)
    normal_y = stress[1] + time_step * (lame_value * volume + 2.0 * shear_value * strain_y)
    normal_z = stress[2] + time_step * (lame_value * volume + 2.0 * shear_value * strain_z)
    shear_xy = stress[3] + time_step * shear_value * ((next_cell(x_speed, 1) - x_speed) + (next_cell(y_speed, 0) - y_speed))
    shear_xz = stress[4] + time_step * shear_value * ((next_cell(x_speed, 2) - x_speed) + (next_cell(z_speed, 0) - z_speed))
    shear_yz = stress[5] + time_step * shear_value * ((next_cell(y_speed, 2) - y_speed) + (next_cell(z_speed, 1) - z_speed))
    return jnp.stack([normal_x, normal_y, normal_z, shear_xy, shear_xz, shear_yz])


def velocity_update(velocity, stress, buoy_value):
    normal_x, normal_y, normal_z = stress[0], stress[1], stress[2]
    shear_xy, shear_xz, shear_yz = stress[3], stress[4], stress[5]
    x_speed = velocity[0] + time_step * buoy_value * ((next_cell(normal_x, 0) - normal_x) + (shear_xy - prior_cell(shear_xy, 1)) + (shear_xz - prior_cell(shear_xz, 2)))
    y_speed = velocity[1] + time_step * buoy_value * ((shear_xy - prior_cell(shear_xy, 0)) + (next_cell(normal_y, 1) - normal_y) + (shear_yz - prior_cell(shear_yz, 2)))
    z_speed = velocity[2] + time_step * buoy_value * ((shear_xz - prior_cell(shear_xz, 0)) + (shear_yz - prior_cell(shear_yz, 1)) + (next_cell(normal_z, 2) - normal_z))
    return jnp.stack([x_speed, y_speed, z_speed])


def signed_index(positions, length):
    half_length = length // 2
    signed = jnp.where(positions < half_length, positions, jnp.where(positions == half_length, 0, positions - length))
    return signed.astype(jnp.float32)


def reference(velocity, stress, lame_lambda, shear_modulus, buoyancy, source_p, source_s):
    lame_value = lame_lambda.astype(jnp.float32)
    shear_value = shear_modulus.astype(jnp.float32)
    buoy_value = buoyancy.astype(jnp.float32)
    for step_index in range(STEPS):
        stress = stress_update(velocity, stress, lame_value, shear_value)
        velocity = velocity_update(velocity, stress, buoy_value)
    spectra = jnp.fft.fftn(velocity, axes=(1, 2, 3))
    wave_x = signed_index(jnp.arange(NX, dtype=jnp.int32), NX)[:, None, None]
    wave_y = signed_index(jnp.arange(NY, dtype=jnp.int32), NY)[None, :, None]
    wave_z = signed_index(jnp.arange(NZ, dtype=jnp.int32), NZ)[None, None, :]
    inverse_norm = 1.0 / jnp.maximum(wave_x * wave_x + wave_y * wave_y + wave_z * wave_z, 1.0)
    radial = (wave_x * spectra[0] + wave_y * spectra[1] + wave_z * spectra[2]) * inverse_norm
    compression = jnp.stack([wave_x * radial, wave_y * radial, wave_z * radial])
    p_field = jnp.real(jnp.fft.ifftn(compression, axes=(1, 2, 3))).astype(jnp.float32)
    s_field = jnp.real(jnp.fft.ifftn(spectra - compression, axes=(1, 2, 3))).astype(jnp.float32)
    image_p = jnp.sum(source_p.astype(jnp.float32) * p_field, axis=0)
    image_s = jnp.sum(source_s.astype(jnp.float32) * s_field, axis=0)
    return image_p, image_s
```

```python
import numpy as np
import ml_dtypes
import jax
import jax.numpy as jnp
from jax import lax
from jax.experimental import pallas as pl
from jax.experimental.pallas import tpu as pltpu
from jax.sharding import PartitionSpec as P

STEPS = 2
MOST_CHUNKS = 2
VMEM_BYTES = 56 * 2**20

time_step = 0.2


def passed_along(block, axis, distance):
    devices = range(lax.axis_size(axis))
    route = [(i - distance, i) for i in devices if i - distance in devices]
    return lax.ppermute(block, axis, route)


def x_rims(planes, offset):
    return passed_along(planes, "gx", offset)


def y_rims(planes, offset):
    return passed_along(planes, "gy", offset)


def with_next(field, rim, which):
    length = field.shape[which]
    return jnp.concatenate([lax.slice_in_dim(field, 1, length, axis=which), rim], axis=which)


def with_prior(field, rim, which):
    length = field.shape[which]
    return jnp.concatenate([rim, lax.slice_in_dim(field, 0, length - 1, axis=which)], axis=which)


def zero_rim(field, which):
    return jnp.zeros_like(lax.slice_in_dim(field, 0, 1, axis=which))


def stress_step(velocity, stress, lame_value, shear_value):
    x_speed, y_speed, z_speed = (velocity[0], velocity[1], velocity[2])
    prior_x = x_rims(x_speed[None, -1:], 1)
    next_x = x_rims(jnp.stack([y_speed[:1], z_speed[:1]]), -1)
    prior_y = y_rims(y_speed[None, :, -1:], 1)
    next_y = y_rims(jnp.stack([x_speed[:, :1], z_speed[:, :1]]), -1)
    strain_x = x_speed - with_prior(x_speed, prior_x[0], 0)
    strain_y = y_speed - with_prior(y_speed, prior_y[0], 1)
    strain_z = z_speed - with_prior(z_speed, zero_rim(z_speed, 2), 2)
    volume = strain_x + strain_y + strain_z
    normal_x = stress[0] + time_step * (lame_value * volume + 2.0 * shear_value * strain_x)
    normal_y = stress[1] + time_step * (lame_value * volume + 2.0 * shear_value * strain_y)
    normal_z = stress[2] + time_step * (lame_value * volume + 2.0 * shear_value * strain_z)
    shear_xy = stress[3] + time_step * shear_value * (
        with_next(x_speed, next_y[0], 1) - x_speed + (with_next(y_speed, next_x[0], 0) - y_speed)
    )
    shear_xz = stress[4] + time_step * shear_value * (
        with_next(x_speed, zero_rim(x_speed, 2), 2)
        - x_speed
        + (with_next(z_speed, next_x[1], 0) - z_speed)
    )
    shear_yz = stress[5] + time_step * shear_value * (
        with_next(y_speed, zero_rim(y_speed, 2), 2)
        - y_speed
        + (with_next(z_speed, next_y[1], 1) - z_speed)
    )
    return jnp.stack([normal_x, normal_y, normal_z, shear_xy, shear_xz, shear_yz])


def velocity_step(velocity, stress, buoy_value):
    normal_x, normal_y, normal_z = (stress[0], stress[1], stress[2])
    shear_xy, shear_xz, shear_yz = (stress[3], stress[4], stress[5])
    next_x = x_rims(normal_x[None, :1], -1)
    prior_x = x_rims(jnp.stack([shear_xy[-1:], shear_xz[-1:]]), 1)
    next_y = y_rims(normal_y[None, :, :1], -1)
    prior_y = y_rims(jnp.stack([shear_xy[:, -1:], shear_yz[:, -1:]]), 1)
    x_speed = velocity[0] + time_step * buoy_value * (
        with_next(normal_x, next_x[0], 0)
        - normal_x
        + (shear_xy - with_prior(shear_xy, prior_y[0], 1))
        + (shear_xz - with_prior(shear_xz, zero_rim(shear_xz, 2), 2))
    )
    y_speed = velocity[1] + time_step * buoy_value * (
        shear_xy
        - with_prior(shear_xy, prior_x[0], 0)
        + (with_next(normal_y, next_y[0], 1) - normal_y)
        + (shear_yz - with_prior(shear_yz, zero_rim(shear_yz, 2), 2))
    )
    z_speed = velocity[2] + time_step * buoy_value * (
        shear_xz
        - with_prior(shear_xz, prior_x[1], 0)
        + (shear_yz - with_prior(shear_yz, prior_y[1], 1))
        + (with_next(normal_z, zero_rim(normal_z, 2), 2) - normal_z)
    )
    return jnp.stack([x_speed, y_speed, z_speed])


def basis(length):
    half = length // 2
    wave = np.arange(half)
    place = np.arange(length)
    angle = (wave[:, None] * place[None, :] % length) * (2.0 * np.pi / length)
    cosine, sine = np.cos(angle), np.sin(angle)
    sine[0] = 1.0 - 2.0 * (place % 2)
    return np.concatenate([cosine, sine])


def waves_of(length):
    return np.tile(np.arange(length // 2, dtype=np.float64), 2)


def inverse_basis(length):
    weight = np.where(waves_of(length) == 0, 1.0, 2.0) / length
    return basis(length) * weight[:, None]


def turned(table):
    half = table.shape[0] // 2
    return np.concatenate([table[half:], -table[:half]]) * waves_of(table.shape[0])[:, None]


def halves(table):
    high = table.astype(ml_dtypes.bfloat16)
    low = (table - high.astype(np.float64)).astype(ml_dtypes.bfloat16)
    return np.stack([high, low])


def split(value):
    high = value.astype(jnp.bfloat16)
    return high, (value - high.astype(jnp.float32)).astype(jnp.bfloat16)


def times(left, right, dims=((1,), (0,))):
    def one(a, b):
        return lax.dot_general(a, b, (dims, ((), ())), preferred_element_type=jnp.float32)

    return one(left[0], right[0]) + (one(left[1], right[0]) + one(left[0], right[1]))


def joined(pieces, axis):
    return pieces[0] if len(pieces) == 1 else jnp.concatenate(pieces, axis=axis)


def fit(length, most):
    size = min(length, most)
    while length % size:
        size -= 1
    return size


def params():
    return pltpu.CompilerParams(vmem_limit_bytes=VMEM_BYTES)


def whole_block(shape):
    return pl.BlockSpec(shape, lambda *_: (0,) * len(shape))


def scalars():
    return pl.BlockSpec(memory_space=pltpu.SMEM)


class Plan:
    def __init__(self, brick):
        self.x, self.y, self.z = brick
        self.gx, self.gy = lax.axis_size("gx"), lax.axis_size("gy")
        self.nx, self.ny = self.x * self.gx, self.y * self.gy
        chunks = MOST_CHUNKS
        while chunks > 1 and self.z % (chunks * self.gy * self.gx):
            chunks -= 1
        self.chunks = chunks
        self.kz = self.z // (chunks * self.gy)
        self.parts = max(1, self.gx // self.kz)
        self.per = max(1, self.kz // self.gx)
        self.ky = self.ny // self.parts


def source(me, step, count):
    return lax.rem(me - step + count, count)


def z_forward(plan, place, velocity):
    x, y, z, kz = plan.x, plan.y, plan.z, plan.kz
    table = np.stack([halves(basis(z)), halves(turned(basis(z)))])
    table = table.reshape(2, 2, plan.chunks, plan.gy, kz, z)
    count = plan.chunks * plan.gy

    def kernel(place_ref, table_ref, v_ref, *outs):
        at = pl.program_id(0)
        me = place_ref[1]
        for comp in range(3):
            kind = 1 if comp == 2 else 0
            field = split(v_ref[comp, 0])
            for chunk in range(plan.chunks):
                for step in range(plan.gy):
                    group = lax.rem(me + step, plan.gy)
                    rows = (table_ref[kind, 0, chunk, group], table_ref[kind, 1, chunk, group])
                    value = times(rows, field, ((1,), (1,)))
                    outs[chunk * plan.gy + step][comp, pl.ds(at, kz, stride=x), :] = value

    outs = pl.pallas_call(
        kernel,
        grid=(x,),
        in_specs=[
            scalars(),
            whole_block(table.shape),
            pl.BlockSpec((3, 1, y, z), lambda i: (0, i, 0, 0)),
        ],
        out_specs=[whole_block((3, kz * x, y))] * count,
        out_shape=[jax.ShapeDtypeStruct((3, kz * x, y), jnp.float32)] * count,
        compiler_params=params(),
        cost_estimate=pl.CostEstimate(
            flops=18 * x * y * z * z, bytes_accessed=24 * x * y * z, transcendentals=0
        ),
        name="z_forward",
    )(place, jnp.asarray(table), velocity)
    outs = [out.reshape(3, kz, x, y) for out in outs]
    return [outs[c * plan.gy : (c + 1) * plan.gy] for c in range(plan.chunks)]


def swap_gy(blocks):
    count = len(blocks)
    moved = [blocks[0]]
    for step in range(1, count):
        route = [(i, (i + step) % count) for i in range(count)]
        moved.append(lax.ppermute(blocks[step], "gy", route))
    return moved


def y_forward(plan, place, blocks):
    x, y, ny, kz = plan.x, plan.y, plan.ny, plan.kz
    table = halves(basis(ny).T).reshape(2, plan.gy, y, ny)
    deep = fit(kz, 8)
    rows = deep * x
    half = ny // 2
    aligned = y % 128 == 0

    def kernel(place_ref, table_ref, *refs):
        ins, out = refs[:-1], refs[-1]
        me = place_ref[1]
        groups = [source(me, step, plan.gy) for step in range(plan.gy)]
        tables = [(table_ref[0, g], table_ref[1, g]) for g in groups]
        if aligned:
            tables = [tuple(joined([t[i] for t in tables], 0) for i in range(2))]

        def moved(comp):
            fields = [ref[comp].reshape(rows, y) for ref in ins]
            if aligned:
                fields = [joined(fields, 1)]
            return sum(times(split(f), t) for f, t in zip(fields, tables))

        wave = lax.broadcasted_iota(jnp.int32, (1, half), 1).astype(jnp.float32)
        out[:, 0] = moved(0).reshape(deep, x, ny)
        along, rest = moved(1), moved(2)
        out[:, 1, :, :half] = (rest[:, :half] + wave * along[:, half:]).reshape(deep, x, half)
        out[:, 1, :, half:] = (rest[:, half:] - wave * along[:, :half]).reshape(deep, x, half)

    return pl.pallas_call(
        kernel,
        grid=(kz // deep,),
        in_specs=[scalars(), whole_block(table.shape)]
        + [pl.BlockSpec((3, deep, x, y), lambda i: (0, i, 0, 0))] * plan.gy,
        out_specs=pl.BlockSpec((deep, 2, x, ny), lambda i: (i, 0, 0, 0)),
        out_shape=jax.ShapeDtypeStruct((kz, 2, x, ny), jnp.float32),
        compiler_params=params(),
        cost_estimate=pl.CostEstimate(
            flops=18 * kz * x * ny * ny, bytes_accessed=20 * kz * x * ny, transcendentals=0
        ),
        name="y_forward",
    )(place, jnp.asarray(table), *blocks)


def to_lines(plan, planes):
    if plan.parts > 1:
        planes = planes.reshape(plan.kz, 2, plan.x, plan.parts, plan.ky).transpose(0, 3, 1, 2, 4)
    planes = planes.reshape(plan.gx, plan.per, 2, plan.x, plan.ky)
    return lax.all_to_all(planes, "gx", 0, 0, tiled=True)


def to_planes(plan, lines):
    planes = lax.all_to_all(lines, "gx", 0, 0, tiled=True)
    if plan.parts > 1:
        planes = planes.reshape(plan.kz, plan.parts, 2, plan.x, plan.ky).transpose(0, 2, 3, 1, 4)
    return planes.reshape(plan.kz, 2, plan.x, plan.ny)


def x_lines(plan, place, lines, chunk):
    x, nx, ny, ky, gx = plan.x, plan.nx, plan.ny, plan.ky, plan.gx
    forth = halves(basis(nx))
    back = halves(-inverse_basis(nx).T)
    lanes = 128 if ky % 128 == 0 else ky
    half = nx // 2
    aligned = lanes % 128 == 0

    def kernel(place_ref, forth_ref, back_ref, in_ref, out_ref):
        me_x, me_y = place_ref[0], place_ref[1]
        which, lane = pl.program_id(0), pl.program_id(1)

        def through(table_ref, pair):
            table = (table_ref[0], table_ref[1])
            if aligned:
                both = times(table, split(jnp.concatenate(pair, axis=1)))
                return both[:, :lanes], both[:, lanes:]
            return tuple(times(table, split(value)) for value in pair)

        pair = [in_ref[:, 0, i].reshape(nx, lanes) for i in range(2)]
        along, rest = through(forth_ref, pair)
        wave_x = lax.broadcasted_iota(jnp.int32, (half, lanes), 0).astype(jnp.float32)
        slot_y = lax.broadcasted_iota(jnp.int32, (1, lanes), 1) + (
            lane * lanes + lax.rem(me_x, plan.parts) * ky
        )
        wave_y = lax.rem(slot_y, ny // 2).astype(jnp.float32)
        slot_z = (chunk * plan.gy + me_y) * plan.kz + me_x // plan.parts * plan.per + which
        wave_z = lax.rem(slot_z, plan.z // 2).astype(jnp.float32)
        scale = 1.0 / jnp.maximum(wave_x * wave_x + (wave_y * wave_y + wave_z * wave_z), 1.0)
        cosine = (rest[:half] + wave_x * along[half:]) * scale
        sine = (rest[half:] - wave_x * along[:half]) * scale
        plain = jnp.concatenate([cosine, sine], axis=0)
        slope = jnp.concatenate([wave_x * sine, -wave_x * cosine], axis=0)
        for i, value in enumerate(through(back_ref, [slope, plain])):
            out_ref[:, 0, i] = value.reshape(gx, x, lanes)

    block = pl.BlockSpec((gx, 1, 2, x, lanes), lambda i, j: (0, i, 0, 0, j))
    return pl.pallas_call(
        kernel,
        grid=(plan.per, ky // lanes),
        in_specs=[scalars(), whole_block(forth.shape), whole_block(back.shape), block],
        out_specs=block,
        out_shape=jax.ShapeDtypeStruct(lines.shape, jnp.float32),
        compiler_params=params(),
        cost_estimate=pl.CostEstimate(
            flops=24 * plan.per * ky * nx * nx,
            bytes_accessed=16 * plan.per * ky * nx,
            transcendentals=0,
        ),
        name="x_lines",
    )(place, jnp.asarray(forth), jnp.asarray(back), lines)


def y_inverse(plan, place, planes):
    x, y, ny, kz = plan.x, plan.y, plan.ny, plan.kz
    table = np.stack(np.split(inverse_basis(ny), plan.gy, axis=1))
    table = halves(table)
    deep = fit(kz, 8)
    rows = deep * x
    half = ny // 2
    aligned = y % 128 == 0

    def kernel(place_ref, table_ref, in_ref, *outs):
        me = place_ref[1]
        groups = [lax.rem(me + step, plan.gy) for step in range(plan.gy)]
        tables = [(table_ref[0, g], table_ref[1, g]) for g in groups]
        slope = in_ref[:, 0].reshape(rows, ny)
        plain = in_ref[:, 1].reshape(rows, ny)
        wave = lax.broadcasted_iota(jnp.int32, (1, half), 1).astype(jnp.float32)
        along = jnp.concatenate([wave * plain[:, half:], -wave * plain[:, :half]], axis=1)
        for comp, value in enumerate((slope, along, plain)):
            parts = split(value)
            if aligned:
                table = tuple(joined([t[i] for t in tables], 1) for i in range(2))
                found = times(parts, table)
                pieces = [found[:, s * y : (s + 1) * y] for s in range(plan.gy)]
            else:
                pieces = [times(parts, t) for t in tables]
            for out, piece in zip(outs, pieces):
                out[comp] = piece.reshape(deep, x, y)

    return pl.pallas_call(
        kernel,
        grid=(kz // deep,),
        in_specs=[
            scalars(),
            whole_block(table.shape),
            pl.BlockSpec((deep, 2, x, ny), lambda i: (i, 0, 0, 0)),
        ],
        out_specs=[pl.BlockSpec((3, deep, x, y), lambda i: (0, i, 0, 0))] * plan.gy,
        out_shape=[jax.ShapeDtypeStruct((3, kz, x, y), jnp.float32)] * plan.gy,
        compiler_params=params(),
        cost_estimate=pl.CostEstimate(
            flops=18 * kz * x * ny * ny, bytes_accessed=20 * kz * x * ny, transcendentals=0
        ),
        name="y_inverse",
    )(place, jnp.asarray(table), planes)


def images(plan, place, blocks, velocity, source_p, source_s):
    x, y, z, kz = plan.x, plan.y, plan.z, plan.kz
    table = np.stack([halves(inverse_basis(z)), halves(-turned(inverse_basis(z)))])
    table = table.reshape(2, 2, plan.chunks, plan.gy, kz, z)
    blocks = [block.reshape(3, kz * x, y) for group in blocks for block in group]

    def kernel(place_ref, table_ref, v_ref, p_ref, s_ref, *refs):
        ins, (image_p, image_s) = refs[:-2], refs[-2:]
        at = pl.program_id(0)
        me = place_ref[1]
        order = [
            (chunk, source(me, step, plan.gy))
            for chunk in range(plan.chunks)
            for step in range(plan.gy)
        ]
        total_p = total_s = 0.0
        for comp in range(3):
            kind = 1 if comp == 2 else 0
            value = joined([ref[comp, pl.ds(at, kz, stride=x), :] for ref in ins], 0)
            back = tuple(joined([table_ref[kind, i, c, g] for c, g in order], 0) for i in range(2))
            field = times(split(value), back, ((0,), (0,)))
            total_p += p_ref[comp, 0].astype(jnp.float32) * field
            total_s += s_ref[comp, 0].astype(jnp.float32) * (v_ref[comp, 0] - field)
        image_p[0] = total_p
        image_s[0] = total_s

    plane = pl.BlockSpec((3, 1, y, z), lambda i: (0, i, 0, 0))
    image = pl.BlockSpec((1, y, z), lambda i: (i, 0, 0))
    return pl.pallas_call(
        kernel,
        grid=(x,),
        in_specs=[scalars(), whole_block(table.shape), plane, plane, plane]
        + [whole_block((3, kz * x, y))] * len(blocks),
        out_specs=[image, image],
        out_shape=[jax.ShapeDtypeStruct((x, y, z), jnp.float32)] * 2,
        compiler_params=params(),
        cost_estimate=pl.CostEstimate(
            flops=18 * x * y * z * z, bytes_accessed=44 * x * y * z, transcendentals=0
        ),
        name="images",
    )(place, jnp.asarray(table), velocity, source_p, source_s, *blocks)


def shards(velocity, stress, lame_lambda, shear_modulus, buoyancy, source_p, source_s):
    lame_value = lame_lambda.astype(jnp.float32)
    shear_value = shear_modulus.astype(jnp.float32)
    buoy_value = buoyancy.astype(jnp.float32)
    for step_index in range(STEPS):
        stress = stress_step(velocity, stress, lame_value, shear_value)
        velocity = velocity_step(velocity, stress, buoy_value)
    plan = Plan(velocity.shape[1:])
    place = jnp.stack([lax.axis_index("gx"), lax.axis_index("gy")]).astype(jnp.int32)
    blocks = z_forward(plan, place, velocity)
    lines = [to_lines(plan, y_forward(plan, place, swap_gy(group))) for group in blocks]
    lines = [x_lines(plan, place, part, chunk) for chunk, part in enumerate(lines)]
    blocks = [swap_gy(y_inverse(plan, place, to_planes(plan, part))) for part in lines]
    return tuple(images(plan, place, blocks, velocity, source_p, source_s))


def solution(mesh):
    in_specs = (
        P(None, "gx", "gy", None),
        P(None, "gx", "gy", None),
        P("gx", "gy", None),
        P("gx", "gy", None),
        P("gx", "gy", None),
        P(None, "gx", "gy", None),
        P(None, "gx", "gy", None),
    )
    out_specs = (P("gx", "gy", None), P("gx", "gy", None))
    return jax.shard_map(shards, mesh=mesh, in_specs=in_specs, out_specs=out_specs, check_vma=False)
```

```python
import numpy as np
import ml_dtypes
import jax
import jax.numpy as jnp
from jax import lax
from jax.experimental import pallas as pl
from jax.experimental.pallas import tpu as pltpu
from jax.sharding import PartitionSpec as P

STEPS = 2
MOST_CHUNKS = 2
VMEM_BYTES = 56 * 2**20

time_step = 0.2


def passed_along(block, axis, distance):
    devices = range(lax.axis_size(axis))
    route = [(i - distance, i) for i in devices if i - distance in devices]
    return lax.ppermute(block, axis, route)


def across_corner(row, x_way, y_way):
    x_count, y_count = lax.axis_size("gx"), lax.axis_size("gy")
    route = [
        ((i - x_way) * y_count + j - y_way, i * y_count + j)
        for i in range(x_count)
        for j in range(y_count)
        if 0 <= i - x_way < x_count and 0 <= j - y_way < y_count
    ]
    return lax.ppermute(row, ("gx", "gy"), route)


def exchange(x_last, x_first, y_last, y_first):
    return (
        passed_along(x_last, "gx", 1),
        passed_along(x_first, "gx", -1),
        passed_along(y_last, "gy", 1),
        passed_along(y_first, "gy", -1),
        across_corner(y_last[1, :1], -1, 1),
        across_corner(y_first[0, -1:], 1, -1),
    )


def stencil(brick, velocity, stress, lame, shear, buoyancy, rims, medium, last):
    x, y, z = brick
    group = fit(x, 4)
    steps = x // group

    def kernel(*refs):
        (v_ref, s_ref, lame_ref, shear_ref, buoy_ref, v_next_ref, xx_next_ref) = refs[:7]
        (lame_next_ref, shear_next_ref, xl, xr, yl, yr, edge_y, edge_x) = refs[7:15]
        (xl_medium, xr_medium, yl_medium, yr_medium) = refs[15:19]
        carried = refs[-1]
        outs = refs[19:-1]
        step = pl.program_id(0)
        at = step * group
        row = lax.broadcasted_iota(jnp.int32, (y, z), 0)
        lane = lax.broadcasted_iota(jnp.int32, (y, z), 1)
        first_row, last_row = row == 0, row == y - 1
        first_lane, last_lane = lane == 0, lane == z - 1

        def next_z(field):
            edge = last_lane if field.shape[0] == y else last_lane[:1]
            return jnp.where(edge, 0.0, pltpu.roll(field, z - 1, 1))

        def prior_z(field):
            edge = first_lane if field.shape[0] == y else first_lane[:1]
            return jnp.where(edge, 0.0, pltpu.roll(field, 1, 1))

        def next_y(field, rim):
            return jnp.where(last_row, rim, pltpu.roll(field, y - 1, 0))

        def prior_y(field, rim):
            return jnp.where(first_row, rim, pltpu.roll(field, 1, 0))

        def wide(value):
            return value.astype(jnp.float32)

        def line(ref, which, place):
            return ref[which, pl.ds(place, 1), :]

        def line_after(place):
            inside = line(yl, 1, jnp.minimum(place, x - 1))
            return jnp.where(place == x, edge_y[...], inside)

        @pl.when(step == 0)
        def _():
            shear_rim = xl_medium[5]
            vx, vy, vz = xl[0], xl[1], xl[2]
            carried[0] = vx
            carried[1] = xl[3] + time_step * shear_rim * (
                (next_y(vx, edge_x[...]) - vx) + (v_ref[1, 0] - vy)
            )
            carried[2] = xl[4] + time_step * shear_rim * ((next_z(vx) - vx) + (v_ref[2, 0] - vz))

        end = step == steps - 1
        after = [jnp.where(end, xr[i], v_next_ref[i, 0]) for i in range(3)]
        stresses = []
        vx_prior = carried[0]
        for k in range(group):
            vx, vy, vz = v_ref[0, k], v_ref[1, k], v_ref[2, k]
            vy_next = after[1] if k == group - 1 else v_ref[1, k + 1]
            vz_next = after[2] if k == group - 1 else v_ref[2, k + 1]
            lame_value, shear_value = wide(lame_ref[k]), wide(shear_ref[k])
            ex = vx - vx_prior
            ey = vy - prior_y(vy, line(yl, 1, at + k))
            ez = vz - prior_z(vz)
            swell = lame_value * (ex + ey + ez)
            double = 2.0 * shear_value
            xx = s_ref[0, k] + time_step * (swell + double * ex)
            yy = s_ref[1, k] + time_step * (swell + double * ey)
            zz = s_ref[2, k] + time_step * (swell + double * ez)
            pull = time_step * shear_value
            xy = s_ref[3, k] + pull * ((next_y(vx, line(yr, 0, at + k)) - vx) + (vy_next - vy))
            xz = s_ref[4, k] + pull * ((next_z(vx) - vx) + (vz_next - vz))
            yz = s_ref[5, k] + pull * (
                (next_z(vy) - vy) + (next_y(vz, line(yr, 2, at + k)) - vz)
            )
            stresses.append((xx, yy, zz, xy, xz, yz))
            vx_prior = vx

        ex = after[0] - vx_prior
        ey = after[1] - prior_y(after[1], line_after(at + group))
        ez = after[2] - prior_z(after[2])
        lame_value = jnp.where(end, xr_medium[4], wide(lame_next_ref[0]))
        shear_value = jnp.where(end, xr_medium[5], wide(shear_next_ref[0]))
        xx_after = jnp.where(end, xr[3], xx_next_ref[0, 0]) + time_step * (
            lame_value * (ex + ey + ez) + 2.0 * shear_value * ex
        )

        xy_prior, xz_prior = carried[1], carried[2]
        new = outs[0]
        for k in range(group):
            xx, yy, zz, xy, xz, yz = stresses[k]
            xx_next = xx_after if k == group - 1 else stresses[k + 1][0]
            here = at + k
            vx, vy, vz = v_ref[0, k], v_ref[1, k], v_ref[2, k]
            pull = time_step * line(yl_medium, 5, here)
            vy_rim, vz_rim = line(yl, 1, here), line(yl, 2, here)
            xy_rim = line(yl, 3, here) + pull * (
                (vx[:1] - line(yl, 0, here)) + (line_after(here + 1) - vy_rim)
            )
            yz_rim = line(yl, 4, here) + pull * ((next_z(vy_rim) - vy_rim) + (vz[:1] - vz_rim))
            vx_rim, vz_rim = line(yr, 0, here), line(yr, 2, here)
            vx_before = jnp.where(here == 0, edge_x[...], line(yr, 0, jnp.maximum(here - 1, 0)))
            ex = vx_rim - vx_before
            ey = line(yr, 1, here) - vy[-1:]
            ez = vz_rim - prior_z(vz_rim)
            yy_rim = line(yr, 3, here) + time_step * (
                line(yr_medium, 4, here) * (ex + ey + ez) + 2.0 * line(yr_medium, 5, here) * ey
            )
            push = time_step * wide(buoy_ref[k])
            vx = vx + push * (
                (xx_next - xx) + (xy - prior_y(xy, xy_rim)) + (xz - prior_z(xz))
            )
            vy = vy + push * ((xy - xy_prior) + (next_y(yy, yy_rim) - yy) + (yz - prior_z(yz)))
            vz = vz + push * ((xz - xz_prior) + (yz - prior_y(yz, yz_rim)) + (next_z(zz) - zz))
            xy_prior, xz_prior = xy, xz
            for i, value in enumerate((vx, vy, vz)):
                new[i, k] = value
            if not last:
                s_out, x_last, x_first, y_last, y_first = outs[1:]
                for i, value in enumerate((xx, yy, zz, xy, xz, yz)):
                    s_out[i, k] = value
                for i, value in enumerate((vx, vy, vz, xy, yz)):
                    y_last[i, pl.ds(here, 1), :] = value[-1:]
                for i, value in enumerate((vx, vy, vz, yy)):
                    y_first[i, pl.ds(here, 1), :] = value[:1]
                if k == 0:

                    @pl.when(step == 0)
                    def _():
                        for i, value in enumerate((vx, vy, vz, xx)):
                            x_first[i] = value

                if k == group - 1:

                    @pl.when(end)
                    def _():
                        for i, value in enumerate((vx, vy, vz, xy, xz)):
                            x_last[i] = value

        carried[0] = v_ref[0, group - 1]
        carried[1] = stresses[-1][3]
        carried[2] = stresses[-1][4]

    def after(i):
        return jnp.minimum((i + 1) * group, x - 1)

    def planes(count, depth):
        return pl.BlockSpec((count, depth, y, z), lambda i: (0, i, 0, 0))

    medium_block = pl.BlockSpec((group, y, z), lambda i: (i, 0, 0))
    medium_next = pl.BlockSpec((1, y, z), lambda i: (after(i), 0, 0))
    rim_blocks = [whole_block(rim.shape) for rim in (*rims, *medium)]
    f32 = jnp.float32
    out_shape = [jax.ShapeDtypeStruct((3, x, y, z), f32)]
    out_specs = [planes(3, group)]
    if not last:
        edges = [(5, y, z), (4, y, z), (5, x, z), (4, x, z)]
        out_shape += [jax.ShapeDtypeStruct((6, x, y, z), f32)]
        out_shape += [jax.ShapeDtypeStruct(edge, f32) for edge in edges]
        out_specs += [planes(6, group)] + [whole_block(edge) for edge in edges]
    return pl.pallas_call(
        kernel,
        grid=(steps,),
        in_specs=[
            planes(3, group),
            planes(6, group),
            medium_block,
            medium_block,
            medium_block,
            pl.BlockSpec((3, 1, y, z), lambda i: (0, after(i), 0, 0)),
            pl.BlockSpec((1, 1, y, z), lambda i: (0, after(i), 0, 0)),
            medium_next,
            medium_next,
        ]
        + rim_blocks,
        out_specs=out_specs,
        out_shape=out_shape,
        scratch_shapes=[pltpu.VMEM((3, y, z), f32)],
        compiler_params=params(),
        cost_estimate=pl.CostEstimate(
            flops=80 * x * y * z, bytes_accessed=(54 if last else 78) * x * y * z, transcendentals=0
        ),
        name="stencil",
    )(
        velocity, stress, lame, shear, buoyancy, velocity, stress, lame, shear, *rims, *medium
    )


def propagate(velocity, stress, lame, shear, buoyancy):
    brick = velocity.shape[1:]
    lame_wide, shear_wide = lame.astype(jnp.float32), shear.astype(jnp.float32)

    def side(which, at, chosen, mediums):
        index = (at,) if which == 0 else (slice(None), at)
        fields = [velocity[(i, *index)] for i in range(3)]
        fields += [stress[(i, *index)] for i in chosen]
        return jnp.stack(fields + [medium[index] for medium in mediums])

    rims = exchange(
        side(0, -1, (3, 4), (shear_wide,)),
        side(0, 0, (0,), (lame_wide, shear_wide)),
        side(1, -1, (3, 5), (shear_wide,)),
        side(1, 0, (1,), (lame_wide, shear_wide)),
    )
    medium = rims[:4]
    for step_index in range(STEPS):
        last = step_index == STEPS - 1
        found = stencil(brick, velocity, stress, lame, shear, buoyancy, rims, medium, last)
        velocity = found[0]
        if not last:
            stress = found[1]
            rims = exchange(*found[2:])
    return velocity


def basis(length):
    half = length // 2
    wave = np.arange(half)
    place = np.arange(length)
    angle = (wave[:, None] * place[None, :] % length) * (2.0 * np.pi / length)
    cosine, sine = np.cos(angle), np.sin(angle)
    sine[0] = 1.0 - 2.0 * (place % 2)
    return np.concatenate([cosine, sine])


def waves_of(length):
    return np.tile(np.arange(length // 2, dtype=np.float64), 2)


def inverse_basis(length):
    weight = np.where(waves_of(length) == 0, 1.0, 2.0) / length
    return basis(length) * weight[:, None]


def turned(table):
    half = table.shape[0] // 2
    return np.concatenate([table[half:], -table[:half]]) * waves_of(table.shape[0])[:, None]


def halves(table):
    high = table.astype(ml_dtypes.bfloat16)
    low = (table - high.astype(np.float64)).astype(ml_dtypes.bfloat16)
    return np.stack([high, low])


def split(value):
    high = value.astype(jnp.bfloat16)
    return high, (value - high.astype(jnp.float32)).astype(jnp.bfloat16)


def dot(left, right, dims=((1,), (0,))):
    return lax.dot_general(left, right, (dims, ((), ())), preferred_element_type=jnp.float32)


def times(left, right):
    return dot(left[0], right[0]) + (dot(left[1], right[0]) + dot(left[0], right[1]))


def joined(pieces, axis):
    return pieces[0] if len(pieces) == 1 else jnp.concatenate(pieces, axis=axis)


def fit(length, most):
    size = min(length, most)
    while length % size:
        size -= 1
    return size


def params():
    return pltpu.CompilerParams(vmem_limit_bytes=VMEM_BYTES)


def whole_block(shape):
    return pl.BlockSpec(shape, lambda *_: (0,) * len(shape))


def scalars():
    return pl.BlockSpec(memory_space=pltpu.SMEM)


class Plan:
    def __init__(self, brick):
        self.x, self.y, self.z = brick
        self.gx, self.gy = lax.axis_size("gx"), lax.axis_size("gy")
        self.nx, self.ny = self.x * self.gx, self.y * self.gy
        chunks = MOST_CHUNKS
        while chunks > 1 and self.z % (chunks * self.gy * self.gx):
            chunks -= 1
        self.chunks = chunks
        self.kz = self.z // (chunks * self.gy)
        self.parts = max(1, self.gx // self.kz)
        self.per = max(1, self.kz // self.gx)
        self.ky = self.ny // self.parts


def source(me, step, count):
    return lax.rem(me - step + count, count)


def z_forward(plan, place, velocity):
    x, y, z, kz = plan.x, plan.y, plan.z, plan.kz
    table = np.stack([halves(basis(z)), halves(turned(basis(z)))])
    table = table.reshape(2, 2, plan.chunks, plan.gy, kz, z)
    count = plan.chunks * plan.gy

    group = fit(x, 8)
    deep = fit(group, 2)

    def kernel(place_ref, table_ref, v_ref, *outs):
        at = pl.program_id(0) * group
        me = place_ref[1]
        order = [(c, lax.rem(me + s, plan.gy)) for c in range(plan.chunks) for s in range(plan.gy)]
        tables = []
        for kind in range(2):
            high, low = (joined([table_ref[kind, i, c, g] for c, g in order], 0) for i in range(2))
            tables.append((jnp.concatenate([high, high], axis=1), low))
        for comp in range(3):
            twice, low = tables[1 if comp == 2 else 0]
            for plane in range(0, group, deep):
                field = split(v_ref[comp, plane : plane + deep].reshape(deep * y, z))
                value = dot(twice, jnp.concatenate(field, axis=1), ((1,), (1,)))
                value += dot(low, field[0], ((1,), (1,)))
                for i, out in enumerate(outs):
                    for k in range(deep):
                        part = value[i * kz : (i + 1) * kz, k * y : (k + 1) * y]
                        out[comp, pl.ds(at + plane + k, kz, stride=x), :] = part

    outs = pl.pallas_call(
        kernel,
        grid=(x // group,),
        in_specs=[
            scalars(),
            whole_block(table.shape),
            pl.BlockSpec((3, group, y, z), lambda i: (0, i, 0, 0)),
        ],
        out_specs=[whole_block((3, kz * x, y))] * count,
        out_shape=[jax.ShapeDtypeStruct((3, kz * x, y), jnp.float32)] * count,
        compiler_params=params(),
        cost_estimate=pl.CostEstimate(
            flops=18 * x * y * z * z, bytes_accessed=24 * x * y * z, transcendentals=0
        ),
        name="z_forward",
    )(place, jnp.asarray(table), velocity)
    outs = [out.reshape(3, kz, x, y) for out in outs]
    return [outs[c * plan.gy : (c + 1) * plan.gy] for c in range(plan.chunks)]


def swap_gy(blocks):
    count = len(blocks)
    moved = [blocks[0]]
    for step in range(1, count):
        route = [(i, (i + step) % count) for i in range(count)]
        moved.append(lax.ppermute(blocks[step], "gy", route))
    return moved


def y_forward(plan, place, blocks):
    x, y, ny, kz = plan.x, plan.y, plan.ny, plan.kz
    table = halves(basis(ny).T).reshape(2, plan.gy, y, ny)
    deep = fit(kz, 8)
    rows = deep * x
    half = ny // 2
    aligned = y % 128 == 0

    def kernel(place_ref, table_ref, *refs):
        ins, out = refs[:-1], refs[-1]
        me = place_ref[1]
        groups = [source(me, step, plan.gy) for step in range(plan.gy)]
        tables = [(table_ref[0, g], table_ref[1, g]) for g in groups]
        if aligned:
            tables = [tuple(joined([t[i] for t in tables], 0) for i in range(2))]

        def moved(comp):
            fields = [ref[comp].reshape(rows, y) for ref in ins]
            if aligned:
                fields = [joined(fields, 1)]
            return sum(times(split(f), t) for f, t in zip(fields, tables))

        wave = lax.broadcasted_iota(jnp.int32, (1, half), 1).astype(jnp.float32)
        out[:, 0] = moved(0).reshape(deep, x, ny)
        along, rest = moved(1), moved(2)
        out[:, 1, :, :half] = (rest[:, :half] + wave * along[:, half:]).reshape(deep, x, half)
        out[:, 1, :, half:] = (rest[:, half:] - wave * along[:, :half]).reshape(deep, x, half)

    return pl.pallas_call(
        kernel,
        grid=(kz // deep,),
        in_specs=[scalars(), whole_block(table.shape)]
        + [pl.BlockSpec((3, deep, x, y), lambda i: (0, i, 0, 0))] * plan.gy,
        out_specs=pl.BlockSpec((deep, 2, x, ny), lambda i: (i, 0, 0, 0)),
        out_shape=jax.ShapeDtypeStruct((kz, 2, x, ny), jnp.float32),
        compiler_params=params(),
        cost_estimate=pl.CostEstimate(
            flops=18 * kz * x * ny * ny, bytes_accessed=20 * kz * x * ny, transcendentals=0
        ),
        name="y_forward",
    )(place, jnp.asarray(table), *blocks)


def to_lines(plan, planes):
    if plan.parts > 1:
        planes = planes.reshape(plan.kz, 2, plan.x, plan.parts, plan.ky).transpose(0, 3, 1, 2, 4)
    planes = planes.reshape(plan.gx, plan.per, 2, plan.x, plan.ky)
    return lax.all_to_all(planes, "gx", 0, 0, tiled=True)


def to_planes(plan, lines):
    planes = lax.all_to_all(lines, "gx", 0, 0, tiled=True)
    if plan.parts > 1:
        planes = planes.reshape(plan.kz, plan.parts, 2, plan.x, plan.ky).transpose(0, 2, 3, 1, 4)
    return planes.reshape(plan.kz, 2, plan.x, plan.ny)


def x_lines(plan, place, lines, chunk):
    x, nx, ny, ky, gx = plan.x, plan.nx, plan.ny, plan.ky, plan.gx
    forth = halves(basis(nx))
    back = halves(-inverse_basis(nx).T)
    lanes = 128 if ky % 128 == 0 else ky
    half = nx // 2
    aligned = lanes % 128 == 0

    def kernel(place_ref, forth_ref, back_ref, in_ref, out_ref):
        me_x, me_y = place_ref[0], place_ref[1]
        which, lane = pl.program_id(0), pl.program_id(1)

        def through(table_ref, pair):
            table = (table_ref[0], table_ref[1])
            if aligned:
                both = times(table, split(jnp.concatenate(pair, axis=1)))
                return both[:, :lanes], both[:, lanes:]
            return tuple(times(table, split(value)) for value in pair)

        pair = [in_ref[:, 0, i].reshape(nx, lanes) for i in range(2)]
        along, rest = through(forth_ref, pair)
        wave_x = lax.broadcasted_iota(jnp.int32, (half, lanes), 0).astype(jnp.float32)
        slot_y = lax.broadcasted_iota(jnp.int32, (1, lanes), 1) + (
            lane * lanes + lax.rem(me_x, plan.parts) * ky
        )
        wave_y = lax.rem(slot_y, ny // 2).astype(jnp.float32)
        slot_z = (chunk * plan.gy + me_y) * plan.kz + me_x // plan.parts * plan.per + which
        wave_z = lax.rem(slot_z, plan.z // 2).astype(jnp.float32)
        scale = 1.0 / jnp.maximum(wave_x * wave_x + (wave_y * wave_y + wave_z * wave_z), 1.0)
        cosine = (rest[:half] + wave_x * along[half:]) * scale
        sine = (rest[half:] - wave_x * along[:half]) * scale
        plain = jnp.concatenate([cosine, sine], axis=0)
        slope = jnp.concatenate([wave_x * sine, -wave_x * cosine], axis=0)
        for i, value in enumerate(through(back_ref, [slope, plain])):
            out_ref[:, 0, i] = value.reshape(gx, x, lanes)

    block = pl.BlockSpec((gx, 1, 2, x, lanes), lambda i, j: (0, i, 0, 0, j))
    return pl.pallas_call(
        kernel,
        grid=(plan.per, ky // lanes),
        in_specs=[scalars(), whole_block(forth.shape), whole_block(back.shape), block],
        out_specs=block,
        out_shape=jax.ShapeDtypeStruct(lines.shape, jnp.float32),
        compiler_params=params(),
        cost_estimate=pl.CostEstimate(
            flops=24 * plan.per * ky * nx * nx,
            bytes_accessed=16 * plan.per * ky * nx,
            transcendentals=0,
        ),
        name="x_lines",
    )(place, jnp.asarray(forth), jnp.asarray(back), lines)


def y_inverse(plan, place, planes):
    x, y, ny, kz = plan.x, plan.y, plan.ny, plan.kz
    table = np.stack(np.split(inverse_basis(ny), plan.gy, axis=1))
    table = halves(table)
    deep = fit(kz, 8)
    rows = deep * x
    half = ny // 2
    aligned = y % 128 == 0

    def kernel(place_ref, table_ref, in_ref, *outs):
        me = place_ref[1]
        groups = [lax.rem(me + step, plan.gy) for step in range(plan.gy)]
        tables = [(table_ref[0, g], table_ref[1, g]) for g in groups]
        slope = in_ref[:, 0].reshape(rows, ny)
        plain = in_ref[:, 1].reshape(rows, ny)
        wave = lax.broadcasted_iota(jnp.int32, (1, half), 1).astype(jnp.float32)
        along = jnp.concatenate([wave * plain[:, half:], -wave * plain[:, :half]], axis=1)
        for comp, value in enumerate((slope, along, plain)):
            parts = split(value)
            if aligned:
                table = tuple(joined([t[i] for t in tables], 1) for i in range(2))
                found = times(parts, table)
                pieces = [found[:, s * y : (s + 1) * y] for s in range(plan.gy)]
            else:
                pieces = [times(parts, t) for t in tables]
            for out, piece in zip(outs, pieces):
                out[comp] = piece.reshape(deep, x, y)

    return pl.pallas_call(
        kernel,
        grid=(kz // deep,),
        in_specs=[
            scalars(),
            whole_block(table.shape),
            pl.BlockSpec((deep, 2, x, ny), lambda i: (i, 0, 0, 0)),
        ],
        out_specs=[pl.BlockSpec((3, deep, x, y), lambda i: (0, i, 0, 0))] * plan.gy,
        out_shape=[jax.ShapeDtypeStruct((3, kz, x, y), jnp.float32)] * plan.gy,
        compiler_params=params(),
        cost_estimate=pl.CostEstimate(
            flops=18 * kz * x * ny * ny, bytes_accessed=20 * kz * x * ny, transcendentals=0
        ),
        name="y_inverse",
    )(place, jnp.asarray(table), planes)


def images(plan, place, blocks, velocity, source_p, source_s):
    x, y, z, kz = plan.x, plan.y, plan.z, plan.kz
    table = np.stack([halves(inverse_basis(z)), halves(-turned(inverse_basis(z)))])
    table = table.reshape(2, 2, plan.chunks, plan.gy, kz, z)
    blocks = [block.reshape(3, kz * x, y) for group in blocks for block in group]

    group = fit(x, 8)
    deep = fit(group, 2)

    def kernel(place_ref, table_ref, v_ref, p_ref, s_ref, *refs):
        ins, (image_p, image_s) = refs[:-2], refs[-2:]
        at = pl.program_id(0) * group
        me = place_ref[1]
        order = [
            (chunk, source(me, step, plan.gy))
            for chunk in range(plan.chunks)
            for step in range(plan.gy)
        ]
        tables = []
        for kind in range(2):
            high, low = (joined([table_ref[kind, i, c, g] for c, g in order], 0) for i in range(2))
            high, low = (part.astype(jnp.float32).T.astype(jnp.bfloat16) for part in (high, low))
            tables.append((jnp.concatenate([high, high], axis=1), low))
        for plane in range(0, group, deep):
            here = slice(plane, plane + deep)
            total_p = total_s = 0.0
            for comp in range(3):
                twice, low = tables[1 if comp == 2 else 0]
                columns = [
                    joined([ref[comp, pl.ds(at + plane + k, kz, stride=x), :] for ref in ins], 0)
                    for k in range(deep)
                ]
                high, rest = split(joined(columns, 1))
                field = dot(twice, jnp.concatenate([high, rest], axis=0)) + dot(low, high)
                field = field.T.reshape(deep, y, z)
                total_p += p_ref[comp, here].astype(jnp.float32) * field
                total_s += s_ref[comp, here].astype(jnp.float32) * (v_ref[comp, here] - field)
            image_p[here] = total_p
            image_s[here] = total_s

    plane = pl.BlockSpec((3, group, y, z), lambda i: (0, i, 0, 0))
    image = pl.BlockSpec((group, y, z), lambda i: (i, 0, 0))
    return pl.pallas_call(
        kernel,
        grid=(x // group,),
        in_specs=[scalars(), whole_block(table.shape), plane, plane, plane]
        + [whole_block((3, kz * x, y))] * len(blocks),
        out_specs=[image, image],
        out_shape=[jax.ShapeDtypeStruct((x, y, z), jnp.float32)] * 2,
        compiler_params=params(),
        cost_estimate=pl.CostEstimate(
            flops=18 * x * y * z * z, bytes_accessed=44 * x * y * z, transcendentals=0
        ),
        name="images",
    )(place, jnp.asarray(table), velocity, source_p, source_s, *blocks)


def shards(velocity, stress, lame_lambda, shear_modulus, buoyancy, source_p, source_s):
    velocity = propagate(velocity, stress, lame_lambda, shear_modulus, buoyancy)
    plan = Plan(velocity.shape[1:])
    place = jnp.stack([lax.axis_index("gx"), lax.axis_index("gy")]).astype(jnp.int32)
    blocks = z_forward(plan, place, velocity)
    lines = [to_lines(plan, y_forward(plan, place, swap_gy(group))) for group in blocks]
    lines = [x_lines(plan, place, part, chunk) for chunk, part in enumerate(lines)]
    blocks = [swap_gy(y_inverse(plan, place, to_planes(plan, part))) for part in lines]
    return tuple(images(plan, place, blocks, velocity, source_p, source_s))


def solution(mesh):
    in_specs = (
        P(None, "gx", "gy", None),
        P(None, "gx", "gy", None),
        P("gx", "gy", None),
        P("gx", "gy", None),
        P("gx", "gy", None),
        P(None, "gx", "gy", None),
        P(None, "gx", "gy", None),
    )
    out_specs = (P("gx", "gy", None), P("gx", "gy", None))
    return jax.shard_map(shards, mesh=mesh, in_specs=in_specs, out_specs=out_specs, check_vma=False)
```

```python
import numpy as np
import ml_dtypes
import jax
import jax.numpy as jnp
from jax import lax
from jax.experimental import pallas as pl
from jax.experimental.pallas import tpu as pltpu
from jax.sharding import PartitionSpec as P

STEPS = 2
MOST_CHUNKS = 1
VMEM_BYTES = 56 * 2**20

time_step = 0.2


def passed_along(block, axis, distance):
    devices = range(lax.axis_size(axis))
    route = [(i - distance, i) for i in devices if i - distance in devices]
    return lax.ppermute(block, axis, route)


def across_corner(row, x_way, y_way):
    x_count, y_count = lax.axis_size("gx"), lax.axis_size("gy")
    route = [
        ((i - x_way) * y_count + j - y_way, i * y_count + j)
        for i in range(x_count)
        for j in range(y_count)
        if 0 <= i - x_way < x_count and 0 <= j - y_way < y_count
    ]
    return lax.ppermute(row, ("gx", "gy"), route)


def exchange(x_last, x_first, y_last, y_first, corner_y, corner_x):
    yl, yr = passed_along(y_last, "gy", 1), passed_along(y_first, "gy", -1)
    xl, xr = passed_along(x_last, "gx", 1), passed_along(x_first, "gx", -1)
    return (yl, yr), (xl, xr, across_corner(corner_y, -1, 1), across_corner(corner_x, 1, -1))


def first_rims(brick, velocity, stress, lame, shear):
    x, y, z = brick
    some = fit(y, 8)
    many = fit(y, 16)

    def kernel(*refs):
        (v_first, v_last, s_first, s_last, lame_first, shear_first, shear_last) = refs[:7]
        (v_low, v_high, s_low, s_high, lame_low, shear_low, shear_high) = refs[7:14]
        x_last, x_first, y_last, y_first, corner_y, corner_x = refs[14:]

        def wide(value):
            return value.astype(jnp.float32)

        for i in range(3):
            x_last[i], x_first[i] = v_last[i, 0], v_first[i, 0]
            y_last[i], y_first[i] = v_high[i, :, some - 1], v_low[i, :, 0]
        x_last[3], x_last[4], x_last[5] = s_last[3, 0], s_last[4, 0], wide(shear_last[0])
        x_first[3], x_first[4], x_first[5] = s_first[0, 0], wide(lame_first[0]), wide(shear_first[0])
        y_last[3], y_last[4] = s_high[3, :, some - 1], s_high[5, :, some - 1]
        y_last[5] = wide(shear_high[...])[:, many - 1]
        y_first[3], y_first[4] = s_low[1, :, 0], wide(lame_low[...])[:, 0]
        y_first[5] = wide(shear_low[...])[:, 0]
        corner_y[...] = v_first[1, 0, y - 1 :]
        corner_x[...] = v_last[0, 0, :1]

    def plane(count, at):
        return pl.BlockSpec((count, 1, y, z), lambda i: (0, at, 0, 0))

    def medium_plane(at):
        return pl.BlockSpec((1, y, z), lambda i: (at, 0, 0))

    def rows(count, at):
        return pl.BlockSpec((count, x, some, z), lambda i: (0, 0, at, 0))

    def medium_rows(at):
        return pl.BlockSpec((x, many, z), lambda i: (0, at, 0))

    shapes = [(6, y, z), (6, y, z), (6, x, z), (6, x, z), (1, z), (1, z)]
    ends, highs, most = x - 1, y // some - 1, y // many - 1
    return pl.pallas_call(
        kernel,
        grid=(1,),
        in_specs=[plane(3, 0), plane(3, ends), plane(6, 0), plane(6, ends)]
        + [medium_plane(0), medium_plane(0), medium_plane(ends)]
        + [rows(3, 0), rows(3, highs), rows(6, 0), rows(6, highs)]
        + [medium_rows(0), medium_rows(0), medium_rows(most)],
        out_specs=[whole_block(shape) for shape in shapes],
        out_shape=[jax.ShapeDtypeStruct(shape, jnp.float32) for shape in shapes],
        compiler_params=params(),
        cost_estimate=pl.CostEstimate(
            flops=0, bytes_accessed=80 * (y + 8 * x) * z, transcendentals=0
        ),
        name="first_rims",
    )(
        *(velocity, velocity, stress, stress, lame, shear, shear),
        *(velocity, velocity, stress, stress, lame, shear, shear),
    )


def stencil(brick, state, rims, medium, x_rims, x_medium, done, last):
    x, y, z = brick
    velocity, stress, lame, shear, buoyancy = state
    group = fit(x, 4)
    groups = x // group
    ends = x_rims is not None
    if ends:
        count, of = min(groups, 2), lambda i: i * (groups - 1)
    else:
        count, of = groups - 2, lambda i: i + 1
    f32 = jnp.float32

    def kernel(*refs):
        refs = list(refs)

        def take(number):
            taken = refs[:number]
            del refs[:number]
            return taken

        v_ref, s_ref, lame_ref, shear_ref, buoy_ref = take(5)
        v_next_ref, xx_next_ref, lame_next_ref, shear_next_ref = take(4)
        v_prior_ref, xy_prior_ref, xz_prior_ref, shear_prior_ref = take(4)
        yl, yr = take(2)
        yl_medium, yr_medium = take(2) if medium else (yl, yr)
        if ends:
            xl, xr, edge_y, edge_x = take(4)
            xl_medium, xr_medium = take(2) if medium else (xl, xr)
        given = take(len(done))
        new = take(1)[0]
        if not last:
            s_out, y_last, y_first = take(3)
            if ends:
                x_last, x_first, corner_y, corner_x = take(4)
        carried = take(1)[0]
        turn = pl.program_id(0)
        here_group = of(turn)
        at = here_group * group
        start, end = here_group == 0, here_group == groups - 1
        row = lax.broadcasted_iota(jnp.int32, (y, z), 0)
        lane = lax.broadcasted_iota(jnp.int32, (y, z), 1)
        first_row, last_row = row == 0, row == y - 1
        first_lane, last_lane = lane == 0, lane == z - 1

        def next_z(field):
            edge = last_lane if field.shape[0] == y else last_lane[:1]
            return jnp.where(edge, 0.0, pltpu.roll(field, z - 1, 1))

        def prior_z(field):
            edge = first_lane if field.shape[0] == y else first_lane[:1]
            return jnp.where(edge, 0.0, pltpu.roll(field, 1, 1))

        def next_y(field, rim):
            return jnp.where(last_row, rim, pltpu.roll(field, y - 1, 0))

        def prior_y(field, rim):
            return jnp.where(first_row, rim, pltpu.roll(field, 1, 0))

        def wide(value):
            return value.astype(f32)

        def line(ref, which, place):
            return ref[which, pl.ds(place, 1), :]

        def line_after(place):
            if not ends:
                return line(yl, 1, place)
            return jnp.where(place == x, edge_y[...], line(yl, 1, jnp.minimum(place, x - 1)))

        def line_before(place):
            if not ends:
                return line(yr, 0, place)
            return jnp.where(place < 0, edge_x[...], line(yr, 0, jnp.maximum(place, 0)))

        def begin(value, rim):
            return jnp.where(start, rim(), value) if ends else value

        def finish(value, rim):
            return jnp.where(end, rim(), value) if ends else value

        def fresh():
            shear_rim = begin(wide(shear_prior_ref[0]), lambda: xl_medium[5])
            vx, vy, vz = (begin(v_prior_ref[i, 0], lambda: xl[i]) for i in range(3))
            xy = begin(xy_prior_ref[0, 0], lambda: xl[3])
            xz = begin(xz_prior_ref[0, 0], lambda: xl[4])
            pull = time_step * shear_rim
            carried[0] = vx
            carried[1] = xy + pull * ((next_y(vx, line_before(at - 1)) - vx) + (v_ref[1, 0] - vy))
            carried[2] = xz + pull * ((next_z(vx) - vx) + (v_ref[2, 0] - vz))

        if ends:
            fresh()
        else:
            pl.when(turn == 0)(fresh)
        if not last and done:

            @pl.when(turn == 0)
            def _():
                y_last[...] = given[2][...]
                y_first[...] = given[3][...]

        after = [finish(v_next_ref[i, 0], lambda: xr[i]) for i in range(3)]
        stresses = []
        vx_prior = carried[0]
        for k in range(group):
            vx, vy, vz = v_ref[0, k], v_ref[1, k], v_ref[2, k]
            vy_next = after[1] if k == group - 1 else v_ref[1, k + 1]
            vz_next = after[2] if k == group - 1 else v_ref[2, k + 1]
            lame_value, shear_value = wide(lame_ref[k]), wide(shear_ref[k])
            ex = vx - vx_prior
            ey = vy - prior_y(vy, line(yl, 1, at + k))
            ez = vz - prior_z(vz)
            swell = lame_value * (ex + ey + ez)
            double = 2.0 * shear_value
            xx = s_ref[0, k] + time_step * (swell + double * ex)
            yy = s_ref[1, k] + time_step * (swell + double * ey)
            zz = s_ref[2, k] + time_step * (swell + double * ez)
            pull = time_step * shear_value
            xy = s_ref[3, k] + pull * ((next_y(vx, line(yr, 0, at + k)) - vx) + (vy_next - vy))
            xz = s_ref[4, k] + pull * ((next_z(vx) - vx) + (vz_next - vz))
            yz = s_ref[5, k] + pull * (
                (next_z(vy) - vy) + (next_y(vz, line(yr, 2, at + k)) - vz)
            )
            stresses.append((xx, yy, zz, xy, xz, yz))
            vx_prior = vx

        ex = after[0] - vx_prior
        ey = after[1] - prior_y(after[1], line_after(at + group))
        ez = after[2] - prior_z(after[2])
        lame_value = finish(wide(lame_next_ref[0]), lambda: xr_medium[4])
        shear_value = finish(wide(shear_next_ref[0]), lambda: xr_medium[5])
        xx_after = finish(xx_next_ref[0, 0], lambda: xr[3]) + time_step * (
            lame_value * (ex + ey + ez) + 2.0 * shear_value * ex
        )

        xy_prior, xz_prior = carried[1], carried[2]
        for k in range(group):
            xx, yy, zz, xy, xz, yz = stresses[k]
            xx_next = xx_after if k == group - 1 else stresses[k + 1][0]
            here = at + k
            vx, vy, vz = v_ref[0, k], v_ref[1, k], v_ref[2, k]
            pull = time_step * line(yl_medium, 5, here)
            vy_rim, vz_rim = line(yl, 1, here), line(yl, 2, here)
            xy_rim = line(yl, 3, here) + pull * (
                (vx[:1] - line(yl, 0, here)) + (line_after(here + 1) - vy_rim)
            )
            yz_rim = line(yl, 4, here) + pull * ((next_z(vy_rim) - vy_rim) + (vz[:1] - vz_rim))
            vx_rim, vz_rim = line(yr, 0, here), line(yr, 2, here)
            ex = vx_rim - line_before(here - 1)
            ey = line(yr, 1, here) - vy[-1:]
            ez = vz_rim - prior_z(vz_rim)
            yy_rim = line(yr, 3, here) + time_step * (
                line(yr_medium, 4, here) * (ex + ey + ez) + 2.0 * line(yr_medium, 5, here) * ey
            )
            push = time_step * wide(buoy_ref[k])
            vx = vx + push * (
                (xx_next - xx) + (xy - prior_y(xy, xy_rim)) + (xz - prior_z(xz))
            )
            vy = vy + push * ((xy - xy_prior) + (next_y(yy, yy_rim) - yy) + (yz - prior_z(yz)))
            vz = vz + push * ((xz - xz_prior) + (yz - prior_y(yz, yz_rim)) + (next_z(zz) - zz))
            xy_prior, xz_prior = xy, xz
            for i, value in enumerate((vx, vy, vz)):
                new[i, k] = value
            if last:
                continue
            for i, value in enumerate((xx, yy, zz, xy, xz, yz)):
                s_out[i, k] = value
            for i, value in enumerate((vx, vy, vz, xy, yz)):
                y_last[i, pl.ds(here, 1), :] = value[-1:]
            for i, value in enumerate((vx, vy, vz, yy)):
                y_first[i, pl.ds(here, 1), :] = value[:1]
            if ends and k == 0:

                @pl.when(start)
                def _():
                    for i, value in enumerate((vx, vy, vz, xx)):
                        x_first[i] = value
                    corner_y[...] = vy[-1:]

            if ends and k == group - 1:

                @pl.when(end)
                def _():
                    for i, value in enumerate((vx, vy, vz, xy, xz)):
                        x_last[i] = value
                    corner_x[...] = vx[:1]

        if not ends:
            carried[0] = v_ref[0, group - 1]
            carried[1] = stresses[-1][3]
            carried[2] = stresses[-1][4]

    def next_plane(i):
        return jnp.minimum((of(i) + 1) * group, x - 1)

    def prior_plane(i):
        return jnp.maximum(of(i) * group - 1, 0)

    def planes(number):
        return pl.BlockSpec((number, group, y, z), lambda i: (0, of(i), 0, 0))

    def one(number, which, place):
        return pl.BlockSpec((number, 1, y, z), lambda i: (which, place(i), 0, 0))

    def medium_one(place):
        return pl.BlockSpec((1, y, z), lambda i: (place(i), 0, 0))

    medium_block = pl.BlockSpec((group, y, z), lambda i: (of(i), 0, 0))
    args = [velocity, stress, lame, shear, buoyancy, velocity, stress, lame, shear]
    args += [velocity, stress, stress, shear, *rims, *medium]
    in_specs = [planes(3), planes(6), medium_block, medium_block, medium_block]
    in_specs += [one(3, 0, next_plane), one(1, 0, next_plane)]
    in_specs += [medium_one(next_plane), medium_one(next_plane)]
    in_specs += [one(3, 0, prior_plane), one(1, 3, prior_plane), one(1, 4, prior_plane)]
    in_specs += [medium_one(prior_plane)]
    in_specs += [whole_block(rim.shape) for rim in (*rims, *medium)]
    if ends:
        args += [*x_rims, *x_medium]
        in_specs += [whole_block(rim.shape) for rim in (*x_rims, *x_medium)]
    aliases = {}
    for i, value in enumerate(done):
        if i < 2:
            aliases[len(args)] = i
        in_specs.append(unread() if i < 2 else whole_block(value.shape))
        args.append(value)
    out_shape = [(3, x, y, z)]
    out_specs = [planes(3)]
    if not last:
        out_shape += [(6, x, y, z), (5, x, z), (4, x, z)]
        out_specs += [planes(6)]
        if ends:
            out_shape += [(5, y, z), (4, y, z), (1, z), (1, z)]
        out_specs += [whole_block(shape) for shape in out_shape[2:]]
    part = count * group * y * z
    return pl.pallas_call(
        kernel,
        grid=(count,),
        in_specs=in_specs,
        out_specs=out_specs,
        out_shape=[jax.ShapeDtypeStruct(shape, f32) for shape in out_shape],
        scratch_shapes=[pltpu.VMEM((3, y, z), f32)],
        input_output_aliases=aliases,
        compiler_params=params(),
        cost_estimate=pl.CostEstimate(
            flops=80 * part, bytes_accessed=(54 if last else 78) * part, transcendentals=0
        ),
        name="stencil_ends" if ends else "stencil_middle",
    )(*args)


def propagate(velocity, stress, lame, shear, buoyancy):
    brick = velocity.shape[1:]
    between = brick[0] // fit(brick[0], 4) > 2
    rims, x_rims = exchange(*first_rims(brick, velocity, stress, lame, shear))
    held, medium, x_medium = (rims, x_rims[:2]), (), ()
    for step_index in range(STEPS):
        last = step_index == STEPS - 1
        state = (velocity, stress, lame, shear, buoyancy)
        done = []
        if between:
            done = stencil(brick, state, rims, medium, None, None, done, last)
        found = stencil(brick, state, rims, medium, x_rims, x_medium, done, last)
        velocity = found[0]
        if not last:
            stress, y_last, y_first, x_last, x_first, corner_y, corner_x = found[1:]
            rims, x_rims = exchange(x_last, x_first, y_last, y_first, corner_y, corner_x)
            medium, x_medium = held
    return velocity


def basis(length):
    half = length // 2
    wave = np.arange(half)
    place = np.arange(length)
    angle = (wave[:, None] * place[None, :] % length) * (2.0 * np.pi / length)
    cosine, sine = np.cos(angle), np.sin(angle)
    sine[0] = 1.0 - 2.0 * (place % 2)
    return np.concatenate([cosine, sine])


def waves_of(length):
    return np.tile(np.arange(length // 2, dtype=np.float64), 2)


def inverse_basis(length):
    weight = np.where(waves_of(length) == 0, 1.0, 2.0) / length
    return basis(length) * weight[:, None]


def turned(table):
    half = table.shape[0] // 2
    return np.concatenate([table[half:], -table[:half]]) * waves_of(table.shape[0])[:, None]


def halves(table):
    high = table.astype(ml_dtypes.bfloat16)
    low = (table - high.astype(np.float64)).astype(ml_dtypes.bfloat16)
    return np.stack([high, low])


def split(value):
    high = value.astype(jnp.bfloat16)
    return high, (value - high.astype(jnp.float32)).astype(jnp.bfloat16)


def dot(left, right, dims=((1,), (0,))):
    return lax.dot_general(left, right, (dims, ((), ())), preferred_element_type=jnp.float32)


def times(left, right):
    return dot(left[0], right[0]) + (dot(left[1], right[0]) + dot(left[0], right[1]))


def joined(pieces, axis):
    return pieces[0] if len(pieces) == 1 else jnp.concatenate(pieces, axis=axis)


def fit(length, most):
    size = min(length, most)
    while length % size:
        size -= 1
    return size


def params():
    return pltpu.CompilerParams(vmem_limit_bytes=VMEM_BYTES)


def whole_block(shape):
    return pl.BlockSpec(shape, lambda *_: (0,) * len(shape))


def scalars():
    return pl.BlockSpec(memory_space=pltpu.SMEM)


class Plan:
    def __init__(self, brick):
        self.x, self.y, self.z = brick
        self.gx, self.gy = lax.axis_size("gx"), lax.axis_size("gy")
        self.nx, self.ny = self.x * self.gx, self.y * self.gy
        chunks = MOST_CHUNKS
        while chunks > 1 and self.z % (chunks * self.gy * self.gx):
            chunks -= 1
        self.chunks = chunks
        self.kz = self.z // (chunks * self.gy)
        self.parts = max(1, self.gx // self.kz)
        self.per = max(1, self.kz // self.gx)
        self.ky = self.ny // self.parts


def source(me, step, count):
    return lax.rem(me - step + count, count)


def z_forward(plan, place, velocity):
    x, y, z, kz = plan.x, plan.y, plan.z, plan.kz
    table = np.stack([halves(basis(z)), halves(turned(basis(z)))])
    table = table.reshape(2, 2, plan.chunks, plan.gy, kz, z)
    count = plan.chunks * plan.gy

    group = fit(x, 8)
    deep = fit(group, 2)

    def kernel(place_ref, table_ref, v_ref, *outs):
        at = pl.program_id(0) * group
        me = place_ref[1]
        order = [(c, lax.rem(me + s, plan.gy)) for c in range(plan.chunks) for s in range(plan.gy)]
        tables = []
        for kind in range(2):
            high, low = (joined([table_ref[kind, i, c, g] for c, g in order], 0) for i in range(2))
            tables.append((jnp.concatenate([high, high], axis=1), low))
        for comp in range(3):
            twice, low = tables[1 if comp == 2 else 0]
            for plane in range(0, group, deep):
                field = split(v_ref[comp, plane : plane + deep].reshape(deep * y, z))
                value = dot(twice, jnp.concatenate(field, axis=1), ((1,), (1,)))
                value += dot(low, field[0], ((1,), (1,)))
                for i, out in enumerate(outs):
                    for k in range(deep):
                        part = value[i * kz : (i + 1) * kz, k * y : (k + 1) * y]
                        out[comp, pl.ds(at + plane + k, kz, stride=x), :] = part

    outs = pl.pallas_call(
        kernel,
        grid=(x // group,),
        in_specs=[
            scalars(),
            whole_block(table.shape),
            pl.BlockSpec((3, group, y, z), lambda i: (0, i, 0, 0)),
        ],
        out_specs=[whole_block((3, kz * x, y))] * count,
        out_shape=[jax.ShapeDtypeStruct((3, kz * x, y), jnp.float32)] * count,
        compiler_params=params(),
        cost_estimate=pl.CostEstimate(
            flops=18 * x * y * z * z, bytes_accessed=24 * x * y * z, transcendentals=0
        ),
        name="z_forward",
    )(place, jnp.asarray(table), velocity)
    outs = [out.reshape(3, kz, x, y) for out in outs]
    return [outs[c * plan.gy : (c + 1) * plan.gy] for c in range(plan.chunks)]


def swap_gy(blocks):
    count = len(blocks)
    moved = [blocks[0]]
    for step in range(1, count):
        route = [(i, (i + step) % count) for i in range(count)]
        moved.append(lax.ppermute(blocks[step], "gy", route))
    return moved


def y_forward(plan, place, blocks):
    x, y, ny, kz = plan.x, plan.y, plan.ny, plan.kz
    table = halves(basis(ny).T).reshape(2, plan.gy, y, ny)
    deep = fit(kz, 8)
    rows = deep * x
    half = ny // 2
    aligned = y % 128 == 0

    def kernel(place_ref, table_ref, *refs):
        ins, out = refs[:-1], refs[-1]
        me = place_ref[1]
        groups = [source(me, step, plan.gy) for step in range(plan.gy)]
        tables = [(table_ref[0, g], table_ref[1, g]) for g in groups]
        if aligned:
            tables = [tuple(joined([t[i] for t in tables], 0) for i in range(2))]

        def moved(comp):
            fields = [ref[comp].reshape(rows, y) for ref in ins]
            if aligned:
                fields = [joined(fields, 1)]
            return sum(times(split(f), t) for f, t in zip(fields, tables))

        wave = lax.broadcasted_iota(jnp.int32, (1, half), 1).astype(jnp.float32)
        out[:, 0] = moved(0).reshape(deep, x, ny)
        along, rest = moved(1), moved(2)
        out[:, 1, :, :half] = (rest[:, :half] + wave * along[:, half:]).reshape(deep, x, half)
        out[:, 1, :, half:] = (rest[:, half:] - wave * along[:, :half]).reshape(deep, x, half)

    return pl.pallas_call(
        kernel,
        grid=(kz // deep,),
        in_specs=[scalars(), whole_block(table.shape)]
        + [pl.BlockSpec((3, deep, x, y), lambda i: (0, i, 0, 0))] * plan.gy,
        out_specs=pl.BlockSpec((deep, 2, x, ny), lambda i: (i, 0, 0, 0)),
        out_shape=jax.ShapeDtypeStruct((kz, 2, x, ny), jnp.float32),
        compiler_params=params(),
        cost_estimate=pl.CostEstimate(
            flops=18 * kz * x * ny * ny, bytes_accessed=20 * kz * x * ny, transcendentals=0
        ),
        name="y_forward",
    )(place, jnp.asarray(table), *blocks)


def to_lines(plan, planes):
    if plan.parts > 1:
        planes = planes.reshape(plan.kz, 2, plan.x, plan.parts, plan.ky).transpose(0, 3, 1, 2, 4)
    planes = planes.reshape(plan.gx, plan.per, 2, plan.x, plan.ky)
    return lax.all_to_all(planes, "gx", 0, 0, tiled=True)


def to_planes(plan, lines):
    planes = lax.all_to_all(lines, "gx", 0, 0, tiled=True)
    if plan.parts > 1:
        planes = planes.reshape(plan.kz, plan.parts, 2, plan.x, plan.ky).transpose(0, 2, 3, 1, 4)
    return planes.reshape(plan.kz, 2, plan.x, plan.ny)


def x_lines(plan, place, lines, chunk):
    x, nx, ny, ky, gx = plan.x, plan.nx, plan.ny, plan.ky, plan.gx
    forth = halves(basis(nx))
    back = halves(-inverse_basis(nx).T)
    lanes = 128 if ky % 128 == 0 else ky
    half = nx // 2
    aligned = lanes % 128 == 0

    def kernel(place_ref, forth_ref, back_ref, in_ref, out_ref):
        me_x, me_y = place_ref[0], place_ref[1]
        which, lane = pl.program_id(0), pl.program_id(1)

        def through(table_ref, pair):
            table = (table_ref[0], table_ref[1])
            if aligned:
                both = times(table, split(jnp.concatenate(pair, axis=1)))
                return both[:, :lanes], both[:, lanes:]
            return tuple(times(table, split(value)) for value in pair)

        pair = [in_ref[:, 0, i].reshape(nx, lanes) for i in range(2)]
        along, rest = through(forth_ref, pair)
        wave_x = lax.broadcasted_iota(jnp.int32, (half, lanes), 0).astype(jnp.float32)
        slot_y = lax.broadcasted_iota(jnp.int32, (1, lanes), 1) + (
            lane * lanes + lax.rem(me_x, plan.parts) * ky
        )
        wave_y = lax.rem(slot_y, ny // 2).astype(jnp.float32)
        slot_z = (chunk * plan.gy + me_y) * plan.kz + me_x // plan.parts * plan.per + which
        wave_z = lax.rem(slot_z, plan.z // 2).astype(jnp.float32)
        scale = 1.0 / jnp.maximum(wave_x * wave_x + (wave_y * wave_y + wave_z * wave_z), 1.0)
        cosine = (rest[:half] + wave_x * along[half:]) * scale
        sine = (rest[half:] - wave_x * along[:half]) * scale
        plain = jnp.concatenate([cosine, sine], axis=0)
        slope = jnp.concatenate([wave_x * sine, -wave_x * cosine], axis=0)
        for i, value in enumerate(through(back_ref, [slope, plain])):
            out_ref[:, 0, i] = value.reshape(gx, x, lanes)

    block = pl.BlockSpec((gx, 1, 2, x, lanes), lambda i, j: (0, i, 0, 0, j))
    return pl.pallas_call(
        kernel,
        grid=(plan.per, ky // lanes),
        in_specs=[scalars(), whole_block(forth.shape), whole_block(back.shape), block],
        out_specs=block,
        out_shape=jax.ShapeDtypeStruct(lines.shape, jnp.float32),
        compiler_params=params(),
        cost_estimate=pl.CostEstimate(
            flops=24 * plan.per * ky * nx * nx,
            bytes_accessed=16 * plan.per * ky * nx,
            transcendentals=0,
        ),
        name="x_lines",
    )(place, jnp.asarray(forth), jnp.asarray(back), lines)


def y_inverse(plan, place, planes):
    x, y, ny, kz = plan.x, plan.y, plan.ny, plan.kz
    table = np.stack(np.split(inverse_basis(ny), plan.gy, axis=1))
    table = halves(table)
    deep = fit(kz, 8)
    rows = deep * x
    half = ny // 2
    aligned = y % 128 == 0

    def kernel(place_ref, table_ref, in_ref, *outs):
        me = place_ref[1]
        groups = [lax.rem(me + step, plan.gy) for step in range(plan.gy)]
        tables = [(table_ref[0, g], table_ref[1, g]) for g in groups]
        slope = in_ref[:, 0].reshape(rows, ny)
        plain = in_ref[:, 1].reshape(rows, ny)
        wave = lax.broadcasted_iota(jnp.int32, (1, half), 1).astype(jnp.float32)
        along = jnp.concatenate([wave * plain[:, half:], -wave * plain[:, :half]], axis=1)
        for comp, value in enumerate((slope, along, plain)):
            parts = split(value)
            if aligned:
                table = tuple(joined([t[i] for t in tables], 1) for i in range(2))
                found = times(parts, table)
                pieces = [found[:, s * y : (s + 1) * y] for s in range(plan.gy)]
            else:
                pieces = [times(parts, t) for t in tables]
            for out, piece in zip(outs, pieces):
                out[comp] = piece.reshape(deep, x, y)

    return pl.pallas_call(
        kernel,
        grid=(kz // deep,),
        in_specs=[
            scalars(),
            whole_block(table.shape),
            pl.BlockSpec((deep, 2, x, ny), lambda i: (i, 0, 0, 0)),
        ],
        out_specs=[pl.BlockSpec((3, deep, x, y), lambda i: (0, i, 0, 0))] * plan.gy,
        out_shape=[jax.ShapeDtypeStruct((3, kz, x, y), jnp.float32)] * plan.gy,
        compiler_params=params(),
        cost_estimate=pl.CostEstimate(
            flops=18 * kz * x * ny * ny, bytes_accessed=20 * kz * x * ny, transcendentals=0
        ),
        name="y_inverse",
    )(place, jnp.asarray(table), planes)


def images(plan, place, blocks, velocity, source_p, source_s):
    x, y, z, kz = plan.x, plan.y, plan.z, plan.kz
    table = np.stack([halves(inverse_basis(z)), halves(-turned(inverse_basis(z)))])
    table = table.reshape(2, 2, plan.chunks, plan.gy, kz, z)
    blocks = [block.reshape(3, kz * x, y) for group in blocks for block in group]

    group = fit(x, 8)
    deep = fit(group, 2)

    def kernel(place_ref, table_ref, v_ref, p_ref, s_ref, *refs):
        ins, (image_p, image_s) = refs[:-2], refs[-2:]
        at = pl.program_id(0) * group
        me = place_ref[1]
        order = [
            (chunk, source(me, step, plan.gy))
            for chunk in range(plan.chunks)
            for step in range(plan.gy)
        ]
        tables = []
        for kind in range(2):
            high, low = (joined([table_ref[kind, i, c, g] for c, g in order], 0) for i in range(2))
            high, low = (part.astype(jnp.float32).T.astype(jnp.bfloat16) for part in (high, low))
            tables.append((jnp.concatenate([high, high], axis=1), low))
        for plane in range(0, group, deep):
            here = slice(plane, plane + deep)
            total_p = total_s = 0.0
            for comp in range(3):
                twice, low = tables[1 if comp == 2 else 0]
                columns = [
                    joined([ref[comp, pl.ds(at + plane + k, kz, stride=x), :] for ref in ins], 0)
                    for k in range(deep)
                ]
                high, rest = split(joined(columns, 1))
                field = dot(twice, jnp.concatenate([high, rest], axis=0)) + dot(low, high)
                field = field.T.reshape(deep, y, z)
                total_p += p_ref[comp, here].astype(jnp.float32) * field
                total_s += s_ref[comp, here].astype(jnp.float32) * (v_ref[comp, here] - field)
            image_p[here] = total_p
            image_s[here] = total_s

    plane = pl.BlockSpec((3, group, y, z), lambda i: (0, i, 0, 0))
    image = pl.BlockSpec((group, y, z), lambda i: (i, 0, 0))
    return pl.pallas_call(
        kernel,
        grid=(x // group,),
        in_specs=[scalars(), whole_block(table.shape), plane, plane, plane]
        + [whole_block((3, kz * x, y))] * len(blocks),
        out_specs=[image, image],
        out_shape=[jax.ShapeDtypeStruct((x, y, z), jnp.float32)] * 2,
        compiler_params=params(),
        cost_estimate=pl.CostEstimate(
            flops=18 * x * y * z * z, bytes_accessed=44 * x * y * z, transcendentals=0
        ),
        name="images",
    )(place, jnp.asarray(table), velocity, source_p, source_s, *blocks)


def doubled(table, axis):
    high, low = halves(table)
    return np.concatenate([high, high], axis=axis), low


def left_times(table, value):
    high, low = split(value)
    return dot(table[0], jnp.concatenate([high, low], axis=0)) + dot(table[1], high)


def right_times(value, table):
    high, low = split(value)
    return dot(jnp.concatenate([high, low], axis=1), table[0]) + dot(high, table[1])


def side_by_side(table, values):
    width = values[0].shape[1]
    if width % 128:
        return [left_times(table, value) for value in values]
    both = left_times(table, joined(values, 1))
    return [both[:, i * width : (i + 1) * width] for i in range(len(values))]


def cost(flops, values):
    return pl.CostEstimate(flops=6 * flops, bytes_accessed=4 * values, transcendentals=0)


WEIGHT = 1000


def crossed(table, plan):
    shape = (plan.gy, plan.gx, plan.per, table.shape[-1])
    return table.reshape(shape).transpose(1, 0, 2, 3).reshape(table.shape)


def unread():
    return pl.BlockSpec(memory_space=pl.ANY)


def along_z(plan, place, velocity, comps, tables, outs, ahead=()):
    x, y, z = plan.x, plan.y, plan.z
    table = np.stack([halves(table) for table in tables]).reshape(len(comps), 2, outs, z // outs, z)
    group = fit(x, 8)
    deep = fit(group, 2)
    rows = z // outs

    def kernel(place_ref, table_ref, *refs):
        fields, found = refs[: len(comps)], refs[len(comps) + len(ahead) :]
        at = pl.program_id(0) * group
        me = place_ref[1]
        order = [lax.rem(me + s, outs) if outs > 1 else 0 for s in range(outs)]
        for comp, field in enumerate(fields):
            high, low = (joined([table_ref[comp, i, g] for g in order], 0) for i in range(2))
            twice = jnp.concatenate([high, high], axis=1)
            for plane in range(0, group, deep):
                parts = split(field[0, plane : plane + deep].reshape(deep * y, z))
                value = dot(twice, jnp.concatenate(parts, axis=1), ((1,), (1,)))
                value += dot(low, parts[0], ((1,), (1,)))
                for i, out in enumerate(found):
                    for k in range(deep):
                        part = value[i * rows : (i + 1) * rows, k * y : (k + 1) * y]
                        out[comp, pl.ds(at + plane + k, rows, stride=x), :] = part

    def block(comp):
        return pl.BlockSpec((1, group, y, z), lambda i: (comp, i, 0, 0))

    shape = (len(comps), rows * x, y)
    found = pl.pallas_call(
        kernel,
        grid=(x // group,),
        in_specs=[scalars(), whole_block(table.shape)]
        + [block(comp) for comp in comps]
        + [unread()] * len(ahead),
        out_specs=[whole_block(shape)] * outs,
        out_shape=[jax.ShapeDtypeStruct(shape, jnp.float32)] * outs,
        compiler_params=params(),
        cost_estimate=cost(len(comps) * x * y * z * z, 2 * len(comps) * x * y * z),
        name="along_z",
    )(place, jnp.asarray(table), *[velocity] * len(comps), *ahead)
    return [out.reshape(len(comps), rows, x, y) for out in found]


def y_table(plan, table_ref, groups):
    tables = [(table_ref[0, g], table_ref[1, g]) for g in groups]
    if plan.y % 128 == 0:
        high, low = (joined([table[i] for table in tables], 0) for i in range(2))
        return [(jnp.concatenate([high, high], axis=0), low)]
    return [(jnp.concatenate([high, high], axis=0), low) for high, low in tables]


def over_y(fields, tables):
    if len(tables) == 1:
        fields = [joined(fields, 1)]
    return sum(right_times(field, table) for field, table in zip(fields, tables))


def pair_y_forward(plan, place, blocks):
    x, y, ny = plan.x, plan.y, plan.ny
    count = blocks[0].shape[1]
    table = halves(basis(ny).T).reshape(2, plan.gy, y, ny)
    deep = fit(count, 8)
    rows = deep * x
    half = ny // 2

    def kernel(place_ref, table_ref, *refs):
        ins, out = refs[:-1], refs[-1]
        me = place_ref[1]
        tables = y_table(plan, table_ref, [source(me, s, plan.gy) for s in range(plan.gy)])
        along, rest = (
            over_y([ref[comp].reshape(rows, y) for ref in ins], tables) for comp in range(2)
        )
        wave = lax.broadcasted_iota(jnp.int32, (1, half), 1).astype(jnp.float32)
        out[:, :, :half] = (rest[:, :half] + wave * along[:, half:]).reshape(deep, x, half)
        out[:, :, half:] = (rest[:, half:] - wave * along[:, :half]).reshape(deep, x, half)

    return pl.pallas_call(
        kernel,
        grid=(count // deep,),
        in_specs=[scalars(), whole_block(table.shape)]
        + [pl.BlockSpec((2, deep, x, y), lambda i: (0, i, 0, 0))] * plan.gy,
        out_specs=pl.BlockSpec((deep, x, ny), lambda i: (i, 0, 0)),
        out_shape=jax.ShapeDtypeStruct((count, x, ny), jnp.float32),
        compiler_params=params(),
        cost_estimate=cost(2 * WEIGHT * count * x * ny * ny, 3 * WEIGHT * count * x * ny),
        name="pair_y_forward",
    )(place, jnp.asarray(table), *blocks)


def first_x_forward(plan, place, lines):
    x, y, nx = plan.x, plan.y, plan.nx
    twice, low = doubled(basis(nx), 1)

    def kernel(place_ref, twice_ref, low_ref, in_ref, *outs):
        me = place_ref[1]
        fields = [in_ref[:, lax.rem(me + s, plan.gy), 0].reshape(nx, y) for s in range(plan.gy)]
        found = side_by_side((twice_ref[...], low_ref[...]), fields)
        for out, value in zip(outs, found):
            out[0] = value

    return pl.pallas_call(
        kernel,
        grid=(plan.per,),
        in_specs=[
            scalars(),
            whole_block(twice.shape),
            whole_block(low.shape),
            pl.BlockSpec((plan.gx, plan.gy, 1, x, y), lambda i: (0, 0, i, 0, 0)),
        ],
        out_specs=[pl.BlockSpec((1, nx, y), lambda i: (i, 0, 0))] * plan.gy,
        out_shape=[jax.ShapeDtypeStruct((plan.per, nx, y), jnp.float32)] * plan.gy,
        compiler_params=params(),
        cost_estimate=cost(plan.per * plan.ny * nx * nx, 2 * plan.per * plan.ny * nx),
        name="first_x_forward",
    )(place, jnp.asarray(twice), jnp.asarray(low), lines)


def slope_x(value):
    half = value.shape[0] // 2
    wave = lax.broadcasted_iota(jnp.int32, (half, 1), 0).astype(jnp.float32)
    return wave * value[half:], -wave * value[:half]


def first_y_forward(plan, place, blocks):
    y, nx, ny = plan.y, plan.nx, plan.ny
    table = halves(basis(ny).T).reshape(2, plan.gy, y, ny)
    half = nx // 2

    def kernel(place_ref, table_ref, *refs):
        ins, out = refs[:-1], refs[-1]
        me = place_ref[1]
        tables = y_table(plan, table_ref, [source(me, s, plan.gy) for s in range(plan.gy)])
        cosine, sine = slope_x(over_y([ref[0] for ref in ins], tables))
        out[0, :half] = cosine
        out[0, half:] = sine

    return pl.pallas_call(
        kernel,
        grid=(plan.per,),
        in_specs=[scalars(), whole_block(table.shape)]
        + [pl.BlockSpec((1, nx, y), lambda i: (i, 0, 0))] * plan.gy,
        out_specs=pl.BlockSpec((1, nx, ny), lambda i: (i, 0, 0)),
        out_shape=jax.ShapeDtypeStruct((plan.per, nx, ny), jnp.float32),
        compiler_params=params(),
        cost_estimate=cost(plan.per * nx * ny * ny, 2 * plan.per * nx * ny),
        name="first_y_forward",
    )(place, jnp.asarray(table), *blocks)


def potential(plan, place, first, lines):
    x, nx, ny, gx = plan.x, plan.nx, plan.ny, plan.gx
    forth_twice, forth_low = doubled(basis(nx), 1)
    back_twice, back_low = doubled(-inverse_basis(nx).T, 1)
    half = nx // 2

    def kernel(place_ref, ft_ref, fl_ref, bt_ref, bl_ref, first_ref, in_ref, out_ref, slope_ref):
        me_x, me_y = place_ref[0], place_ref[1]
        total = left_times((ft_ref[...], fl_ref[...]), in_ref[:, 0].reshape(nx, ny))
        wave_x = lax.broadcasted_iota(jnp.int32, (half, 1), 0).astype(jnp.float32)
        slot_y = lax.broadcasted_iota(jnp.int32, (1, ny), 1)
        wave_y = lax.rem(slot_y, ny // 2).astype(jnp.float32)
        slot_z = (me_y * gx + me_x) * plan.per + pl.program_id(0)
        wave_z = lax.rem(slot_z, plan.z // 2).astype(jnp.float32)
        scale = 1.0 / jnp.maximum(wave_x * wave_x + (wave_y * wave_y + wave_z * wave_z), 1.0)
        cosine = (total[:half] + first_ref[0, :half]) * scale
        sine = (total[half:] + first_ref[0, half:]) * scale
        found = jnp.concatenate([cosine, sine], axis=0)
        out_ref[:, 0] = left_times((bt_ref[...], bl_ref[...]), found).reshape(gx, x, ny)
        slope_ref[0, :half], slope_ref[0, half:] = slope_x(found)

    tables = [forth_twice, forth_low, back_twice, back_low]
    spectrum = pl.BlockSpec((1, nx, ny), lambda i: (i, 0, 0))
    block = pl.BlockSpec((gx, 1, x, ny), lambda i: (0, i, 0, 0))
    return pl.pallas_call(
        kernel,
        grid=(plan.per,),
        in_specs=[scalars()] + [whole_block(t.shape) for t in tables] + [spectrum, block],
        out_specs=[block, spectrum],
        out_shape=[
            jax.ShapeDtypeStruct(lines.shape, jnp.float32),
            jax.ShapeDtypeStruct((plan.per, nx, ny), jnp.float32),
        ],
        compiler_params=params(),
        cost_estimate=cost(2 * plan.per * ny * nx * nx, 4 * plan.per * ny * nx),
        name="potential",
    )(place, *[jnp.asarray(t) for t in tables], first, lines)


def pieces_of_y(plan, table_ref, me, values):
    groups = [lax.rem(me + s, plan.gy) for s in range(plan.gy)]
    y = plan.y
    tables = [(table_ref[0, g], table_ref[1, g]) for g in groups]
    if y % 128 == 0:
        tables = [tuple(joined([table[i] for table in tables], 1) for i in range(2))]
    tables = [(jnp.concatenate([high, high], axis=0), low) for high, low in tables]
    found = []
    for value in values:
        pieces = [right_times(value, table) for table in tables]
        if y % 128 == 0:
            pieces = [pieces[0][:, s * y : (s + 1) * y] for s in range(plan.gy)]
        found.append(pieces)
    return found


def last_y_inverse(plan, place, slope):
    y, nx, ny = plan.y, plan.nx, plan.ny
    table = halves(np.stack(np.split(inverse_basis(ny), plan.gy, axis=1)))

    def kernel(place_ref, table_ref, in_ref, *outs):
        (pieces,) = pieces_of_y(plan, table_ref, place_ref[1], [in_ref[0]])
        for out, piece in zip(outs, pieces):
            out[0] = piece

    return pl.pallas_call(
        kernel,
        grid=(plan.per,),
        in_specs=[
            scalars(),
            whole_block(table.shape),
            pl.BlockSpec((1, nx, ny), lambda i: (i, 0, 0)),
        ],
        out_specs=[pl.BlockSpec((1, nx, y), lambda i: (i, 0, 0))] * plan.gy,
        out_shape=[jax.ShapeDtypeStruct((plan.per, nx, y), jnp.float32)] * plan.gy,
        compiler_params=params(),
        cost_estimate=cost(plan.per * nx * ny * ny, 2 * plan.per * nx * ny),
        name="last_y_inverse",
    )(place, jnp.asarray(table), slope)


def last_x_inverse(plan, place, blocks):
    x, y, nx, gx = plan.x, plan.y, plan.nx, plan.gx
    twice, low = doubled(-inverse_basis(nx).T, 1)

    def kernel(place_ref, twice_ref, low_ref, *refs):
        ins, out = refs[:-1], refs[-1]
        me = place_ref[1]
        found = side_by_side((twice_ref[...], low_ref[...]), [ref[0] for ref in ins])
        for s, value in enumerate(found):
            out[:, source(me, s, plan.gy), 0] = value.reshape(gx, x, y)

    return pl.pallas_call(
        kernel,
        grid=(plan.per,),
        in_specs=[scalars(), whole_block(twice.shape), whole_block(low.shape)]
        + [pl.BlockSpec((1, nx, y), lambda i: (i, 0, 0))] * plan.gy,
        out_specs=pl.BlockSpec((gx, plan.gy, 1, x, y), lambda i: (0, 0, i, 0, 0)),
        out_shape=jax.ShapeDtypeStruct((gx, plan.gy, plan.per, x, y), jnp.float32),
        compiler_params=params(),
        cost_estimate=cost(plan.per * plan.ny * nx * nx, 2 * plan.per * plan.ny * nx),
        name="last_x_inverse",
    )(place, jnp.asarray(twice), jnp.asarray(low), *blocks)


def pair_y_inverse(plan, place, planes, behind):
    x, y, ny = plan.x, plan.y, plan.ny
    count = planes.shape[0]
    table = halves(np.stack(np.split(inverse_basis(ny), plan.gy, axis=1)))
    deep = fit(count, 8)
    rows = deep * x
    half = ny // 2

    def kernel(place_ref, table_ref, in_ref, _, *outs):
        plain = in_ref[...].reshape(rows, ny)
        wave = lax.broadcasted_iota(jnp.int32, (1, half), 1).astype(jnp.float32)
        along = jnp.concatenate([wave * plain[:, half:], -wave * plain[:, :half]], axis=1)
        found = pieces_of_y(plan, table_ref, place_ref[1], [along, plain])
        for comp, pieces in enumerate(found):
            for out, piece in zip(outs[:-1], pieces):
                out[comp] = piece.reshape(deep, x, y)

    return pl.pallas_call(
        kernel,
        grid=(count // deep,),
        in_specs=[
            scalars(),
            whole_block(table.shape),
            pl.BlockSpec((deep, x, ny), lambda i: (i, 0, 0)),
            unread(),
        ],
        out_specs=[pl.BlockSpec((2, deep, x, y), lambda i: (0, i, 0, 0))] * plan.gy + [unread()],
        out_shape=[jax.ShapeDtypeStruct((2, count, x, y), jnp.float32)] * plan.gy
        + [jax.ShapeDtypeStruct(behind.shape, behind.dtype)],
        input_output_aliases={3: plan.gy},
        compiler_params=params(),
        cost_estimate=cost(2 * count * x * ny * ny, 3 * count * x * ny),
        name="pair_y_inverse",
    )(place, jnp.asarray(table), planes, behind)


def image_part(plan, place, comps, tables, blocks, fields, before, weight):
    x, y, z = plan.x, plan.y, plan.z
    outs = len(blocks)
    rows = z // outs
    table = np.stack([halves(table) for table in tables]).reshape(len(comps), 2, outs, rows, z)
    group = fit(x, 8)
    deep = fit(group, 2)

    def kernel(place_ref, table_ref, *refs):
        refs = list(refs)
        inputs = [[refs.pop(0) for _ in comps] for _ in range(3)]
        started = [refs.pop(0) for _ in before]
        *ins, image_p, image_s = refs
        at = pl.program_id(0) * group
        order = [source(place_ref[1], s, outs) if outs > 1 else 0 for s in range(outs)]
        turned_tables = []
        for comp in range(len(comps)):
            parts = [joined([table_ref[comp, i, g] for g in order], 0) for i in range(2)]
            high, low = (part.astype(jnp.float32).T.astype(jnp.bfloat16) for part in parts)
            turned_tables.append((jnp.concatenate([high, high], axis=1), low))
        for plane in range(0, group, deep):
            here = slice(plane, plane + deep)
            total_p, total_s = (ref[here] for ref in started) if before else (0.0, 0.0)
            for comp, table in enumerate(turned_tables):
                v_ref, p_ref, s_ref = (each[comp] for each in inputs)
                columns = []
                for k in range(deep):
                    cut = pl.ds(at + plane + k, rows, stride=x)
                    columns.append(joined([ref[comp, cut, :] for ref in ins], 0))
                field = left_times(table, joined(columns, 1)).T.reshape(deep, y, z)
                total_p += p_ref[0, here].astype(jnp.float32) * field
                total_s += s_ref[0, here].astype(jnp.float32) * (v_ref[0, here] - field)
            image_p[here] = total_p
            image_s[here] = total_s

    def block(comp):
        return pl.BlockSpec((1, group, y, z), lambda i: (comp, i, 0, 0))

    blocks = [part.reshape(len(comps), rows * x, y) for part in blocks]
    image = pl.BlockSpec((group, y, z), lambda i: (i, 0, 0))
    return pl.pallas_call(
        kernel,
        grid=(x // group,),
        in_specs=[scalars(), whole_block(table.shape)]
        + [block(comp) for _ in fields for comp in comps]
        + [image] * len(before)
        + [whole_block(part.shape) for part in blocks],
        out_specs=[image, image],
        out_shape=[jax.ShapeDtypeStruct((x, y, z), jnp.float32)] * 2,
        compiler_params=params(),
        cost_estimate=cost(
            weight * len(comps) * x * y * z * z, weight * (2 + 3 * len(comps)) * x * y * z
        ),
        name="image_part",
    )(
        place,
        jnp.asarray(table),
        *[field for field in fields for _ in comps],
        *before,
        *blocks,
    )


def over_gx(blocks):
    return lax.all_to_all(blocks, "gx", 0, 0, tiled=True)


def separated(plan, place, velocity, source_p, source_s):
    x, y, z, gx, gy, per = plan.x, plan.y, plan.z, plan.gx, plan.gy, plan.per
    plain = basis(z)
    pair = along_z(plan, place, velocity, (1, 2), (plain, turned(plain)), gy)
    (first,) = along_z(plan, place, velocity, (0,), (crossed(plain, plan),), 1, pair[:1])
    first = over_gx(first.reshape(gx, gy, per, x, y))
    pair = pair_y_forward(plan, place, swap_gy(pair))
    pair = over_gx(pair.reshape(gx, per, x, plan.ny))
    first = first_y_forward(plan, place, swap_gy(first_x_forward(plan, place, first)))
    lines, slope = potential(plan, place, first, pair)
    pair = over_gx(lines)
    last = last_x_inverse(plan, place, swap_gy(last_y_inverse(plan, place, slope)))
    *pair, last = pair_y_inverse(plan, place, pair.reshape(gx * per, x, plan.ny), last)
    pair = swap_gy(pair)
    last = over_gx(last)
    back = inverse_basis(z)
    fields = (velocity, source_p, source_s)
    found = image_part(plan, place, (1, 2), (back, -turned(back)), pair, fields, (), WEIGHT)
    return image_part(plan, place, (0,), (crossed(back, plan),), [last], fields, found, 1)


def shards(velocity, stress, lame_lambda, shear_modulus, buoyancy, source_p, source_s):
    velocity = propagate(velocity, stress, lame_lambda, shear_modulus, buoyancy)
    plan = Plan(velocity.shape[1:])
    place = jnp.stack([lax.axis_index("gx"), lax.axis_index("gy")]).astype(jnp.int32)
    if plan.z % (plan.gx * plan.gy) == 0:
        return tuple(separated(plan, place, velocity, source_p, source_s))
    blocks = z_forward(plan, place, velocity)
    lines = [to_lines(plan, y_forward(plan, place, swap_gy(group))) for group in blocks]
    lines = [x_lines(plan, place, part, chunk) for chunk, part in enumerate(lines)]
    blocks = [swap_gy(y_inverse(plan, place, to_planes(plan, part))) for part in lines]
    return tuple(images(plan, place, blocks, velocity, source_p, source_s))


def solution(mesh):
    in_specs = (
        P(None, "gx", "gy", None),
        P(None, "gx", "gy", None),
        P("gx", "gy", None),
        P("gx", "gy", None),
        P("gx", "gy", None),
        P(None, "gx", "gy", None),
        P(None, "gx", "gy", None),
    )
    out_specs = (P("gx", "gy", None), P("gx", "gy", None))
    return jax.shard_map(shards, mesh=mesh, in_specs=in_specs, out_specs=out_specs, check_vma=False)
```

```python
import numpy as np
import ml_dtypes
import jax
import jax.numpy as jnp
from jax import lax
from jax.experimental import pallas as pl
from jax.experimental.pallas import tpu as pltpu
from jax.sharding import PartitionSpec as P

STEPS = 2
MOST_CHUNKS = 1
VMEM_BYTES = 63 * 2**20
STENCIL_BYTES = 22 * 2**20
Y_DEEP = 32
Z_GROUP = 16
X_GROUP = 4
Y_TILE = 32
WEIGHT = 1000

time_step = 0.2


def passed_along(block, axis, distance):
    devices = range(lax.axis_size(axis))
    route = [(i - distance, i) for i in devices if i - distance in devices]
    return lax.ppermute(block, axis, route)


def across_corner(row, x_way, y_way):
    x_count, y_count = lax.axis_size("gx"), lax.axis_size("gy")
    route = [
        ((i - x_way) * y_count + j - y_way, i * y_count + j)
        for i in range(x_count)
        for j in range(y_count)
        if 0 <= i - x_way < x_count and 0 <= j - y_way < y_count
    ]
    return lax.ppermute(row, ("gx", "gy"), route)


def exchange(x_last, x_first, y_last, y_first, corner_y, corner_x):
    yl, yr = passed_along(y_last, "gy", 1), passed_along(y_first, "gy", -1)
    xl, xr = passed_along(x_last, "gx", 1), passed_along(x_first, "gx", -1)
    return (yl, yr), (xl, xr, across_corner(corner_y, -1, 1), across_corner(corner_x, 1, -1))


def first_rims(brick, velocity, stress, lame, shear):
    x, y, z = brick
    some = fit(y, 8)
    many = fit(y, 16)

    def kernel(*refs):
        (v_first, v_last, s_first, s_last, lame_first, shear_first, shear_last) = refs[:7]
        (v_low, v_high, s_low, s_high, lame_low, shear_low, shear_high) = refs[7:14]
        x_last, x_first, y_last, y_first, corner_y, corner_x = refs[14:]

        def wide(value):
            return value.astype(jnp.float32)

        for i in range(3):
            x_last[i], x_first[i] = v_last[i, 0], v_first[i, 0]
            y_last[i], y_first[i] = v_high[i, :, some - 1], v_low[i, :, 0]
        x_last[3], x_last[4], x_last[5] = s_last[3, 0], s_last[4, 0], wide(shear_last[0])
        x_first[3], x_first[4], x_first[5] = s_first[0, 0], wide(lame_first[0]), wide(shear_first[0])
        y_last[3], y_last[4] = s_high[3, :, some - 1], s_high[5, :, some - 1]
        y_last[5] = wide(shear_high[...])[:, many - 1]
        y_first[3], y_first[4] = s_low[1, :, 0], wide(lame_low[...])[:, 0]
        y_first[5] = wide(shear_low[...])[:, 0]
        corner_y[...] = v_first[1, 0, y - 1 :]
        corner_x[...] = v_last[0, 0, :1]

    def plane(count, at):
        return pl.BlockSpec((count, 1, y, z), lambda i: (0, at, 0, 0))

    def medium_plane(at):
        return pl.BlockSpec((1, y, z), lambda i: (at, 0, 0))

    def rows(count, at):
        return pl.BlockSpec((count, x, some, z), lambda i: (0, 0, at, 0))

    def medium_rows(at):
        return pl.BlockSpec((x, many, z), lambda i: (0, at, 0))

    shapes = [(6, y, z), (6, y, z), (6, x, z), (6, x, z), (1, z), (1, z)]
    ends, highs, most = x - 1, y // some - 1, y // many - 1
    return pl.pallas_call(
        kernel,
        grid=(1,),
        in_specs=[plane(3, 0), plane(3, ends), plane(6, 0), plane(6, ends)]
        + [medium_plane(0), medium_plane(0), medium_plane(ends)]
        + [rows(3, 0), rows(3, highs), rows(6, 0), rows(6, highs)]
        + [medium_rows(0), medium_rows(0), medium_rows(most)],
        out_specs=[whole_block(shape) for shape in shapes],
        out_shape=[jax.ShapeDtypeStruct(shape, jnp.float32) for shape in shapes],
        compiler_params=params(),
        cost_estimate=pl.CostEstimate(
            flops=0, bytes_accessed=80 * (y + 8 * x) * z, transcendentals=0
        ),
        name="first_rims",
    )(
        *(velocity, velocity, stress, stress, lame, shear, shear),
        *(velocity, velocity, stress, stress, lame, shear, shear),
    )


def stencil(brick, state, rims, medium, x_rims, x_medium, done, last):
    x, y, z = brick
    velocity, stress, lame, shear, buoyancy = state
    group = fit(x, X_GROUP)
    groups = x // group
    tall = fit(y, Y_TILE)
    ends = x_rims is not None
    if ends:
        count, of = min(groups, 2), lambda i: i * (groups - 1)
    else:
        count, of = groups - 2, lambda i: i + 1
    f32 = jnp.float32

    def kernel(*refs):
        refs = list(refs)

        def take(number):
            taken = refs[:number]
            del refs[:number]
            return taken

        v_ref, s_ref, lame_ref, shear_ref, buoy_ref = take(5)
        v_next_ref, xx_next_ref, lame_next_ref, shear_next_ref = take(4)
        v_prior_ref, xy_prior_ref, xz_prior_ref, shear_prior_ref = take(4)
        yl, yr = take(2)
        yl_medium, yr_medium = take(2) if medium else (yl, yr)
        if ends:
            xl, xr, edge_y, edge_x = take(4)
            xl_medium, xr_medium = take(2) if medium else (xl, xr)
        given = take(len(done))
        new = take(1)[0]
        if not last:
            s_out, y_last, y_first = take(3)
            if ends:
                x_last, x_first, corner_y, corner_x = take(4)
        carried, xx_after = take(2)
        s_new = take(1)[0] if last else s_out
        turn = pl.program_id(0)
        here_group = of(turn)
        at = here_group * group
        start, end = here_group == 0, here_group == groups - 1
        row = lax.broadcasted_iota(jnp.int32, (y, z), 0)
        lane = lax.broadcasted_iota(jnp.int32, (y, z), 1)

        def next_z(field):
            edge = lane[: field.shape[0]] == z - 1
            return jnp.where(edge, 0.0, pltpu.roll(field, z - 1, 1))

        def prior_z(field):
            edge = lane[: field.shape[0]] == 0
            return jnp.where(edge, 0.0, pltpu.roll(field, 1, 1))

        def next_y(field, rim):
            rows = field.shape[0]
            return jnp.where(row[:rows] == rows - 1, rim, pltpu.roll(field, rows - 1, 0))

        def prior_y(field, rim):
            return jnp.where(row[: field.shape[0]] == 0, rim, pltpu.roll(field, 1, 0))

        def wide(value):
            return value.astype(f32)

        def line(ref, which, place):
            return ref[which, pl.ds(place, 1), :]

        def line_after(place):
            if not ends:
                return line(yl, 1, place)
            return jnp.where(place == x, edge_y[...], line(yl, 1, jnp.minimum(place, x - 1)))

        def line_before(place):
            if not ends:
                return line(yr, 0, place)
            return jnp.where(place < 0, edge_x[...], line(yr, 0, jnp.maximum(place, 0)))

        def begin(value, rim):
            return jnp.where(start, rim(), value) if ends else value

        def finish(value, rim):
            return jnp.where(end, rim(), value) if ends else value

        def fresh():
            shear_rim = begin(wide(shear_prior_ref[0]), lambda: xl_medium[5])
            vx, vy, vz = (begin(v_prior_ref[i, 0], lambda: xl[i]) for i in range(3))
            xy = begin(xy_prior_ref[0, 0], lambda: xl[3])
            xz = begin(xz_prior_ref[0, 0], lambda: xl[4])
            pull = time_step * shear_rim
            carried[0] = vx
            carried[1] = xy + pull * ((next_y(vx, line_before(at - 1)) - vx) + (v_ref[1, 0] - vy))
            carried[2] = xz + pull * ((next_z(vx) - vx) + (v_ref[2, 0] - vz))

        if ends:
            fresh()
        else:
            pl.when(turn == 0)(fresh)
        if not last and done:

            @pl.when(turn == 0)
            def _():
                y_last[...] = given[2][...]
                y_first[...] = given[3][...]

        def after(i, rows):
            return finish(v_next_ref[i, 0, rows], lambda: xr[i, rows])

        spans = [slice(top, top + tall) for top in range(0, y, tall)]

        def row_before(span, field, rim):
            return rim() if span.start == 0 else field[span.start - 1 : span.start]

        def row_after(span, field, rim):
            return rim() if span.stop == y else field[span.stop : span.stop + 1]

        for k in range(group):
            here = at + k
            v_here = [v_ref.at[i, k] for i in range(3)]
            for span in spans:
                vx, vy, vz = (field[span] for field in v_here)
                vx_prior = carried[0, span] if k == 0 else v_ref[0, k - 1, span]
                vy_next = after(1, span) if k == group - 1 else v_ref[1, k + 1, span]
                vz_next = after(2, span) if k == group - 1 else v_ref[2, k + 1, span]
                vy_rim = row_before(span, v_here[1], lambda: line(yl, 1, here))
                vx_rim = row_after(span, v_here[0], lambda: line(yr, 0, here))
                vz_rim = row_after(span, v_here[2], lambda: line(yr, 2, here))
                lame_value, shear_value = wide(lame_ref[k, span]), wide(shear_ref[k, span])
                ex = vx - vx_prior
                ey = vy - prior_y(vy, vy_rim)
                ez = vz - prior_z(vz)
                swell = lame_value * (ex + ey + ez)
                double = 2.0 * shear_value
                pull = time_step * shear_value
                found = (
                    s_ref[0, k, span] + time_step * (swell + double * ex),
                    s_ref[1, k, span] + time_step * (swell + double * ey),
                    s_ref[2, k, span] + time_step * (swell + double * ez),
                    s_ref[3, k, span] + pull * ((next_y(vx, vx_rim) - vx) + (vy_next - vy)),
                    s_ref[4, k, span] + pull * ((next_z(vx) - vx) + (vz_next - vz)),
                    s_ref[5, k, span] + pull * ((next_z(vy) - vy) + (next_y(vz, vz_rim) - vz)),
                )
                for i, value in enumerate(found):
                    s_new[i, k, span] = value

        for span in spans:
            vx, vy, vz = (after(i, span) for i in range(3))
            vy_rim = (
                line_after(at + group)
                if span.start == 0
                else after(1, slice(span.start - 1, span.start))
            )
            ex = vx - v_ref[0, group - 1, span]
            ey = vy - prior_y(vy, vy_rim)
            ez = vz - prior_z(vz)
            lame_value = finish(wide(lame_next_ref[0, span]), lambda: xr_medium[4, span])
            shear_value = finish(wide(shear_next_ref[0, span]), lambda: xr_medium[5, span])
            xx_after[span] = finish(xx_next_ref[0, 0, span], lambda: xr[3, span]) + time_step * (
                lame_value * (ex + ey + ez) + 2.0 * shear_value * ex
            )

        for k in range(group):
            here = at + k
            v_here = [v_ref.at[i, k] for i in range(3)]
            vx_edge, vy_edge, vz_edge = v_here[0][:1], v_here[1][y - 1 :], v_here[2][:1]
            pull = time_step * line(yl_medium, 5, here)
            vy_rim, vz_rim = line(yl, 1, here), line(yl, 2, here)
            xy_rim = line(yl, 3, here) + pull * (
                (vx_edge - line(yl, 0, here)) + (line_after(here + 1) - vy_rim)
            )
            yz_rim = line(yl, 4, here) + pull * ((next_z(vy_rim) - vy_rim) + (vz_edge - vz_rim))
            vx_rim, vz_rim = line(yr, 0, here), line(yr, 2, here)
            ex = vx_rim - line_before(here - 1)
            ey = line(yr, 1, here) - vy_edge
            ez = vz_rim - prior_z(vz_rim)
            yy_rim = line(yr, 3, here) + time_step * (
                line(yr_medium, 4, here) * (ex + ey + ez) + 2.0 * line(yr_medium, 5, here) * ey
            )
            s_here = [s_new.at[i, k] for i in range(6)]
            for span in spans:
                xx, yy, zz, xy, xz, yz = (field[span] for field in s_here)
                xx_next = xx_after[span] if k == group - 1 else s_new[0, k + 1, span]
                xy_prior = carried[1, span] if k == 0 else s_new[3, k - 1, span]
                xz_prior = carried[2, span] if k == 0 else s_new[4, k - 1, span]
                xy_before = row_before(span, s_here[3], lambda: xy_rim)
                yz_before = row_before(span, s_here[5], lambda: yz_rim)
                yy_after = row_after(span, s_here[1], lambda: yy_rim)
                push = time_step * wide(buoy_ref[k, span])
                new[0, k, span] = v_ref[0, k, span] + push * (
                    (xx_next - xx) + (xy - prior_y(xy, xy_before)) + (xz - prior_z(xz))
                )
                new[1, k, span] = v_ref[1, k, span] + push * (
                    (xy - xy_prior) + (next_y(yy, yy_after) - yy) + (yz - prior_z(yz))
                )
                new[2, k, span] = v_ref[2, k, span] + push * (
                    (xz - xz_prior) + (yz - prior_y(yz, yz_before)) + (next_z(zz) - zz)
                )
            if last:
                continue
            for i in range(3):
                y_last[i, pl.ds(here, 1), :] = new[i, k, y - 1 :]
                y_first[i, pl.ds(here, 1), :] = new[i, k, :1]
            y_last[3, pl.ds(here, 1), :] = s_new[3, k, y - 1 :]
            y_last[4, pl.ds(here, 1), :] = s_new[5, k, y - 1 :]
            y_first[3, pl.ds(here, 1), :] = s_new[1, k, :1]

        if ends and not last:

            @pl.when(start)
            def _():
                for i in range(3):
                    x_first[i] = new[i, 0]
                x_first[3] = s_new[0, 0]
                corner_y[...] = new[1, 0, y - 1 :]

            @pl.when(end)
            def _():
                for i in range(3):
                    x_last[i] = new[i, group - 1]
                x_last[3], x_last[4] = s_new[3, group - 1], s_new[4, group - 1]
                corner_x[...] = new[0, group - 1, :1]

        if not ends:
            carried[0] = v_ref[0, group - 1]
            carried[1] = s_new[3, group - 1]
            carried[2] = s_new[4, group - 1]

    def next_plane(i):
        return jnp.minimum((of(i) + 1) * group, x - 1)

    def prior_plane(i):
        return jnp.maximum(of(i) * group - 1, 0) if ends else group - 1

    def planes(number):
        return pl.BlockSpec((number, group, y, z), lambda i: (0, of(i), 0, 0))

    def one(number, which, place):
        return pl.BlockSpec((number, 1, y, z), lambda i: (which, place(i), 0, 0))

    def medium_one(place):
        return pl.BlockSpec((1, y, z), lambda i: (place(i), 0, 0))

    medium_block = pl.BlockSpec((group, y, z), lambda i: (of(i), 0, 0))
    args = [velocity, stress, lame, shear, buoyancy, velocity, stress, lame, shear]
    args += [velocity, stress, stress, shear, *rims, *medium]
    in_specs = [planes(3), planes(6), medium_block, medium_block, medium_block]
    in_specs += [one(3, 0, next_plane), one(1, 0, next_plane)]
    in_specs += [medium_one(next_plane), medium_one(next_plane)]
    in_specs += [one(3, 0, prior_plane), one(1, 3, prior_plane), one(1, 4, prior_plane)]
    in_specs += [medium_one(prior_plane)]
    in_specs += [whole_block(rim.shape) for rim in (*rims, *medium)]
    if ends:
        args += [*x_rims, *x_medium]
        in_specs += [whole_block(rim.shape) for rim in (*x_rims, *x_medium)]
    aliases = {}
    for i, value in enumerate(done):
        if i < 2:
            aliases[len(args)] = i
        in_specs.append(unread() if i < 2 else whole_block(value.shape))
        args.append(value)
    out_shape = [(3, x, y, z)]
    out_specs = [planes(3)]
    if not last:
        out_shape += [(6, x, y, z), (5, x, z), (4, x, z)]
        out_specs += [planes(6)]
        if ends:
            out_shape += [(5, y, z), (4, y, z), (1, z), (1, z)]
        out_specs += [whole_block(shape) for shape in out_shape[2:]]
    part = (1 if ends else WEIGHT) * count * group * y * z
    return pl.pallas_call(
        kernel,
        grid=(count,),
        in_specs=in_specs,
        out_specs=out_specs,
        out_shape=[jax.ShapeDtypeStruct(shape, f32) for shape in out_shape],
        scratch_shapes=[pltpu.VMEM((3, y, z), f32), pltpu.VMEM((y, z), f32)]
        + ([pltpu.VMEM((6, group, y, z), f32)] if last else []),
        input_output_aliases=aliases,
        compiler_params=params(STENCIL_BYTES),
        cost_estimate=pl.CostEstimate(
            flops=80 * part, bytes_accessed=(54 if last else 78) * part, transcendentals=0
        ),
        name="stencil_ends" if ends else "stencil_middle",
    )(*args)


def propagate(velocity, stress, lame, shear, buoyancy):
    brick = velocity.shape[1:]
    between = brick[0] // fit(brick[0], X_GROUP) > 2
    rims, x_rims = exchange(*first_rims(brick, velocity, stress, lame, shear))
    held, medium, x_medium = (rims, x_rims[:2]), (), ()
    for step_index in range(STEPS):
        last = step_index == STEPS - 1
        state = (velocity, stress, lame, shear, buoyancy)
        done = []
        if between:
            done = stencil(brick, state, rims, medium, None, None, done, last)
        found = stencil(brick, state, rims, medium, x_rims, x_medium, done, last)
        velocity = found[0]
        if not last:
            stress, y_last, y_first, x_last, x_first, corner_y, corner_x = found[1:]
            rims, x_rims = exchange(x_last, x_first, y_last, y_first, corner_y, corner_x)
            medium, x_medium = held
    return velocity


def basis(length):
    half = length // 2
    wave = np.arange(half)
    place = np.arange(length)
    angle = (wave[:, None] * place[None, :] % length) * (2.0 * np.pi / length)
    cosine, sine = np.cos(angle), np.sin(angle)
    sine[0] = 1.0 - 2.0 * (place % 2)
    return np.concatenate([cosine, sine])


def waves_of(length):
    return np.tile(np.arange(length // 2, dtype=np.float64), 2)


def inverse_basis(length):
    weight = np.where(waves_of(length) == 0, 1.0, 2.0) / length
    return basis(length) * weight[:, None]


def turned(table):
    half = table.shape[0] // 2
    return np.concatenate([table[half:], -table[:half]]) * waves_of(table.shape[0])[:, None]


def halves(table):
    high = table.astype(ml_dtypes.bfloat16)
    low = (table - high.astype(np.float64)).astype(ml_dtypes.bfloat16)
    return np.stack([high, low])


def split(value):
    high = value.astype(jnp.bfloat16)
    return high, (value - high.astype(jnp.float32)).astype(jnp.bfloat16)


def dot(left, right, dims=((1,), (0,))):
    return lax.dot_general(left, right, (dims, ((), ())), preferred_element_type=jnp.float32)


def times(left, right):
    return dot(left[0], right[0]) + (dot(left[1], right[0]) + dot(left[0], right[1]))


def joined(pieces, axis):
    return pieces[0] if len(pieces) == 1 else jnp.concatenate(pieces, axis=axis)


def fit(length, most):
    size = min(length, most)
    while length % size:
        size -= 1
    return size


def params(limit=VMEM_BYTES):
    return pltpu.CompilerParams(vmem_limit_bytes=limit)


def whole_block(shape):
    return pl.BlockSpec(shape, lambda *_: (0,) * len(shape))


def scalars():
    return pl.BlockSpec(memory_space=pltpu.SMEM)


class Plan:
    def __init__(self, brick):
        self.x, self.y, self.z = brick
        self.gx, self.gy = lax.axis_size("gx"), lax.axis_size("gy")
        self.nx, self.ny = self.x * self.gx, self.y * self.gy
        chunks = MOST_CHUNKS
        while chunks > 1 and self.z % (chunks * self.gy * self.gx):
            chunks -= 1
        self.chunks = chunks
        self.kz = self.z // (chunks * self.gy)
        self.parts = max(1, self.gx // self.kz)
        self.per = max(1, self.kz // self.gx)
        self.ky = self.ny // self.parts


def source(me, step, count):
    return lax.rem(me - step + count, count)


def z_forward(plan, place, velocity):
    x, y, z, kz = plan.x, plan.y, plan.z, plan.kz
    table = np.stack([halves(basis(z)), halves(turned(basis(z)))])
    table = table.reshape(2, 2, plan.chunks, plan.gy, kz, z)
    count = plan.chunks * plan.gy

    group = fit(x, Z_GROUP)
    deep = fit(group, 2)

    def kernel(place_ref, table_ref, v_ref, *outs):
        at = pl.program_id(0) * group
        me = place_ref[1]
        order = [(c, lax.rem(me + s, plan.gy)) for c in range(plan.chunks) for s in range(plan.gy)]
        tables = []
        for kind in range(2):
            high, low = (joined([table_ref[kind, i, c, g] for c, g in order], 0) for i in range(2))
            tables.append((jnp.concatenate([high, high], axis=1), low))
        for comp in range(3):
            twice, low = tables[1 if comp == 2 else 0]
            for plane in range(0, group, deep):
                field = split(v_ref[comp, plane : plane + deep].reshape(deep * y, z))
                value = dot(twice, jnp.concatenate(field, axis=1), ((1,), (1,)))
                value += dot(low, field[0], ((1,), (1,)))
                for i, out in enumerate(outs):
                    for k in range(deep):
                        part = value[i * kz : (i + 1) * kz, k * y : (k + 1) * y]
                        out[comp, pl.ds(at + plane + k, kz, stride=x), :] = part

    outs = pl.pallas_call(
        kernel,
        grid=(x // group,),
        in_specs=[
            scalars(),
            whole_block(table.shape),
            pl.BlockSpec((3, group, y, z), lambda i: (0, i, 0, 0)),
        ],
        out_specs=[whole_block((3, kz * x, y))] * count,
        out_shape=[jax.ShapeDtypeStruct((3, kz * x, y), jnp.float32)] * count,
        compiler_params=params(),
        cost_estimate=pl.CostEstimate(
            flops=18 * x * y * z * z, bytes_accessed=24 * x * y * z, transcendentals=0
        ),
        name="z_forward",
    )(place, jnp.asarray(table), velocity)
    outs = [out.reshape(3, kz, x, y) for out in outs]
    return [outs[c * plan.gy : (c + 1) * plan.gy] for c in range(plan.chunks)]


def swap_gy(blocks):
    count = len(blocks)
    moved = [blocks[0]]
    for step in range(1, count):
        route = [(i, (i + step) % count) for i in range(count)]
        moved.append(lax.ppermute(blocks[step], "gy", route))
    return moved


def y_forward(plan, place, blocks):
    x, y, ny, kz = plan.x, plan.y, plan.ny, plan.kz
    table = halves(basis(ny).T).reshape(2, plan.gy, y, ny)
    deep = fit(kz, 8)
    rows = deep * x
    half = ny // 2
    aligned = y % 128 == 0

    def kernel(place_ref, table_ref, *refs):
        ins, out = refs[:-1], refs[-1]
        me = place_ref[1]
        groups = [source(me, step, plan.gy) for step in range(plan.gy)]
        tables = [(table_ref[0, g], table_ref[1, g]) for g in groups]
        if aligned:
            tables = [tuple(joined([t[i] for t in tables], 0) for i in range(2))]

        def moved(comp):
            fields = [ref[comp].reshape(rows, y) for ref in ins]
            if aligned:
                fields = [joined(fields, 1)]
            return sum(times(split(f), t) for f, t in zip(fields, tables))

        wave = lax.broadcasted_iota(jnp.int32, (1, half), 1).astype(jnp.float32)
        out[:, 0] = moved(0).reshape(deep, x, ny)
        along, rest = moved(1), moved(2)
        out[:, 1, :, :half] = (rest[:, :half] + wave * along[:, half:]).reshape(deep, x, half)
        out[:, 1, :, half:] = (rest[:, half:] - wave * along[:, :half]).reshape(deep, x, half)

    return pl.pallas_call(
        kernel,
        grid=(kz // deep,),
        in_specs=[scalars(), whole_block(table.shape)]
        + [pl.BlockSpec((3, deep, x, y), lambda i: (0, i, 0, 0))] * plan.gy,
        out_specs=pl.BlockSpec((deep, 2, x, ny), lambda i: (i, 0, 0, 0)),
        out_shape=jax.ShapeDtypeStruct((kz, 2, x, ny), jnp.float32),
        compiler_params=params(),
        cost_estimate=pl.CostEstimate(
            flops=18 * kz * x * ny * ny, bytes_accessed=20 * kz * x * ny, transcendentals=0
        ),
        name="y_forward",
    )(place, jnp.asarray(table), *blocks)


def to_lines(plan, planes):
    if plan.parts > 1:
        planes = planes.reshape(plan.kz, 2, plan.x, plan.parts, plan.ky).transpose(0, 3, 1, 2, 4)
    planes = planes.reshape(plan.gx, plan.per, 2, plan.x, plan.ky)
    return lax.all_to_all(planes, "gx", 0, 0, tiled=True)


def to_planes(plan, lines):
    planes = lax.all_to_all(lines, "gx", 0, 0, tiled=True)
    if plan.parts > 1:
        planes = planes.reshape(plan.kz, plan.parts, 2, plan.x, plan.ky).transpose(0, 2, 3, 1, 4)
    return planes.reshape(plan.kz, 2, plan.x, plan.ny)


def x_lines(plan, place, lines, chunk):
    x, nx, ny, ky, gx = plan.x, plan.nx, plan.ny, plan.ky, plan.gx
    forth = halves(basis(nx))
    back = halves(-inverse_basis(nx).T)
    lanes = 128 if ky % 128 == 0 else ky
    half = nx // 2
    aligned = lanes % 128 == 0

    def kernel(place_ref, forth_ref, back_ref, in_ref, out_ref):
        me_x, me_y = place_ref[0], place_ref[1]
        which, lane = pl.program_id(0), pl.program_id(1)

        def through(table_ref, pair):
            table = (table_ref[0], table_ref[1])
            if aligned:
                both = times(table, split(jnp.concatenate(pair, axis=1)))
                return both[:, :lanes], both[:, lanes:]
            return tuple(times(table, split(value)) for value in pair)

        pair = [in_ref[:, 0, i].reshape(nx, lanes) for i in range(2)]
        along, rest = through(forth_ref, pair)
        wave_x = lax.broadcasted_iota(jnp.int32, (half, lanes), 0).astype(jnp.float32)
        slot_y = lax.broadcasted_iota(jnp.int32, (1, lanes), 1) + (
            lane * lanes + lax.rem(me_x, plan.parts) * ky
        )
        wave_y = lax.rem(slot_y, ny // 2).astype(jnp.float32)
        slot_z = (chunk * plan.gy + me_y) * plan.kz + me_x // plan.parts * plan.per + which
        wave_z = lax.rem(slot_z, plan.z // 2).astype(jnp.float32)
        scale = 1.0 / jnp.maximum(wave_x * wave_x + (wave_y * wave_y + wave_z * wave_z), 1.0)
        cosine = (rest[:half] + wave_x * along[half:]) * scale
        sine = (rest[half:] - wave_x * along[:half]) * scale
        plain = jnp.concatenate([cosine, sine], axis=0)
        slope = jnp.concatenate([wave_x * sine, -wave_x * cosine], axis=0)
        for i, value in enumerate(through(back_ref, [slope, plain])):
            out_ref[:, 0, i] = value.reshape(gx, x, lanes)

    block = pl.BlockSpec((gx, 1, 2, x, lanes), lambda i, j: (0, i, 0, 0, j))
    return pl.pallas_call(
        kernel,
        grid=(plan.per, ky // lanes),
        in_specs=[scalars(), whole_block(forth.shape), whole_block(back.shape), block],
        out_specs=block,
        out_shape=jax.ShapeDtypeStruct(lines.shape, jnp.float32),
        compiler_params=params(),
        cost_estimate=pl.CostEstimate(
            flops=24 * plan.per * ky * nx * nx,
            bytes_accessed=16 * plan.per * ky * nx,
            transcendentals=0,
        ),
        name="x_lines",
    )(place, jnp.asarray(forth), jnp.asarray(back), lines)


def y_inverse(plan, place, planes):
    x, y, ny, kz = plan.x, plan.y, plan.ny, plan.kz
    table = np.stack(np.split(inverse_basis(ny), plan.gy, axis=1))
    table = halves(table)
    deep = fit(kz, 8)
    rows = deep * x
    half = ny // 2
    aligned = y % 128 == 0

    def kernel(place_ref, table_ref, in_ref, *outs):
        me = place_ref[1]
        groups = [lax.rem(me + step, plan.gy) for step in range(plan.gy)]
        tables = [(table_ref[0, g], table_ref[1, g]) for g in groups]
        slope = in_ref[:, 0].reshape(rows, ny)
        plain = in_ref[:, 1].reshape(rows, ny)
        wave = lax.broadcasted_iota(jnp.int32, (1, half), 1).astype(jnp.float32)
        along = jnp.concatenate([wave * plain[:, half:], -wave * plain[:, :half]], axis=1)
        for comp, value in enumerate((slope, along, plain)):
            parts = split(value)
            if aligned:
                table = tuple(joined([t[i] for t in tables], 1) for i in range(2))
                found = times(parts, table)
                pieces = [found[:, s * y : (s + 1) * y] for s in range(plan.gy)]
            else:
                pieces = [times(parts, t) for t in tables]
            for out, piece in zip(outs, pieces):
                out[comp] = piece.reshape(deep, x, y)

    return pl.pallas_call(
        kernel,
        grid=(kz // deep,),
        in_specs=[
            scalars(),
            whole_block(table.shape),
            pl.BlockSpec((deep, 2, x, ny), lambda i: (i, 0, 0, 0)),
        ],
        out_specs=[pl.BlockSpec((3, deep, x, y), lambda i: (0, i, 0, 0))] * plan.gy,
        out_shape=[jax.ShapeDtypeStruct((3, kz, x, y), jnp.float32)] * plan.gy,
        compiler_params=params(),
        cost_estimate=pl.CostEstimate(
            flops=18 * kz * x * ny * ny, bytes_accessed=20 * kz * x * ny, transcendentals=0
        ),
        name="y_inverse",
    )(place, jnp.asarray(table), planes)


def images(plan, place, blocks, velocity, source_p, source_s):
    x, y, z, kz = plan.x, plan.y, plan.z, plan.kz
    table = np.stack([halves(inverse_basis(z)), halves(-turned(inverse_basis(z)))])
    table = table.reshape(2, 2, plan.chunks, plan.gy, kz, z)
    blocks = [block.reshape(3, kz * x, y) for group in blocks for block in group]

    group = fit(x, Z_GROUP)
    deep = fit(group, 2)

    def kernel(place_ref, table_ref, v_ref, p_ref, s_ref, *refs):
        ins, (image_p, image_s) = refs[:-2], refs[-2:]
        at = pl.program_id(0) * group
        me = place_ref[1]
        order = [
            (chunk, source(me, step, plan.gy))
            for chunk in range(plan.chunks)
            for step in range(plan.gy)
        ]
        tables = []
        for kind in range(2):
            high, low = (joined([table_ref[kind, i, c, g] for c, g in order], 0) for i in range(2))
            high, low = (part.astype(jnp.float32).T.astype(jnp.bfloat16) for part in (high, low))
            tables.append((jnp.concatenate([high, high], axis=1), low))
        for plane in range(0, group, deep):
            here = slice(plane, plane + deep)
            total_p = total_s = 0.0
            for comp in range(3):
                twice, low = tables[1 if comp == 2 else 0]
                columns = [
                    joined([ref[comp, pl.ds(at + plane + k, kz, stride=x), :] for ref in ins], 0)
                    for k in range(deep)
                ]
                high, rest = split(joined(columns, 1))
                field = dot(twice, jnp.concatenate([high, rest], axis=0)) + dot(low, high)
                field = field.T.reshape(deep, y, z)
                total_p += p_ref[comp, here].astype(jnp.float32) * field
                total_s += s_ref[comp, here].astype(jnp.float32) * (v_ref[comp, here] - field)
            image_p[here] = total_p
            image_s[here] = total_s

    plane = pl.BlockSpec((3, group, y, z), lambda i: (0, i, 0, 0))
    image = pl.BlockSpec((group, y, z), lambda i: (i, 0, 0))
    return pl.pallas_call(
        kernel,
        grid=(x // group,),
        in_specs=[scalars(), whole_block(table.shape), plane, plane, plane]
        + [whole_block((3, kz * x, y))] * len(blocks),
        out_specs=[image, image],
        out_shape=[jax.ShapeDtypeStruct((x, y, z), jnp.float32)] * 2,
        compiler_params=params(),
        cost_estimate=pl.CostEstimate(
            flops=18 * x * y * z * z, bytes_accessed=44 * x * y * z, transcendentals=0
        ),
        name="images",
    )(place, jnp.asarray(table), velocity, source_p, source_s, *blocks)


def doubled(table, axis):
    high, low = halves(table)
    return np.concatenate([high, high], axis=axis), low


def left_times(table, value):
    high, low = split(value)
    return dot(table[0], jnp.concatenate([high, low], axis=0)) + dot(table[1], high)


def right_times(value, table):
    high, low = split(value)
    return dot(jnp.concatenate([high, low], axis=1), table[0]) + dot(high, table[1])


def side_by_side(table, values):
    width = values[0].shape[1]
    if width % 128:
        return [left_times(table, value) for value in values]
    both = left_times(table, joined(values, 1))
    return [both[:, i * width : (i + 1) * width] for i in range(len(values))]


def cost(flops, values):
    return pl.CostEstimate(flops=6 * flops, bytes_accessed=4 * values, transcendentals=0)


def crossed(table, plan):
    shape = (plan.gy, plan.gx, plan.per, table.shape[-1])
    return table.reshape(shape).transpose(1, 0, 2, 3).reshape(table.shape)


def unread():
    return pl.BlockSpec(memory_space=pl.ANY)


def along_z(plan, place, velocity, comps, tables, outs, ahead=()):
    x, y, z = plan.x, plan.y, plan.z
    table = np.stack([halves(table) for table in tables]).reshape(len(comps), 2, outs, z // outs, z)
    group = fit(x, Z_GROUP)
    deep = fit(group, 2)
    rows = z // outs

    def kernel(place_ref, table_ref, *refs):
        fields, found = refs[: len(comps)], refs[len(comps) + len(ahead) :]
        at = pl.program_id(0) * group
        me = place_ref[1]
        order = [lax.rem(me + s, outs) if outs > 1 else 0 for s in range(outs)]
        for comp, field in enumerate(fields):
            high, low = (joined([table_ref[comp, i, g] for g in order], 0) for i in range(2))
            twice = jnp.concatenate([high, high], axis=1)
            for plane in range(0, group, deep):
                parts = split(field[0, plane : plane + deep].reshape(deep * y, z))
                value = dot(twice, jnp.concatenate(parts, axis=1), ((1,), (1,)))
                value += dot(low, parts[0], ((1,), (1,)))
                for i, out in enumerate(found):
                    for k in range(deep):
                        part = value[i * rows : (i + 1) * rows, k * y : (k + 1) * y]
                        out[comp, pl.ds(at + plane + k, rows, stride=x), :] = part

    def block(comp):
        return pl.BlockSpec((1, group, y, z), lambda i: (comp, i, 0, 0))

    shape = (len(comps), rows * x, y)
    found = pl.pallas_call(
        kernel,
        grid=(x // group,),
        in_specs=[scalars(), whole_block(table.shape)]
        + [block(comp) for comp in comps]
        + [unread()] * len(ahead),
        out_specs=[whole_block(shape)] * outs,
        out_shape=[jax.ShapeDtypeStruct(shape, jnp.float32)] * outs,
        compiler_params=params(STENCIL_BYTES),
        cost_estimate=cost(len(comps) * x * y * z * z, 2 * len(comps) * x * y * z),
        name="along_z",
    )(place, jnp.asarray(table), *[velocity] * len(comps), *ahead)
    return [out.reshape(len(comps), rows, x, y) for out in found]


def y_table(plan, table_ref, groups):
    tables = [(table_ref[0, g], table_ref[1, g]) for g in groups]
    if plan.y % 128 == 0:
        high, low = (joined([table[i] for table in tables], 0) for i in range(2))
        return [(jnp.concatenate([high, high], axis=0), low)]
    return [(jnp.concatenate([high, high], axis=0), low) for high, low in tables]


def over_y(fields, tables):
    if len(tables) == 1:
        fields = [joined(fields, 1)]
    return sum(right_times(field, table) for field, table in zip(fields, tables))


def pair_y_forward(plan, place, blocks):
    x, y, ny = plan.x, plan.y, plan.ny
    count = blocks[0].shape[1]
    table = halves(basis(ny).T).reshape(2, plan.gy, y, ny)
    deep = fit(count, Y_DEEP)
    rows = deep * x
    half = ny // 2

    def kernel(place_ref, table_ref, *refs):
        ins, out = refs[:-1], refs[-1]
        me = place_ref[1]
        tables = y_table(plan, table_ref, [source(me, s, plan.gy) for s in range(plan.gy)])
        along, rest = (
            over_y([ref[comp].reshape(rows, y) for ref in ins], tables) for comp in range(2)
        )
        wave = lax.broadcasted_iota(jnp.int32, (1, half), 1).astype(jnp.float32)
        out[:, :, :half] = (rest[:, :half] + wave * along[:, half:]).reshape(deep, x, half)
        out[:, :, half:] = (rest[:, half:] - wave * along[:, :half]).reshape(deep, x, half)

    return pl.pallas_call(
        kernel,
        grid=(count // deep,),
        in_specs=[scalars(), whole_block(table.shape)]
        + [pl.BlockSpec((2, deep, x, y), lambda i: (0, i, 0, 0))] * plan.gy,
        out_specs=pl.BlockSpec((deep, x, ny), lambda i: (i, 0, 0)),
        out_shape=jax.ShapeDtypeStruct((count, x, ny), jnp.float32),
        compiler_params=params(),
        cost_estimate=cost(2 * WEIGHT * count * x * ny * ny, 3 * WEIGHT * count * x * ny),
        name="pair_y_forward",
    )(place, jnp.asarray(table), *blocks)


def first_x_forward(plan, place, lines):
    x, y, nx = plan.x, plan.y, plan.nx
    twice, low = doubled(basis(nx), 1)

    def kernel(place_ref, twice_ref, low_ref, in_ref, *outs):
        me = place_ref[1]
        fields = [in_ref[:, lax.rem(me + s, plan.gy), 0].reshape(nx, y) for s in range(plan.gy)]
        found = side_by_side((twice_ref[...], low_ref[...]), fields)
        for out, value in zip(outs, found):
            out[0] = value

    return pl.pallas_call(
        kernel,
        grid=(plan.per,),
        in_specs=[
            scalars(),
            whole_block(twice.shape),
            whole_block(low.shape),
            pl.BlockSpec((plan.gx, plan.gy, 1, x, y), lambda i: (0, 0, i, 0, 0)),
        ],
        out_specs=[pl.BlockSpec((1, nx, y), lambda i: (i, 0, 0))] * plan.gy,
        out_shape=[jax.ShapeDtypeStruct((plan.per, nx, y), jnp.float32)] * plan.gy,
        compiler_params=params(),
        cost_estimate=cost(plan.per * plan.ny * nx * nx, 2 * plan.per * plan.ny * nx),
        name="first_x_forward",
    )(place, jnp.asarray(twice), jnp.asarray(low), lines)


def slope_x(value):
    half = value.shape[0] // 2
    wave = lax.broadcasted_iota(jnp.int32, (half, 1), 0).astype(jnp.float32)
    return wave * value[half:], -wave * value[:half]


def first_y_forward(plan, place, blocks):
    y, nx, ny = plan.y, plan.nx, plan.ny
    table = halves(basis(ny).T).reshape(2, plan.gy, y, ny)
    half = nx // 2

    def kernel(place_ref, table_ref, *refs):
        ins, out = refs[:-1], refs[-1]
        me = place_ref[1]
        tables = y_table(plan, table_ref, [source(me, s, plan.gy) for s in range(plan.gy)])
        cosine, sine = slope_x(over_y([ref[0] for ref in ins], tables))
        out[0, :half] = cosine
        out[0, half:] = sine

    return pl.pallas_call(
        kernel,
        grid=(plan.per,),
        in_specs=[scalars(), whole_block(table.shape)]
        + [pl.BlockSpec((1, nx, y), lambda i: (i, 0, 0))] * plan.gy,
        out_specs=pl.BlockSpec((1, nx, ny), lambda i: (i, 0, 0)),
        out_shape=jax.ShapeDtypeStruct((plan.per, nx, ny), jnp.float32),
        compiler_params=params(),
        cost_estimate=cost(plan.per * nx * ny * ny, 2 * plan.per * nx * ny),
        name="first_y_forward",
    )(place, jnp.asarray(table), *blocks)


def potential(plan, place, first, lines):
    x, nx, ny, gx = plan.x, plan.nx, plan.ny, plan.gx
    forth_twice, forth_low = doubled(basis(nx), 1)
    back_twice, back_low = doubled(-inverse_basis(nx).T, 1)
    half = nx // 2

    def kernel(place_ref, ft_ref, fl_ref, bt_ref, bl_ref, first_ref, in_ref, out_ref, slope_ref):
        me_x, me_y = place_ref[0], place_ref[1]
        total = left_times((ft_ref[...], fl_ref[...]), in_ref[:, 0].reshape(nx, ny))
        wave_x = lax.broadcasted_iota(jnp.int32, (half, 1), 0).astype(jnp.float32)
        slot_y = lax.broadcasted_iota(jnp.int32, (1, ny), 1)
        wave_y = lax.rem(slot_y, ny // 2).astype(jnp.float32)
        slot_z = (me_y * gx + me_x) * plan.per + pl.program_id(0)
        wave_z = lax.rem(slot_z, plan.z // 2).astype(jnp.float32)
        scale = 1.0 / jnp.maximum(wave_x * wave_x + (wave_y * wave_y + wave_z * wave_z), 1.0)
        cosine = (total[:half] + first_ref[0, :half]) * scale
        sine = (total[half:] + first_ref[0, half:]) * scale
        found = jnp.concatenate([cosine, sine], axis=0)
        out_ref[:, 0] = left_times((bt_ref[...], bl_ref[...]), found).reshape(gx, x, ny)
        slope_ref[0, :half], slope_ref[0, half:] = slope_x(found)

    tables = [forth_twice, forth_low, back_twice, back_low]
    spectrum = pl.BlockSpec((1, nx, ny), lambda i: (i, 0, 0))
    block = pl.BlockSpec((gx, 1, x, ny), lambda i: (0, i, 0, 0))
    return pl.pallas_call(
        kernel,
        grid=(plan.per,),
        in_specs=[scalars()] + [whole_block(t.shape) for t in tables] + [spectrum, block],
        out_specs=[block, spectrum],
        out_shape=[
            jax.ShapeDtypeStruct(lines.shape, jnp.float32),
            jax.ShapeDtypeStruct((plan.per, nx, ny), jnp.float32),
        ],
        compiler_params=params(),
        cost_estimate=cost(2 * plan.per * ny * nx * nx, 4 * plan.per * ny * nx),
        name="potential",
    )(place, *[jnp.asarray(t) for t in tables], first, lines)


def pieces_of_y(plan, table_ref, me, values):
    groups = [lax.rem(me + s, plan.gy) for s in range(plan.gy)]
    y = plan.y
    tables = [(table_ref[0, g], table_ref[1, g]) for g in groups]
    if y % 128 == 0:
        tables = [tuple(joined([table[i] for table in tables], 1) for i in range(2))]
    tables = [(jnp.concatenate([high, high], axis=0), low) for high, low in tables]
    found = []
    for value in values:
        pieces = [right_times(value, table) for table in tables]
        if y % 128 == 0:
            pieces = [pieces[0][:, s * y : (s + 1) * y] for s in range(plan.gy)]
        found.append(pieces)
    return found


def last_y_inverse(plan, place, slope):
    y, nx, ny = plan.y, plan.nx, plan.ny
    table = halves(np.stack(np.split(inverse_basis(ny), plan.gy, axis=1)))

    def kernel(place_ref, table_ref, in_ref, *outs):
        (pieces,) = pieces_of_y(plan, table_ref, place_ref[1], [in_ref[0]])
        for out, piece in zip(outs, pieces):
            out[0] = piece

    return pl.pallas_call(
        kernel,
        grid=(plan.per,),
        in_specs=[
            scalars(),
            whole_block(table.shape),
            pl.BlockSpec((1, nx, ny), lambda i: (i, 0, 0)),
        ],
        out_specs=[pl.BlockSpec((1, nx, y), lambda i: (i, 0, 0))] * plan.gy,
        out_shape=[jax.ShapeDtypeStruct((plan.per, nx, y), jnp.float32)] * plan.gy,
        compiler_params=params(),
        cost_estimate=cost(plan.per * nx * ny * ny, 2 * plan.per * nx * ny),
        name="last_y_inverse",
    )(place, jnp.asarray(table), slope)


def last_x_inverse(plan, place, blocks):
    x, y, nx, gx = plan.x, plan.y, plan.nx, plan.gx
    twice, low = doubled(-inverse_basis(nx).T, 1)

    def kernel(place_ref, twice_ref, low_ref, *refs):
        ins, out = refs[:-1], refs[-1]
        me = place_ref[1]
        found = side_by_side((twice_ref[...], low_ref[...]), [ref[0] for ref in ins])
        for s, value in enumerate(found):
            out[:, source(me, s, plan.gy), 0] = value.reshape(gx, x, y)

    return pl.pallas_call(
        kernel,
        grid=(plan.per,),
        in_specs=[scalars(), whole_block(twice.shape), whole_block(low.shape)]
        + [pl.BlockSpec((1, nx, y), lambda i: (i, 0, 0))] * plan.gy,
        out_specs=pl.BlockSpec((gx, plan.gy, 1, x, y), lambda i: (0, 0, i, 0, 0)),
        out_shape=jax.ShapeDtypeStruct((gx, plan.gy, plan.per, x, y), jnp.float32),
        compiler_params=params(),
        cost_estimate=cost(plan.per * plan.ny * nx * nx, 2 * plan.per * plan.ny * nx),
        name="last_x_inverse",
    )(place, jnp.asarray(twice), jnp.asarray(low), *blocks)


def pair_y_inverse(plan, place, planes, behind):
    x, y, ny = plan.x, plan.y, plan.ny
    count = planes.shape[0]
    table = halves(np.stack(np.split(inverse_basis(ny), plan.gy, axis=1)))
    deep = fit(count, Y_DEEP)
    rows = deep * x
    half = ny // 2

    def kernel(place_ref, table_ref, in_ref, _, *outs):
        plain = in_ref[...].reshape(rows, ny)
        wave = lax.broadcasted_iota(jnp.int32, (1, half), 1).astype(jnp.float32)
        along = jnp.concatenate([wave * plain[:, half:], -wave * plain[:, :half]], axis=1)
        found = pieces_of_y(plan, table_ref, place_ref[1], [along, plain])
        for comp, pieces in enumerate(found):
            for out, piece in zip(outs[:-1], pieces):
                out[comp] = piece.reshape(deep, x, y)

    return pl.pallas_call(
        kernel,
        grid=(count // deep,),
        in_specs=[
            scalars(),
            whole_block(table.shape),
            pl.BlockSpec((deep, x, ny), lambda i: (i, 0, 0)),
            unread(),
        ],
        out_specs=[pl.BlockSpec((2, deep, x, y), lambda i: (0, i, 0, 0))] * plan.gy + [unread()],
        out_shape=[jax.ShapeDtypeStruct((2, count, x, y), jnp.float32)] * plan.gy
        + [jax.ShapeDtypeStruct(behind.shape, behind.dtype)],
        input_output_aliases={3: plan.gy},
        compiler_params=params(),
        cost_estimate=cost(2 * count * x * ny * ny, 3 * count * x * ny),
        name="pair_y_inverse",
    )(place, jnp.asarray(table), planes, behind)


def image_part(plan, place, comps, tables, blocks, fields, before, weight):
    x, y, z = plan.x, plan.y, plan.z
    outs = len(blocks)
    rows = z // outs
    table = np.stack([halves(table) for table in tables]).reshape(len(comps), 2, outs, rows, z)
    group = fit(x, Z_GROUP)
    deep = fit(group, 2)

    def kernel(place_ref, table_ref, *refs):
        refs = list(refs)
        inputs = [[refs.pop(0) for _ in comps] for _ in range(3)]
        started = [refs.pop(0) for _ in before]
        *ins, image_p, image_s = refs
        at = pl.program_id(0) * group
        order = [source(place_ref[1], s, outs) if outs > 1 else 0 for s in range(outs)]
        turned_tables = []
        for comp in range(len(comps)):
            parts = [joined([table_ref[comp, i, g] for g in order], 0) for i in range(2)]
            high, low = (part.astype(jnp.float32).T.astype(jnp.bfloat16) for part in parts)
            turned_tables.append((jnp.concatenate([high, high], axis=1), low))
        for plane in range(0, group, deep):
            here = slice(plane, plane + deep)
            total_p, total_s = (ref[here] for ref in started) if before else (0.0, 0.0)
            for comp, table in enumerate(turned_tables):
                v_ref, p_ref, s_ref = (each[comp] for each in inputs)
                columns = []
                for k in range(deep):
                    cut = pl.ds(at + plane + k, rows, stride=x)
                    columns.append(joined([ref[comp, cut, :] for ref in ins], 0))
                field = left_times(table, joined(columns, 1)).T.reshape(deep, y, z)
                total_p += p_ref[0, here].astype(jnp.float32) * field
                total_s += s_ref[0, here].astype(jnp.float32) * (v_ref[0, here] - field)
            image_p[here] = total_p
            image_s[here] = total_s

    def block(comp):
        return pl.BlockSpec((1, group, y, z), lambda i: (comp, i, 0, 0))

    blocks = [part.reshape(len(comps), rows * x, y) for part in blocks]
    image = pl.BlockSpec((group, y, z), lambda i: (i, 0, 0))
    return pl.pallas_call(
        kernel,
        grid=(x // group,),
        in_specs=[scalars(), whole_block(table.shape)]
        + [block(comp) for _ in fields for comp in comps]
        + [image] * len(before)
        + [whole_block(part.shape) for part in blocks],
        out_specs=[image, image],
        out_shape=[jax.ShapeDtypeStruct((x, y, z), jnp.float32)] * 2,
        compiler_params=params(),
        cost_estimate=cost(
            weight * len(comps) * x * y * z * z, weight * (2 + 3 * len(comps)) * x * y * z
        ),
        name="image_part",
    )(
        place,
        jnp.asarray(table),
        *[field for field in fields for _ in comps],
        *before,
        *blocks,
    )


def over_gx(blocks):
    return lax.all_to_all(blocks, "gx", 0, 0, tiled=True)


def separated(plan, place, velocity, source_p, source_s):
    x, y, z, gx, gy, per = plan.x, plan.y, plan.z, plan.gx, plan.gy, plan.per
    plain = basis(z)
    pair = along_z(plan, place, velocity, (1, 2), (plain, turned(plain)), gy)
    (first,) = along_z(plan, place, velocity, (0,), (crossed(plain, plan),), 1, pair[:1])
    first = over_gx(first.reshape(gx, gy, per, x, y))
    pair = pair_y_forward(plan, place, swap_gy(pair))
    pair = over_gx(pair.reshape(gx, per, x, plan.ny))
    first = first_y_forward(plan, place, swap_gy(first_x_forward(plan, place, first)))
    lines, slope = potential(plan, place, first, pair)
    pair = over_gx(lines)
    last = last_x_inverse(plan, place, swap_gy(last_y_inverse(plan, place, slope)))
    *pair, last = pair_y_inverse(plan, place, pair.reshape(gx * per, x, plan.ny), last)
    pair = swap_gy(pair)
    last = over_gx(last)
    back = inverse_basis(z)
    fields = (velocity, source_p, source_s)
    found = image_part(plan, place, (1, 2), (back, -turned(back)), pair, fields, (), WEIGHT)
    return image_part(plan, place, (0,), (crossed(back, plan),), [last], fields, found, 1)


def shards(velocity, stress, lame_lambda, shear_modulus, buoyancy, source_p, source_s):
    velocity = propagate(velocity, stress, lame_lambda, shear_modulus, buoyancy)
    plan = Plan(velocity.shape[1:])
    place = jnp.stack([lax.axis_index("gx"), lax.axis_index("gy")]).astype(jnp.int32)
    if plan.z % (plan.gx * plan.gy) == 0:
        return tuple(separated(plan, place, velocity, source_p, source_s))
    blocks = z_forward(plan, place, velocity)
    lines = [to_lines(plan, y_forward(plan, place, swap_gy(group))) for group in blocks]
    lines = [x_lines(plan, place, part, chunk) for chunk, part in enumerate(lines)]
    blocks = [swap_gy(y_inverse(plan, place, to_planes(plan, part))) for part in lines]
    return tuple(images(plan, place, blocks, velocity, source_p, source_s))


def solution(mesh):
    in_specs = (
        P(None, "gx", "gy", None),
        P(None, "gx", "gy", None),
        P("gx", "gy", None),
        P("gx", "gy", None),
        P("gx", "gy", None),
        P(None, "gx", "gy", None),
        P(None, "gx", "gy", None),
    )
    out_specs = (P("gx", "gy", None), P("gx", "gy", None))
    return jax.shard_map(shards, mesh=mesh, in_specs=in_specs, out_specs=out_specs, check_vma=False)
```

```python
import numpy as np
import ml_dtypes
import jax
import jax.numpy as jnp
from jax import lax
from jax.experimental import pallas as pl
from jax.experimental.pallas import tpu as pltpu
from jax.sharding import PartitionSpec as P

STEPS = 2
MOST_CHUNKS = 1
VMEM_BYTES = 63 * 2**20
STENCIL_BYTES = 22 * 2**20
Y_DEEP = 32
Z_GROUP = 16
X_GROUP = 4
LINE_GROUP = 16
Y_TILE = 32
WEIGHT = 1000

time_step = 0.2


def passed_along(block, axis, distance):
    devices = range(lax.axis_size(axis))
    route = [(i - distance, i) for i in devices if i - distance in devices]
    return lax.ppermute(block, axis, route)


def across_corner(row, x_way, y_way):
    x_count, y_count = lax.axis_size("gx"), lax.axis_size("gy")
    route = [
        ((i - x_way) * y_count + j - y_way, i * y_count + j)
        for i in range(x_count)
        for j in range(y_count)
        if 0 <= i - x_way < x_count and 0 <= j - y_way < y_count
    ]
    return lax.ppermute(row, ("gx", "gy"), route)


def exchange(x_last, x_first, y_last, y_first, corner_y, corner_x):
    yl, yr = passed_along(y_last, "gy", 1), passed_along(y_first, "gy", -1)
    xl, xr = passed_along(x_last, "gx", 1), passed_along(x_first, "gx", -1)
    return (yl, yr), (xl, xr, across_corner(corner_y, -1, 1), across_corner(corner_x, 1, -1))


def first_rims(brick, velocity, stress, lame, shear):
    x, y, z = brick
    some = fit(y, 8)
    many = fit(y, 16)

    def kernel(*refs):
        (v_first, v_last, s_first, s_last, lame_first, shear_first, shear_last) = refs[:7]
        (v_low, v_high, s_low, s_high, lame_low, shear_low, shear_high) = refs[7:14]
        x_last, x_first, y_last, y_first, corner_y, corner_x = refs[14:]

        def wide(value):
            return value.astype(jnp.float32)

        for i in range(3):
            x_last[i], x_first[i] = v_last[i, 0], v_first[i, 0]
            y_last[i], y_first[i] = v_high[i, :, some - 1], v_low[i, :, 0]
        x_last[3], x_last[4], x_last[5] = s_last[3, 0], s_last[4, 0], wide(shear_last[0])
        x_first[3], x_first[4], x_first[5] = s_first[0, 0], wide(lame_first[0]), wide(shear_first[0])
        y_last[3], y_last[4] = s_high[3, :, some - 1], s_high[5, :, some - 1]
        y_last[5] = wide(shear_high[...])[:, many - 1]
        y_first[3], y_first[4] = s_low[1, :, 0], wide(lame_low[...])[:, 0]
        y_first[5] = wide(shear_low[...])[:, 0]
        corner_y[...] = v_first[1, 0, y - 1 :]
        corner_x[...] = v_last[0, 0, :1]

    def plane(count, at):
        return pl.BlockSpec((count, 1, y, z), lambda i: (0, at, 0, 0))

    def medium_plane(at):
        return pl.BlockSpec((1, y, z), lambda i: (at, 0, 0))

    def rows(count, at):
        return pl.BlockSpec((count, x, some, z), lambda i: (0, 0, at, 0))

    def medium_rows(at):
        return pl.BlockSpec((x, many, z), lambda i: (0, at, 0))

    shapes = [(6, y, z), (6, y, z), (6, x, z), (6, x, z), (1, z), (1, z)]
    ends, highs, most = x - 1, y // some - 1, y // many - 1
    return pl.pallas_call(
        kernel,
        grid=(1,),
        in_specs=[plane(3, 0), plane(3, ends), plane(6, 0), plane(6, ends)]
        + [medium_plane(0), medium_plane(0), medium_plane(ends)]
        + [rows(3, 0), rows(3, highs), rows(6, 0), rows(6, highs)]
        + [medium_rows(0), medium_rows(0), medium_rows(most)],
        out_specs=[whole_block(shape) for shape in shapes],
        out_shape=[jax.ShapeDtypeStruct(shape, jnp.float32) for shape in shapes],
        compiler_params=params(),
        cost_estimate=pl.CostEstimate(
            flops=0, bytes_accessed=80 * (y + 8 * x) * z, transcendentals=0
        ),
        name="first_rims",
    )(
        *(velocity, velocity, stress, stress, lame, shear, shear),
        *(velocity, velocity, stress, stress, lame, shear, shear),
    )


def stencil(brick, state, rims, medium, x_rims, x_medium, done, last):
    x, y, z = brick
    velocity, stress, lame, shear, buoyancy = state
    group = fit(x, X_GROUP)
    groups = x // group
    tall = fit(y, Y_TILE)
    ends = x_rims is not None
    if ends:
        count, of = min(groups, 2), lambda i: i * (groups - 1)
    else:
        count, of = groups - 2, lambda i: i + 1
    f32 = jnp.float32

    def kernel(*refs):
        refs = list(refs)

        def take(number):
            taken = refs[:number]
            del refs[:number]
            return taken

        v_ref, s_ref, lame_ref, shear_ref, buoy_ref = take(5)
        v_next_ref, xx_next_ref, lame_next_ref, shear_next_ref = take(4)
        v_prior_ref, xy_prior_ref, xz_prior_ref, shear_prior_ref = take(4)
        yl, yr = take(2)
        yl_medium, yr_medium = take(2) if medium else (yl, yr)
        if ends:
            xl, xr, edge_y, edge_x = take(4)
            xl_medium, xr_medium = take(2) if medium else (xl, xr)
        given = take(len(done))
        new = take(1)[0]
        if not last:
            s_out, y_last, y_first = take(3)
            if ends:
                x_last, x_first, corner_y, corner_x = take(4)
        carried, xx_after = take(2)
        s_new = take(1)[0] if last else s_out
        turn = pl.program_id(0)
        here_group = of(turn)
        at = here_group * group
        start, end = here_group == 0, here_group == groups - 1
        row = lax.broadcasted_iota(jnp.int32, (y, z), 0)
        lane = lax.broadcasted_iota(jnp.int32, (y, z), 1)

        def next_z(field):
            edge = lane[: field.shape[0]] == z - 1
            return jnp.where(edge, 0.0, pltpu.roll(field, z - 1, 1))

        def prior_z(field):
            edge = lane[: field.shape[0]] == 0
            return jnp.where(edge, 0.0, pltpu.roll(field, 1, 1))

        def next_y(field, rim):
            rows = field.shape[0]
            return jnp.where(row[:rows] == rows - 1, rim, pltpu.roll(field, rows - 1, 0))

        def prior_y(field, rim):
            return jnp.where(row[: field.shape[0]] == 0, rim, pltpu.roll(field, 1, 0))

        def wide(value):
            return value.astype(f32)

        def line(ref, which, place):
            return ref[which, pl.ds(place, 1), :]

        def line_after(place):
            if not ends:
                return line(yl, 1, place)
            return jnp.where(place == x, edge_y[...], line(yl, 1, jnp.minimum(place, x - 1)))

        def line_before(place):
            if not ends:
                return line(yr, 0, place)
            return jnp.where(place < 0, edge_x[...], line(yr, 0, jnp.maximum(place, 0)))

        def begin(value, rim):
            return jnp.where(start, rim(), value) if ends else value

        def finish(value, rim):
            return jnp.where(end, rim(), value) if ends else value

        def fresh():
            shear_rim = begin(wide(shear_prior_ref[0]), lambda: xl_medium[5])
            vx, vy, vz = (begin(v_prior_ref[i, 0], lambda: xl[i]) for i in range(3))
            xy = begin(xy_prior_ref[0, 0], lambda: xl[3])
            xz = begin(xz_prior_ref[0, 0], lambda: xl[4])
            pull = time_step * shear_rim
            carried[0] = vx
            carried[1] = xy + pull * ((next_y(vx, line_before(at - 1)) - vx) + (v_ref[1, 0] - vy))
            carried[2] = xz + pull * ((next_z(vx) - vx) + (v_ref[2, 0] - vz))

        if ends:
            fresh()
        else:
            pl.when(turn == 0)(fresh)
        if not last and done:

            @pl.when(turn == 0)
            def _():
                y_last[...] = given[2][...]
                y_first[...] = given[3][...]

        def after(i, rows):
            return finish(v_next_ref[i, 0, rows], lambda: xr[i, rows])

        spans = [slice(top, top + tall) for top in range(0, y, tall)]

        def row_before(span, field, rim):
            return rim() if span.start == 0 else field[span.start - 1 : span.start]

        def row_after(span, field, rim):
            return rim() if span.stop == y else field[span.stop : span.stop + 1]

        for k in range(group):
            here = at + k
            v_here = [v_ref.at[i, k] for i in range(3)]
            for span in spans:
                vx, vy, vz = (field[span] for field in v_here)
                vx_prior = carried[0, span] if k == 0 else v_ref[0, k - 1, span]
                vy_next = after(1, span) if k == group - 1 else v_ref[1, k + 1, span]
                vz_next = after(2, span) if k == group - 1 else v_ref[2, k + 1, span]
                vy_rim = row_before(span, v_here[1], lambda: line(yl, 1, here))
                vx_rim = row_after(span, v_here[0], lambda: line(yr, 0, here))
                vz_rim = row_after(span, v_here[2], lambda: line(yr, 2, here))
                lame_value, shear_value = wide(lame_ref[k, span]), wide(shear_ref[k, span])
                ex = vx - vx_prior
                ey = vy - prior_y(vy, vy_rim)
                ez = vz - prior_z(vz)
                swell = lame_value * (ex + ey + ez)
                double = 2.0 * shear_value
                pull = time_step * shear_value
                found = (
                    s_ref[0, k, span] + time_step * (swell + double * ex),
                    s_ref[1, k, span] + time_step * (swell + double * ey),
                    s_ref[2, k, span] + time_step * (swell + double * ez),
                    s_ref[3, k, span] + pull * ((next_y(vx, vx_rim) - vx) + (vy_next - vy)),
                    s_ref[4, k, span] + pull * ((next_z(vx) - vx) + (vz_next - vz)),
                    s_ref[5, k, span] + pull * ((next_z(vy) - vy) + (next_y(vz, vz_rim) - vz)),
                )
                for i, value in enumerate(found):
                    s_new[i, k, span] = value

        for span in spans:
            vx, vy, vz = (after(i, span) for i in range(3))
            vy_rim = (
                line_after(at + group)
                if span.start == 0
                else after(1, slice(span.start - 1, span.start))
            )
            ex = vx - v_ref[0, group - 1, span]
            ey = vy - prior_y(vy, vy_rim)
            ez = vz - prior_z(vz)
            lame_value = finish(wide(lame_next_ref[0, span]), lambda: xr_medium[4, span])
            shear_value = finish(wide(shear_next_ref[0, span]), lambda: xr_medium[5, span])
            xx_after[span] = finish(xx_next_ref[0, 0, span], lambda: xr[3, span]) + time_step * (
                lame_value * (ex + ey + ez) + 2.0 * shear_value * ex
            )

        for k in range(group):
            here = at + k
            v_here = [v_ref.at[i, k] for i in range(3)]
            vx_edge, vy_edge, vz_edge = v_here[0][:1], v_here[1][y - 1 :], v_here[2][:1]
            pull = time_step * line(yl_medium, 5, here)
            vy_rim, vz_rim = line(yl, 1, here), line(yl, 2, here)
            xy_rim = line(yl, 3, here) + pull * (
                (vx_edge - line(yl, 0, here)) + (line_after(here + 1) - vy_rim)
            )
            yz_rim = line(yl, 4, here) + pull * ((next_z(vy_rim) - vy_rim) + (vz_edge - vz_rim))
            vx_rim, vz_rim = line(yr, 0, here), line(yr, 2, here)
            ex = vx_rim - line_before(here - 1)
            ey = line(yr, 1, here) - vy_edge
            ez = vz_rim - prior_z(vz_rim)
            yy_rim = line(yr, 3, here) + time_step * (
                line(yr_medium, 4, here) * (ex + ey + ez) + 2.0 * line(yr_medium, 5, here) * ey
            )
            s_here = [s_new.at[i, k] for i in range(6)]
            for span in spans:
                xx, yy, zz, xy, xz, yz = (field[span] for field in s_here)
                xx_next = xx_after[span] if k == group - 1 else s_new[0, k + 1, span]
                xy_prior = carried[1, span] if k == 0 else s_new[3, k - 1, span]
                xz_prior = carried[2, span] if k == 0 else s_new[4, k - 1, span]
                xy_before = row_before(span, s_here[3], lambda: xy_rim)
                yz_before = row_before(span, s_here[5], lambda: yz_rim)
                yy_after = row_after(span, s_here[1], lambda: yy_rim)
                push = time_step * wide(buoy_ref[k, span])
                new[0, k, span] = v_ref[0, k, span] + push * (
                    (xx_next - xx) + (xy - prior_y(xy, xy_before)) + (xz - prior_z(xz))
                )
                new[1, k, span] = v_ref[1, k, span] + push * (
                    (xy - xy_prior) + (next_y(yy, yy_after) - yy) + (yz - prior_z(yz))
                )
                new[2, k, span] = v_ref[2, k, span] + push * (
                    (xz - xz_prior) + (yz - prior_y(yz, yz_before)) + (next_z(zz) - zz)
                )
            if last:
                continue
            for i in range(3):
                y_last[i, pl.ds(here, 1), :] = new[i, k, y - 1 :]
                y_first[i, pl.ds(here, 1), :] = new[i, k, :1]
            y_last[3, pl.ds(here, 1), :] = s_new[3, k, y - 1 :]
            y_last[4, pl.ds(here, 1), :] = s_new[5, k, y - 1 :]
            y_first[3, pl.ds(here, 1), :] = s_new[1, k, :1]

        if ends and not last:

            @pl.when(start)
            def _():
                for i in range(3):
                    x_first[i] = new[i, 0]
                x_first[3] = s_new[0, 0]
                corner_y[...] = new[1, 0, y - 1 :]

            @pl.when(end)
            def _():
                for i in range(3):
                    x_last[i] = new[i, group - 1]
                x_last[3], x_last[4] = s_new[3, group - 1], s_new[4, group - 1]
                corner_x[...] = new[0, group - 1, :1]

        if not ends:
            carried[0] = v_ref[0, group - 1]
            carried[1] = s_new[3, group - 1]
            carried[2] = s_new[4, group - 1]

    def next_plane(i):
        return jnp.minimum((of(i) + 1) * group, x - 1)

    def prior_plane(i):
        return jnp.maximum(of(i) * group - 1, 0) if ends else group - 1

    def planes(number):
        return pl.BlockSpec((number, group, y, z), lambda i: (0, of(i), 0, 0))

    def one(number, which, place):
        return pl.BlockSpec((number, 1, y, z), lambda i: (which, place(i), 0, 0))

    def medium_one(place):
        return pl.BlockSpec((1, y, z), lambda i: (place(i), 0, 0))

    medium_block = pl.BlockSpec((group, y, z), lambda i: (of(i), 0, 0))
    args = [velocity, stress, lame, shear, buoyancy, velocity, stress, lame, shear]
    args += [velocity, stress, stress, shear, *rims, *medium]
    in_specs = [planes(3), planes(6), medium_block, medium_block, medium_block]
    in_specs += [one(3, 0, next_plane), one(1, 0, next_plane)]
    in_specs += [medium_one(next_plane), medium_one(next_plane)]
    in_specs += [one(3, 0, prior_plane), one(1, 3, prior_plane), one(1, 4, prior_plane)]
    in_specs += [medium_one(prior_plane)]
    in_specs += [whole_block(rim.shape) for rim in (*rims, *medium)]
    if ends:
        args += [*x_rims, *x_medium]
        in_specs += [whole_block(rim.shape) for rim in (*x_rims, *x_medium)]
    aliases = {}
    for i, value in enumerate(done):
        if i < 2:
            aliases[len(args)] = i
        in_specs.append(unread() if i < 2 else whole_block(value.shape))
        args.append(value)
    out_shape = [(3, x, y, z)]
    out_specs = [planes(3)]
    if not last:
        out_shape += [(6, x, y, z), (5, x, z), (4, x, z)]
        out_specs += [planes(6)]
        if ends:
            out_shape += [(5, y, z), (4, y, z), (1, z), (1, z)]
        out_specs += [whole_block(shape) for shape in out_shape[2:]]
    part = (1 if ends else WEIGHT) * count * group * y * z
    return pl.pallas_call(
        kernel,
        grid=(count,),
        in_specs=in_specs,
        out_specs=out_specs,
        out_shape=[jax.ShapeDtypeStruct(shape, f32) for shape in out_shape],
        scratch_shapes=[pltpu.VMEM((3, y, z), f32), pltpu.VMEM((y, z), f32)]
        + ([pltpu.VMEM((6, group, y, z), f32)] if last else []),
        input_output_aliases=aliases,
        compiler_params=params(STENCIL_BYTES),
        cost_estimate=pl.CostEstimate(
            flops=80 * part, bytes_accessed=(54 if last else 78) * part, transcendentals=0
        ),
        name="stencil_ends" if ends else "stencil_middle",
    )(*args)


def propagate(velocity, stress, lame, shear, buoyancy):
    brick = velocity.shape[1:]
    between = brick[0] // fit(brick[0], X_GROUP) > 2
    rims, x_rims = exchange(*first_rims(brick, velocity, stress, lame, shear))
    held, medium, x_medium = (rims, x_rims[:2]), (), ()
    for step_index in range(STEPS):
        last = step_index == STEPS - 1
        state = (velocity, stress, lame, shear, buoyancy)
        done = []
        if between:
            done = stencil(brick, state, rims, medium, None, None, done, last)
        found = stencil(brick, state, rims, medium, x_rims, x_medium, done, last)
        velocity = found[0]
        if not last:
            stress, y_last, y_first, x_last, x_first, corner_y, corner_x = found[1:]
            rims, x_rims = exchange(x_last, x_first, y_last, y_first, corner_y, corner_x)
            medium, x_medium = held
    return velocity


def basis(length):
    half = length // 2
    wave = np.arange(half)
    place = np.arange(length)
    angle = (wave[:, None] * place[None, :] % length) * (2.0 * np.pi / length)
    cosine, sine = np.cos(angle), np.sin(angle)
    sine[0] = 1.0 - 2.0 * (place % 2)
    return np.concatenate([cosine, sine])


def waves_of(length):
    return np.tile(np.arange(length // 2, dtype=np.float64), 2)


def inverse_basis(length):
    weight = np.where(waves_of(length) == 0, 1.0, 2.0) / length
    return basis(length) * weight[:, None]


def turned(table):
    half = table.shape[0] // 2
    return np.concatenate([table[half:], -table[:half]]) * waves_of(table.shape[0])[:, None]


def halves(table):
    high = table.astype(ml_dtypes.bfloat16)
    low = (table - high.astype(np.float64)).astype(ml_dtypes.bfloat16)
    return np.stack([high, low])


def split(value):
    high = value.astype(jnp.bfloat16)
    return high, (value - high.astype(jnp.float32)).astype(jnp.bfloat16)


def dot(left, right, dims=((1,), (0,))):
    return lax.dot_general(left, right, (dims, ((), ())), preferred_element_type=jnp.float32)


def times(left, right):
    return dot(left[0], right[0]) + (dot(left[1], right[0]) + dot(left[0], right[1]))


def joined(pieces, axis):
    return pieces[0] if len(pieces) == 1 else jnp.concatenate(pieces, axis=axis)


def fit(length, most):
    size = min(length, most)
    while length % size:
        size -= 1
    return size


def params(limit=VMEM_BYTES):
    return pltpu.CompilerParams(vmem_limit_bytes=limit)


def whole_block(shape):
    return pl.BlockSpec(shape, lambda *_: (0,) * len(shape))


def scalars():
    return pl.BlockSpec(memory_space=pltpu.SMEM)


class Plan:
    def __init__(self, brick):
        self.x, self.y, self.z = brick
        self.gx, self.gy = lax.axis_size("gx"), lax.axis_size("gy")
        self.nx, self.ny = self.x * self.gx, self.y * self.gy
        chunks = MOST_CHUNKS
        while chunks > 1 and self.z % (chunks * self.gy * self.gx):
            chunks -= 1
        self.chunks = chunks
        self.kz = self.z // (chunks * self.gy)
        self.parts = max(1, self.gx // self.kz)
        self.per = max(1, self.kz // self.gx)
        self.ky = self.ny // self.parts


def source(me, step, count):
    return lax.rem(me - step + count, count)


def z_forward(plan, place, velocity):
    x, y, z, kz = plan.x, plan.y, plan.z, plan.kz
    table = np.stack([halves(basis(z)), halves(turned(basis(z)))])
    table = table.reshape(2, 2, plan.chunks, plan.gy, kz, z)
    count = plan.chunks * plan.gy

    group = fit(x, Z_GROUP)
    deep = fit(group, 2)

    def kernel(place_ref, table_ref, v_ref, *outs):
        at = pl.program_id(0) * group
        me = place_ref[1]
        order = [(c, lax.rem(me + s, plan.gy)) for c in range(plan.chunks) for s in range(plan.gy)]
        tables = []
        for kind in range(2):
            high, low = (joined([table_ref[kind, i, c, g] for c, g in order], 0) for i in range(2))
            tables.append((jnp.concatenate([high, high], axis=1), low))
        for comp in range(3):
            twice, low = tables[1 if comp == 2 else 0]
            for plane in range(0, group, deep):
                field = split(v_ref[comp, plane : plane + deep].reshape(deep * y, z))
                value = dot(twice, jnp.concatenate(field, axis=1), ((1,), (1,)))
                value += dot(low, field[0], ((1,), (1,)))
                for i, out in enumerate(outs):
                    for k in range(deep):
                        part = value[i * kz : (i + 1) * kz, k * y : (k + 1) * y]
                        out[comp, pl.ds(at + plane + k, kz, stride=x), :] = part

    outs = pl.pallas_call(
        kernel,
        grid=(x // group,),
        in_specs=[
            scalars(),
            whole_block(table.shape),
            pl.BlockSpec((3, group, y, z), lambda i: (0, i, 0, 0)),
        ],
        out_specs=[whole_block((3, kz * x, y))] * count,
        out_shape=[jax.ShapeDtypeStruct((3, kz * x, y), jnp.float32)] * count,
        compiler_params=params(),
        cost_estimate=pl.CostEstimate(
            flops=18 * x * y * z * z, bytes_accessed=24 * x * y * z, transcendentals=0
        ),
        name="z_forward",
    )(place, jnp.asarray(table), velocity)
    outs = [out.reshape(3, kz, x, y) for out in outs]
    return [outs[c * plan.gy : (c + 1) * plan.gy] for c in range(plan.chunks)]


def swap_gy(blocks):
    count = len(blocks)
    moved = [blocks[0]]
    for step in range(1, count):
        route = [(i, (i + step) % count) for i in range(count)]
        moved.append(lax.ppermute(blocks[step], "gy", route))
    return moved


def y_forward(plan, place, blocks):
    x, y, ny, kz = plan.x, plan.y, plan.ny, plan.kz
    table = halves(basis(ny).T).reshape(2, plan.gy, y, ny)
    deep = fit(kz, 8)
    rows = deep * x
    half = ny // 2
    aligned = y % 128 == 0

    def kernel(place_ref, table_ref, *refs):
        ins, out = refs[:-1], refs[-1]
        me = place_ref[1]
        groups = [source(me, step, plan.gy) for step in range(plan.gy)]
        tables = [(table_ref[0, g], table_ref[1, g]) for g in groups]
        if aligned:
            tables = [tuple(joined([t[i] for t in tables], 0) for i in range(2))]

        def moved(comp):
            fields = [ref[comp].reshape(rows, y) for ref in ins]
            if aligned:
                fields = [joined(fields, 1)]
            return sum(times(split(f), t) for f, t in zip(fields, tables))

        wave = lax.broadcasted_iota(jnp.int32, (1, half), 1).astype(jnp.float32)
        out[:, 0] = moved(0).reshape(deep, x, ny)
        along, rest = moved(1), moved(2)
        out[:, 1, :, :half] = (rest[:, :half] + wave * along[:, half:]).reshape(deep, x, half)
        out[:, 1, :, half:] = (rest[:, half:] - wave * along[:, :half]).reshape(deep, x, half)

    return pl.pallas_call(
        kernel,
        grid=(kz // deep,),
        in_specs=[scalars(), whole_block(table.shape)]
        + [pl.BlockSpec((3, deep, x, y), lambda i: (0, i, 0, 0))] * plan.gy,
        out_specs=pl.BlockSpec((deep, 2, x, ny), lambda i: (i, 0, 0, 0)),
        out_shape=jax.ShapeDtypeStruct((kz, 2, x, ny), jnp.float32),
        compiler_params=params(),
        cost_estimate=pl.CostEstimate(
            flops=18 * kz * x * ny * ny, bytes_accessed=20 * kz * x * ny, transcendentals=0
        ),
        name="y_forward",
    )(place, jnp.asarray(table), *blocks)


def to_lines(plan, planes):
    if plan.parts > 1:
        planes = planes.reshape(plan.kz, 2, plan.x, plan.parts, plan.ky).transpose(0, 3, 1, 2, 4)
    planes = planes.reshape(plan.gx, plan.per, 2, plan.x, plan.ky)
    return lax.all_to_all(planes, "gx", 0, 0, tiled=True)


def to_planes(plan, lines):
    planes = lax.all_to_all(lines, "gx", 0, 0, tiled=True)
    if plan.parts > 1:
        planes = planes.reshape(plan.kz, plan.parts, 2, plan.x, plan.ky).transpose(0, 2, 3, 1, 4)
    return planes.reshape(plan.kz, 2, plan.x, plan.ny)


def x_lines(plan, place, lines, chunk):
    x, nx, ny, ky, gx = plan.x, plan.nx, plan.ny, plan.ky, plan.gx
    forth = halves(basis(nx))
    back = halves(-inverse_basis(nx).T)
    lanes = 128 if ky % 128 == 0 else ky
    half = nx // 2
    aligned = lanes % 128 == 0

    def kernel(place_ref, forth_ref, back_ref, in_ref, out_ref):
        me_x, me_y = place_ref[0], place_ref[1]
        which, lane = pl.program_id(0), pl.program_id(1)

        def through(table_ref, pair):
            table = (table_ref[0], table_ref[1])
            if aligned:
                both = times(table, split(jnp.concatenate(pair, axis=1)))
                return both[:, :lanes], both[:, lanes:]
            return tuple(times(table, split(value)) for value in pair)

        pair = [in_ref[:, 0, i].reshape(nx, lanes) for i in range(2)]
        along, rest = through(forth_ref, pair)
        wave_x = lax.broadcasted_iota(jnp.int32, (half, lanes), 0).astype(jnp.float32)
        slot_y = lax.broadcasted_iota(jnp.int32, (1, lanes), 1) + (
            lane * lanes + lax.rem(me_x, plan.parts) * ky
        )
        wave_y = lax.rem(slot_y, ny // 2).astype(jnp.float32)
        slot_z = (chunk * plan.gy + me_y) * plan.kz + me_x // plan.parts * plan.per + which
        wave_z = lax.rem(slot_z, plan.z // 2).astype(jnp.float32)
        scale = 1.0 / jnp.maximum(wave_x * wave_x + (wave_y * wave_y + wave_z * wave_z), 1.0)
        cosine = (rest[:half] + wave_x * along[half:]) * scale
        sine = (rest[half:] - wave_x * along[:half]) * scale
        plain = jnp.concatenate([cosine, sine], axis=0)
        slope = jnp.concatenate([wave_x * sine, -wave_x * cosine], axis=0)
        for i, value in enumerate(through(back_ref, [slope, plain])):
            out_ref[:, 0, i] = value.reshape(gx, x, lanes)

    block = pl.BlockSpec((gx, 1, 2, x, lanes), lambda i, j: (0, i, 0, 0, j))
    return pl.pallas_call(
        kernel,
        grid=(plan.per, ky // lanes),
        in_specs=[scalars(), whole_block(forth.shape), whole_block(back.shape), block],
        out_specs=block,
        out_shape=jax.ShapeDtypeStruct(lines.shape, jnp.float32),
        compiler_params=params(),
        cost_estimate=pl.CostEstimate(
            flops=24 * plan.per * ky * nx * nx,
            bytes_accessed=16 * plan.per * ky * nx,
            transcendentals=0,
        ),
        name="x_lines",
    )(place, jnp.asarray(forth), jnp.asarray(back), lines)


def y_inverse(plan, place, planes):
    x, y, ny, kz = plan.x, plan.y, plan.ny, plan.kz
    table = np.stack(np.split(inverse_basis(ny), plan.gy, axis=1))
    table = halves(table)
    deep = fit(kz, 8)
    rows = deep * x
    half = ny // 2
    aligned = y % 128 == 0

    def kernel(place_ref, table_ref, in_ref, *outs):
        me = place_ref[1]
        groups = [lax.rem(me + step, plan.gy) for step in range(plan.gy)]
        tables = [(table_ref[0, g], table_ref[1, g]) for g in groups]
        slope = in_ref[:, 0].reshape(rows, ny)
        plain = in_ref[:, 1].reshape(rows, ny)
        wave = lax.broadcasted_iota(jnp.int32, (1, half), 1).astype(jnp.float32)
        along = jnp.concatenate([wave * plain[:, half:], -wave * plain[:, :half]], axis=1)
        for comp, value in enumerate((slope, along, plain)):
            parts = split(value)
            if aligned:
                table = tuple(joined([t[i] for t in tables], 1) for i in range(2))
                found = times(parts, table)
                pieces = [found[:, s * y : (s + 1) * y] for s in range(plan.gy)]
            else:
                pieces = [times(parts, t) for t in tables]
            for out, piece in zip(outs, pieces):
                out[comp] = piece.reshape(deep, x, y)

    return pl.pallas_call(
        kernel,
        grid=(kz // deep,),
        in_specs=[
            scalars(),
            whole_block(table.shape),
            pl.BlockSpec((deep, 2, x, ny), lambda i: (i, 0, 0, 0)),
        ],
        out_specs=[pl.BlockSpec((3, deep, x, y), lambda i: (0, i, 0, 0))] * plan.gy,
        out_shape=[jax.ShapeDtypeStruct((3, kz, x, y), jnp.float32)] * plan.gy,
        compiler_params=params(),
        cost_estimate=pl.CostEstimate(
            flops=18 * kz * x * ny * ny, bytes_accessed=20 * kz * x * ny, transcendentals=0
        ),
        name="y_inverse",
    )(place, jnp.asarray(table), planes)


def images(plan, place, blocks, velocity, source_p, source_s):
    x, y, z, kz = plan.x, plan.y, plan.z, plan.kz
    table = np.stack([halves(inverse_basis(z)), halves(-turned(inverse_basis(z)))])
    table = table.reshape(2, 2, plan.chunks, plan.gy, kz, z)
    blocks = [block.reshape(3, kz * x, y) for group in blocks for block in group]

    group = fit(x, Z_GROUP)
    deep = fit(group, 2)

    def kernel(place_ref, table_ref, v_ref, p_ref, s_ref, *refs):
        ins, (image_p, image_s) = refs[:-2], refs[-2:]
        at = pl.program_id(0) * group
        me = place_ref[1]
        order = [
            (chunk, source(me, step, plan.gy))
            for chunk in range(plan.chunks)
            for step in range(plan.gy)
        ]
        tables = []
        for kind in range(2):
            high, low = (joined([table_ref[kind, i, c, g] for c, g in order], 0) for i in range(2))
            high, low = (part.astype(jnp.float32).T.astype(jnp.bfloat16) for part in (high, low))
            tables.append((jnp.concatenate([high, high], axis=1), low))
        for plane in range(0, group, deep):
            here = slice(plane, plane + deep)
            total_p = total_s = 0.0
            for comp in range(3):
                twice, low = tables[1 if comp == 2 else 0]
                columns = [
                    joined([ref[comp, pl.ds(at + plane + k, kz, stride=x), :] for ref in ins], 0)
                    for k in range(deep)
                ]
                high, rest = split(joined(columns, 1))
                field = dot(twice, jnp.concatenate([high, rest], axis=0)) + dot(low, high)
                field = field.T.reshape(deep, y, z)
                total_p += p_ref[comp, here].astype(jnp.float32) * field
                total_s += s_ref[comp, here].astype(jnp.float32) * (v_ref[comp, here] - field)
            image_p[here] = total_p
            image_s[here] = total_s

    plane = pl.BlockSpec((3, group, y, z), lambda i: (0, i, 0, 0))
    image = pl.BlockSpec((group, y, z), lambda i: (i, 0, 0))
    return pl.pallas_call(
        kernel,
        grid=(x // group,),
        in_specs=[scalars(), whole_block(table.shape), plane, plane, plane]
        + [whole_block((3, kz * x, y))] * len(blocks),
        out_specs=[image, image],
        out_shape=[jax.ShapeDtypeStruct((x, y, z), jnp.float32)] * 2,
        compiler_params=params(),
        cost_estimate=pl.CostEstimate(
            flops=18 * x * y * z * z, bytes_accessed=44 * x * y * z, transcendentals=0
        ),
        name="images",
    )(place, jnp.asarray(table), velocity, source_p, source_s, *blocks)


def doubled(table, axis):
    high, low = halves(table)
    return np.concatenate([high, high], axis=axis), low


def left_times(table, value):
    high, low = split(value)
    return dot(table[0], jnp.concatenate([high, low], axis=0)) + dot(table[1], high)


def right_times(value, table):
    high, low = split(value)
    return dot(jnp.concatenate([high, low], axis=1), table[0]) + dot(high, table[1])


def odd_basis(length):
    wave = 2 * np.arange(length // 4) + 1
    angle = (wave[:, None] * np.arange(length // 2) % length) * (2.0 * np.pi / length)
    return np.concatenate([np.cos(angle), np.sin(angle)])


def x_tables(length, inverse):
    even, odd = basis(length // 2), odd_basis(length)
    if inverse:
        even, odd = -inverse_basis(length // 2).T / 2.0, -odd.T * (2.0 / length)
    return [*doubled(even, 1), *doubled(odd, 1)]


def x_forward(tables, value):
    half = value.shape[0] // 2
    even = left_times(tables[:2], value[:half] + value[half:])
    return jnp.concatenate([even, left_times(tables[2:], value[:half] - value[half:])], axis=0)


def x_inverse(tables, value):
    half = value.shape[0] // 2
    even = left_times(tables[:2], value[:half])
    odd = left_times(tables[2:], value[half:])
    return jnp.concatenate([even + odd, even - odd], axis=0)


def x_wave(length):
    slot = lax.broadcasted_iota(jnp.int32, (length, 1), 0)
    wave = 2 * lax.rem(slot, length // 4) + slot // (length // 2)
    return wave.astype(jnp.float32)


def slope_x(value):
    part = value.shape[0] // 4
    wave = x_wave(value.shape[0])
    swapped = [value[part : 2 * part], -value[:part], value[3 * part :], -value[2 * part : 3 * part]]
    return wave * jnp.concatenate(swapped, axis=0)


def side_by_side(through, tables, values):
    width = values[0].shape[1]
    if width % 128:
        return [through(tables, value) for value in values]
    both = through(tables, joined(values, 1))
    return [both[:, i * width : (i + 1) * width] for i in range(len(values))]


def cost(flops, values):
    return pl.CostEstimate(flops=6 * flops, bytes_accessed=4 * values, transcendentals=0)


def crossed(table, plan):
    shape = (plan.gy, plan.gx, plan.per, table.shape[-1])
    return table.reshape(shape).transpose(1, 0, 2, 3).reshape(table.shape)


def unread():
    return pl.BlockSpec(memory_space=pl.ANY)


def along_z(plan, place, velocity, comps, tables, outs, ahead=()):
    x, y, z = plan.x, plan.y, plan.z
    table = np.stack([halves(table) for table in tables]).reshape(len(comps), 2, outs, z // outs, z)
    group = fit(x, LINE_GROUP)
    deep = fit(group, 2)
    rows = z // outs

    def kernel(place_ref, table_ref, *refs):
        fields, found = refs[: len(comps)], refs[len(comps) + len(ahead) :]
        found = [out.reshape(len(comps), rows * group, y) for out in found]
        me = place_ref[1]
        order = [lax.rem(me + s, outs) if outs > 1 else 0 for s in range(outs)]
        for comp, field in enumerate(fields):
            high, low = (joined([table_ref[comp, i, g] for g in order], 0) for i in range(2))
            twice = jnp.concatenate([high, high], axis=1)
            for plane in range(0, group, deep):
                parts = split(field[0, plane : plane + deep].reshape(deep * y, z))
                value = dot(twice, jnp.concatenate(parts, axis=1), ((1,), (1,)))
                value += dot(low, parts[0], ((1,), (1,)))
                for i, out in enumerate(found):
                    for k in range(deep):
                        part = value[i * rows : (i + 1) * rows, k * y : (k + 1) * y]
                        out[comp, pl.ds(plane + k, rows, stride=group), :] = part

    def block(comp):
        return pl.BlockSpec((1, group, y, z), lambda i: (comp, i, 0, 0))

    shape = (len(comps), rows, x, y)
    return pl.pallas_call(
        kernel,
        grid=(x // group,),
        in_specs=[scalars(), whole_block(table.shape)]
        + [block(comp) for comp in comps]
        + [unread()] * len(ahead),
        out_specs=[pl.BlockSpec((len(comps), rows, group, y), lambda i: (0, 0, i, 0))] * outs,
        out_shape=[jax.ShapeDtypeStruct(shape, jnp.float32)] * outs,
        compiler_params=params(STENCIL_BYTES),
        cost_estimate=cost(len(comps) * x * y * z * z, 2 * len(comps) * x * y * z),
        name="along_z",
    )(place, jnp.asarray(table), *[velocity] * len(comps), *ahead)


def y_table(plan, table_ref, groups):
    tables = [(table_ref[0, g], table_ref[1, g]) for g in groups]
    if plan.y % 128 == 0:
        high, low = (joined([table[i] for table in tables], 0) for i in range(2))
        return [(jnp.concatenate([high, high], axis=0), low)]
    return [(jnp.concatenate([high, high], axis=0), low) for high, low in tables]


def over_y(fields, tables):
    if len(tables) == 1:
        fields = [joined(fields, 1)]
    return sum(right_times(field, table) for field, table in zip(fields, tables))


def pair_y_forward(plan, place, blocks):
    x, y, ny = plan.x, plan.y, plan.ny
    count = blocks[0].shape[1]
    table = halves(basis(ny).T).reshape(2, plan.gy, y, ny)
    deep = fit(count, Y_DEEP)
    rows = deep * x
    half = ny // 2

    def kernel(place_ref, table_ref, *refs):
        ins, out = refs[:-1], refs[-1]
        me = place_ref[1]
        tables = y_table(plan, table_ref, [source(me, s, plan.gy) for s in range(plan.gy)])
        along, rest = (
            over_y([ref[comp].reshape(rows, y) for ref in ins], tables) for comp in range(2)
        )
        wave = lax.broadcasted_iota(jnp.int32, (1, half), 1).astype(jnp.float32)
        out[:, :, :half] = (rest[:, :half] + wave * along[:, half:]).reshape(deep, x, half)
        out[:, :, half:] = (rest[:, half:] - wave * along[:, :half]).reshape(deep, x, half)

    return pl.pallas_call(
        kernel,
        grid=(count // deep,),
        in_specs=[scalars(), whole_block(table.shape)]
        + [pl.BlockSpec((2, deep, x, y), lambda i: (0, i, 0, 0))] * plan.gy,
        out_specs=pl.BlockSpec((deep, x, ny), lambda i: (i, 0, 0)),
        out_shape=jax.ShapeDtypeStruct((count, x, ny), jnp.float32),
        compiler_params=params(),
        cost_estimate=cost(2 * WEIGHT * count * x * ny * ny, 3 * WEIGHT * count * x * ny),
        name="pair_y_forward",
    )(place, jnp.asarray(table), *blocks)


def first_x_forward(plan, place, lines):
    x, y, nx = plan.x, plan.y, plan.nx
    tables = x_tables(nx, False)

    def kernel(place_ref, *refs):
        table_refs, in_ref, outs = refs[:4], refs[4], refs[5:]
        me = place_ref[1]
        fields = [in_ref[:, lax.rem(me + s, plan.gy), 0].reshape(nx, y) for s in range(plan.gy)]
        found = side_by_side(x_forward, [ref[...] for ref in table_refs], fields)
        for out, value in zip(outs, found):
            out[0] = value

    return pl.pallas_call(
        kernel,
        grid=(plan.per,),
        in_specs=[scalars()]
        + [whole_block(table.shape) for table in tables]
        + [pl.BlockSpec((plan.gx, plan.gy, 1, x, y), lambda i: (0, 0, i, 0, 0))],
        out_specs=[pl.BlockSpec((1, nx, y), lambda i: (i, 0, 0))] * plan.gy,
        out_shape=[jax.ShapeDtypeStruct((plan.per, nx, y), jnp.float32)] * plan.gy,
        compiler_params=params(),
        cost_estimate=cost(plan.per * plan.ny * nx * nx, 2 * plan.per * plan.ny * nx),
        name="first_x_forward",
    )(place, *[jnp.asarray(table) for table in tables], lines)


def first_y_forward(plan, place, blocks):
    y, nx, ny = plan.y, plan.nx, plan.ny
    table = halves(basis(ny).T).reshape(2, plan.gy, y, ny)

    def kernel(place_ref, table_ref, *refs):
        ins, out = refs[:-1], refs[-1]
        me = place_ref[1]
        tables = y_table(plan, table_ref, [source(me, s, plan.gy) for s in range(plan.gy)])
        out[0] = slope_x(over_y([ref[0] for ref in ins], tables))

    return pl.pallas_call(
        kernel,
        grid=(plan.per,),
        in_specs=[scalars(), whole_block(table.shape)]
        + [pl.BlockSpec((1, nx, y), lambda i: (i, 0, 0))] * plan.gy,
        out_specs=pl.BlockSpec((1, nx, ny), lambda i: (i, 0, 0)),
        out_shape=jax.ShapeDtypeStruct((plan.per, nx, ny), jnp.float32),
        compiler_params=params(),
        cost_estimate=cost(plan.per * nx * ny * ny, 2 * plan.per * nx * ny),
        name="first_y_forward",
    )(place, jnp.asarray(table), *blocks)


def potential(plan, place, first, lines):
    x, nx, ny, gx = plan.x, plan.nx, plan.ny, plan.gx
    tables = x_tables(nx, False) + x_tables(nx, True)

    def kernel(place_ref, *refs):
        first_ref, in_ref, out_ref, slope_ref = refs[8:]
        forth, back = ([ref[...] for ref in refs[i : i + 4]] for i in (0, 4))
        me_x, me_y = place_ref[0], place_ref[1]
        total = x_forward(forth, in_ref[:, 0].reshape(nx, ny)) + first_ref[0]
        wave_x = x_wave(nx)
        slot_y = lax.broadcasted_iota(jnp.int32, (1, ny), 1)
        wave_y = lax.rem(slot_y, ny // 2).astype(jnp.float32)
        slot_z = (me_y * gx + me_x) * plan.per + pl.program_id(0)
        wave_z = lax.rem(slot_z, plan.z // 2).astype(jnp.float32)
        square = wave_x * wave_x + (wave_y * wave_y + wave_z * wave_z)
        found = total / jnp.maximum(square, 1.0)
        out_ref[:, 0] = x_inverse(back, found).reshape(gx, x, ny)
        slope_ref[0] = slope_x(found)

    spectrum = pl.BlockSpec((1, nx, ny), lambda i: (i, 0, 0))
    block = pl.BlockSpec((gx, 1, x, ny), lambda i: (0, i, 0, 0))
    return pl.pallas_call(
        kernel,
        grid=(plan.per,),
        in_specs=[scalars()] + [whole_block(t.shape) for t in tables] + [spectrum, block],
        out_specs=[block, spectrum],
        out_shape=[
            jax.ShapeDtypeStruct(lines.shape, jnp.float32),
            jax.ShapeDtypeStruct((plan.per, nx, ny), jnp.float32),
        ],
        compiler_params=params(),
        cost_estimate=cost(2 * plan.per * ny * nx * nx, 4 * plan.per * ny * nx),
        name="potential",
    )(place, *[jnp.asarray(t) for t in tables], first, lines)


def pieces_of_y(plan, table_ref, me, values):
    groups = [lax.rem(me + s, plan.gy) for s in range(plan.gy)]
    y = plan.y
    tables = [(table_ref[0, g], table_ref[1, g]) for g in groups]
    if y % 128 == 0:
        tables = [tuple(joined([table[i] for table in tables], 1) for i in range(2))]
    tables = [(jnp.concatenate([high, high], axis=0), low) for high, low in tables]
    found = []
    for value in values:
        pieces = [right_times(value, table) for table in tables]
        if y % 128 == 0:
            pieces = [pieces[0][:, s * y : (s + 1) * y] for s in range(plan.gy)]
        found.append(pieces)
    return found


def last_y_inverse(plan, place, slope):
    y, nx, ny = plan.y, plan.nx, plan.ny
    table = halves(np.stack(np.split(inverse_basis(ny), plan.gy, axis=1)))

    def kernel(place_ref, table_ref, in_ref, *outs):
        (pieces,) = pieces_of_y(plan, table_ref, place_ref[1], [in_ref[0]])
        for out, piece in zip(outs, pieces):
            out[0] = piece

    return pl.pallas_call(
        kernel,
        grid=(plan.per,),
        in_specs=[
            scalars(),
            whole_block(table.shape),
            pl.BlockSpec((1, nx, ny), lambda i: (i, 0, 0)),
        ],
        out_specs=[pl.BlockSpec((1, nx, y), lambda i: (i, 0, 0))] * plan.gy,
        out_shape=[jax.ShapeDtypeStruct((plan.per, nx, y), jnp.float32)] * plan.gy,
        compiler_params=params(),
        cost_estimate=cost(plan.per * nx * ny * ny, 2 * plan.per * nx * ny),
        name="last_y_inverse",
    )(place, jnp.asarray(table), slope)


def last_x_inverse(plan, place, blocks):
    x, y, nx, gx = plan.x, plan.y, plan.nx, plan.gx
    tables = x_tables(nx, True)

    def kernel(place_ref, *refs):
        table_refs, ins, out = refs[:4], refs[4:-1], refs[-1]
        me = place_ref[1]
        found = side_by_side(x_inverse, [ref[...] for ref in table_refs], [ref[0] for ref in ins])
        for s, value in enumerate(found):
            out[:, source(me, s, plan.gy), 0] = value.reshape(gx, x, y)

    return pl.pallas_call(
        kernel,
        grid=(plan.per,),
        in_specs=[scalars()]
        + [whole_block(table.shape) for table in tables]
        + [pl.BlockSpec((1, nx, y), lambda i: (i, 0, 0))] * plan.gy,
        out_specs=pl.BlockSpec((gx, plan.gy, 1, x, y), lambda i: (0, 0, i, 0, 0)),
        out_shape=jax.ShapeDtypeStruct((gx, plan.gy, plan.per, x, y), jnp.float32),
        compiler_params=params(),
        cost_estimate=cost(plan.per * plan.ny * nx * nx, 2 * plan.per * plan.ny * nx),
        name="last_x_inverse",
    )(place, *[jnp.asarray(table) for table in tables], *blocks)


def pair_y_inverse(plan, place, planes, behind):
    x, y, ny = plan.x, plan.y, plan.ny
    count = planes.shape[0]
    table = halves(np.stack(np.split(inverse_basis(ny), plan.gy, axis=1)))
    deep = fit(count, Y_DEEP)
    rows = deep * x
    half = ny // 2

    def kernel(place_ref, table_ref, in_ref, _, *outs):
        plain = in_ref[...].reshape(rows, ny)
        wave = lax.broadcasted_iota(jnp.int32, (1, half), 1).astype(jnp.float32)
        along = jnp.concatenate([wave * plain[:, half:], -wave * plain[:, :half]], axis=1)
        found = pieces_of_y(plan, table_ref, place_ref[1], [along, plain])
        for comp, pieces in enumerate(found):
            for out, piece in zip(outs[:-1], pieces):
                out[comp] = piece.reshape(deep, x, y)

    return pl.pallas_call(
        kernel,
        grid=(count // deep,),
        in_specs=[
            scalars(),
            whole_block(table.shape),
            pl.BlockSpec((deep, x, ny), lambda i: (i, 0, 0)),
            unread(),
        ],
        out_specs=[pl.BlockSpec((2, deep, x, y), lambda i: (0, i, 0, 0))] * plan.gy + [unread()],
        out_shape=[jax.ShapeDtypeStruct((2, count, x, y), jnp.float32)] * plan.gy
        + [jax.ShapeDtypeStruct(behind.shape, behind.dtype)],
        input_output_aliases={3: plan.gy},
        compiler_params=params(),
        cost_estimate=cost(2 * count * x * ny * ny, 3 * count * x * ny),
        name="pair_y_inverse",
    )(place, jnp.asarray(table), planes, behind)


def image_part(plan, place, comps, tables, blocks, fields, before, weight):
    x, y, z = plan.x, plan.y, plan.z
    outs = len(blocks)
    rows = z // outs
    table = np.stack([halves(table) for table in tables]).reshape(len(comps), 2, outs, rows, z)
    group = fit(x, LINE_GROUP)
    deep = fit(group, 2)

    def kernel(place_ref, table_ref, *refs):
        refs = list(refs)
        inputs = [[refs.pop(0) for _ in comps] for _ in range(3)]
        started = [refs.pop(0) for _ in before]
        *ins, image_p, image_s = refs
        ins = [ref.reshape(len(comps), rows * group, y) for ref in ins]
        order = [source(place_ref[1], s, outs) if outs > 1 else 0 for s in range(outs)]
        turned_tables = []
        for comp in range(len(comps)):
            parts = [joined([table_ref[comp, i, g] for g in order], 0) for i in range(2)]
            high, low = (part.astype(jnp.float32).T.astype(jnp.bfloat16) for part in parts)
            turned_tables.append((jnp.concatenate([high, high], axis=1), low))
        for plane in range(0, group, deep):
            here = slice(plane, plane + deep)
            total_p, total_s = (ref[here] for ref in started) if before else (0.0, 0.0)
            for comp, table in enumerate(turned_tables):
                v_ref, p_ref, s_ref = (each[comp] for each in inputs)
                columns = []
                for k in range(deep):
                    cut = pl.ds(plane + k, rows, stride=group)
                    columns.append(joined([ref[comp, cut, :] for ref in ins], 0))
                field = left_times(table, joined(columns, 1)).T.reshape(deep, y, z)
                total_p += p_ref[0, here].astype(jnp.float32) * field
                total_s += s_ref[0, here].astype(jnp.float32) * (v_ref[0, here] - field)
            image_p[here] = total_p
            image_s[here] = total_s

    def block(comp):
        return pl.BlockSpec((1, group, y, z), lambda i: (comp, i, 0, 0))

    blocks = [part.reshape(len(comps), rows, x, y) for part in blocks]
    image = pl.BlockSpec((group, y, z), lambda i: (i, 0, 0))
    return pl.pallas_call(
        kernel,
        grid=(x // group,),
        in_specs=[scalars(), whole_block(table.shape)]
        + [block(comp) for _ in fields for comp in comps]
        + [image] * len(before)
        + [pl.BlockSpec((len(comps), rows, group, y), lambda i: (0, 0, i, 0))] * outs,
        out_specs=[image, image],
        out_shape=[jax.ShapeDtypeStruct((x, y, z), jnp.float32)] * 2,
        compiler_params=params(),
        cost_estimate=cost(
            weight * len(comps) * x * y * z * z, weight * (2 + 3 * len(comps)) * x * y * z
        ),
        name="image_part",
    )(
        place,
        jnp.asarray(table),
        *[field for field in fields for _ in comps],
        *before,
        *blocks,
    )


def over_gx(blocks):
    return lax.all_to_all(blocks, "gx", 0, 0, tiled=True)


def separated(plan, place, velocity, source_p, source_s):
    x, y, z, gx, gy, per = plan.x, plan.y, plan.z, plan.gx, plan.gy, plan.per
    plain = basis(z)
    pair = along_z(plan, place, velocity, (1, 2), (plain, turned(plain)), gy)
    (first,) = along_z(plan, place, velocity, (0,), (crossed(plain, plan),), 1, pair[:1])
    first = over_gx(first.reshape(gx, gy, per, x, y))
    pair = pair_y_forward(plan, place, swap_gy(pair))
    pair = over_gx(pair.reshape(gx, per, x, plan.ny))
    first = first_y_forward(plan, place, swap_gy(first_x_forward(plan, place, first)))
    lines, slope = potential(plan, place, first, pair)
    pair = over_gx(lines)
    last = last_x_inverse(plan, place, swap_gy(last_y_inverse(plan, place, slope)))
    *pair, last = pair_y_inverse(plan, place, pair.reshape(gx * per, x, plan.ny), last)
    pair = swap_gy(pair)
    last = over_gx(last)
    back = inverse_basis(z)
    fields = (velocity, source_p, source_s)
    found = image_part(plan, place, (1, 2), (back, -turned(back)), pair, fields, (), WEIGHT)
    return image_part(plan, place, (0,), (crossed(back, plan),), [last], fields, found, 1)


def shards(velocity, stress, lame_lambda, shear_modulus, buoyancy, source_p, source_s):
    velocity = propagate(velocity, stress, lame_lambda, shear_modulus, buoyancy)
    plan = Plan(velocity.shape[1:])
    place = jnp.stack([lax.axis_index("gx"), lax.axis_index("gy")]).astype(jnp.int32)
    if plan.z % (plan.gx * plan.gy) == 0:
        return tuple(separated(plan, place, velocity, source_p, source_s))
    blocks = z_forward(plan, place, velocity)
    lines = [to_lines(plan, y_forward(plan, place, swap_gy(group))) for group in blocks]
    lines = [x_lines(plan, place, part, chunk) for chunk, part in enumerate(lines)]
    blocks = [swap_gy(y_inverse(plan, place, to_planes(plan, part))) for part in lines]
    return tuple(images(plan, place, blocks, velocity, source_p, source_s))


def solution(mesh):
    in_specs = (
        P(None, "gx", "gy", None),
        P(None, "gx", "gy", None),
        P("gx", "gy", None),
        P("gx", "gy", None),
        P("gx", "gy", None),
        P(None, "gx", "gy", None),
        P(None, "gx", "gy", None),
    )
    out_specs = (P("gx", "gy", None), P("gx", "gy", None))
    return jax.shard_map(shards, mesh=mesh, in_specs=in_specs, out_specs=out_specs, check_vma=False)
```

```python
import numpy as np
import ml_dtypes
import jax
import jax.numpy as jnp
from jax import lax
from jax.experimental import pallas as pl
from jax.experimental.pallas import tpu as pltpu
from jax.sharding import PartitionSpec as P

STEPS = 2
MOST_CHUNKS = 1
VMEM_BYTES = 63 * 2**20
STENCIL_BYTES = 22 * 2**20
Y_DEEP = 32
Z_GROUP = 16
X_GROUP = 4
LINE_GROUP = 16
Y_TILE = 32
WEIGHT = 1000

time_step = 0.2


def passed_along(block, axis, distance):
    devices = range(lax.axis_size(axis))
    route = [(i - distance, i) for i in devices if i - distance in devices]
    return lax.ppermute(block, axis, route)


EDGE_ROWS = 8


def with_edges(place, rims, x_last, x_first):
    high, low = rims[-1], rims[0]
    count, z = high.shape[1:]
    some = fit(count, 8)
    lone = len(rims) == 1

    def kernel(place_ref, high_ref, low_ref, _, __, last_ref, first_ref):
        row = lax.broadcasted_iota(jnp.int32, (EDGE_ROWS, z), 0)
        me = place_ref[1]
        keep_high, keep_low = (me == 0, me == 1) if lone else (True, True)
        above = jnp.where(keep_high, high_ref[0, some - 1 :], 0.0)
        below = jnp.where(keep_low, low_ref[0, :1], 0.0)
        last_ref[...] = jnp.where(row == 0, above, 0.0)
        first_ref[...] = jnp.where(row == 0, below, 0.0)

    return pl.pallas_call(
        kernel,
        grid=(1,),
        in_specs=[
            scalars(),
            pl.BlockSpec((1, some, z), lambda i: (0, count // some - 1, 0)),
            pl.BlockSpec((1, some, z), lambda i: (1, 0, 0)),
            unread(),
            unread(),
        ],
        out_specs=[pl.BlockSpec((EDGE_ROWS, z), lambda i: (0, 0))] * 2,
        out_shape=[jax.ShapeDtypeStruct(edge.shape, jnp.float32) for edge in (x_last, x_first)],
        input_output_aliases={3: 0, 4: 1},
        compiler_params=params(4 * 2**20),
        name="with_edges",
    )(place, high, low, x_last, x_first)


def exchange(place, x_last, x_first, *y_outs):
    if len(y_outs) == 1:
        rims = (lax.ppermute(y_outs[0], "gy", [(0, 1), (1, 0)]),)
    else:
        rims = (passed_along(y_outs[0], "gy", 1), passed_along(y_outs[1], "gy", -1))
    x_last, x_first = with_edges(place, rims, x_last, x_first)
    return rims, (passed_along(x_last, "gx", 1), passed_along(x_first, "gx", -1))


def first_rims(brick, place, velocity, stress, lame, shear):
    x, y, z = brick
    some = fit(y, 8)
    many = fit(y, 16)
    swapped = lax.axis_size("gy") == 2

    def kernel(place_ref, *refs):
        (v_first, v_last, s_first, s_last, lame_first, shear_first, shear_last) = refs[:7]
        (v_low, v_high, s_low, s_high, lame_low, shear_low, shear_high) = refs[7:14]
        x_last, x_first, *y_outs = refs[14:]

        def wide(value):
            return value.astype(jnp.float32)

        lasts = [v_last[0, 0], v_last[1, 0], v_last[2, 0], s_last[3, 0], s_last[4, 0]]
        firsts = [v_first[0, 0], v_first[1, 0], v_first[2, 0], s_first[0, 0]]
        lasts += [wide(shear_last[0])]
        firsts += [wide(lame_first[0]), wide(shear_first[0])]
        for ref, values in ((x_last, lasts), (x_first, firsts)):
            ref[:EDGE_ROWS] = jnp.zeros((EDGE_ROWS, z), jnp.float32)
            for i, value in enumerate(values):
                ref[EDGE_ROWS + i * y : EDGE_ROWS + (i + 1) * y] = value
        lasts = [v_high[i, :, some - 1] for i in range(3)]
        firsts = [v_low[i, :, 0] for i in range(3)]
        lasts += [s_high[3, :, some - 1], s_high[5, :, some - 1], wide(shear_high[...])[:, many - 1]]
        firsts += [s_low[1, :, 0], wide(lame_low[...])[:, 0], wide(shear_low[...])[:, 0]]
        for i, (low, high) in enumerate(zip(lasts, firsts)):
            if swapped:
                y_outs[0][i] = jnp.where(place_ref[1] == 0, low, high)
            else:
                y_outs[0][i], y_outs[1][i] = low, high

    def plane(count, at):
        return pl.BlockSpec((count, 1, y, z), lambda i: (0, at, 0, 0))

    def medium_plane(at):
        return pl.BlockSpec((1, y, z), lambda i: (at, 0, 0))

    def rows(count, at):
        return pl.BlockSpec((count, x, some, z), lambda i: (0, 0, at, 0))

    def medium_rows(at):
        return pl.BlockSpec((x, many, z), lambda i: (0, at, 0))

    shapes = [(EDGE_ROWS + 6 * y, z)] * 2 + [(6, x, z)] * (1 if swapped else 2)
    ends, highs, most = x - 1, y // some - 1, y // many - 1
    return pl.pallas_call(
        kernel,
        grid=(1,),
        in_specs=[scalars(), plane(3, 0), plane(3, ends), plane(6, 0), plane(6, ends)]
        + [medium_plane(0), medium_plane(0), medium_plane(ends)]
        + [rows(3, 0), rows(3, highs), rows(6, 0), rows(6, highs)]
        + [medium_rows(0), medium_rows(0), medium_rows(most)],
        out_specs=[whole_block(shape) for shape in shapes],
        out_shape=[jax.ShapeDtypeStruct(shape, jnp.float32) for shape in shapes],
        compiler_params=params(),
        cost_estimate=pl.CostEstimate(
            flops=0, bytes_accessed=80 * (y + 8 * x) * z, transcendentals=0
        ),
        name="first_rims",
    )(
        place,
        *(velocity, velocity, stress, stress, lame, shear, shear),
        *(velocity, velocity, stress, stress, lame, shear, shear),
    )


def stencil(brick, place, state, rims, medium, x_rims, x_medium, done, last):
    x, y, z = brick
    velocity, stress, lame, shear, buoyancy = state
    group = fit(x, X_GROUP)
    groups = x // group
    tall = fit(y, Y_TILE)
    ends = x_rims is not None
    if ends:
        count, of = min(groups, 2), lambda i: i * (groups - 1)
    else:
        count, of = groups - 2, lambda i: i + 1
    f32 = jnp.float32
    swapped = len(rims) == 1

    def kernel(place_ref, *refs):
        refs = list(refs)
        me = place_ref[1]

        def take(number):
            taken = refs[:number]
            del refs[:number]
            return taken

        v_ref, s_ref, lame_ref, shear_ref, buoy_ref = take(5)
        v_next_ref, xx_next_ref, lame_next_ref, shear_next_ref = take(4)
        v_prior_ref, xy_prior_ref, xz_prior_ref, shear_prior_ref = take(4)
        y_rims = take(len(rims))
        y_medium = take(len(rims)) if medium else y_rims
        if ends:
            xl, xr = take(2)
            xl_medium, xr_medium = take(2) if medium else (xl, xr)
        given = take(len(done))
        new = take(1)[0]
        if not last:
            s_out = take(1)[0]
            y_outs = take(len(rims))
            if ends:
                x_last, x_first = take(2)
        carried, xx_after = take(2)
        s_new = take(1)[0] if last else s_out
        turn = pl.program_id(0)
        here_group = of(turn)
        at = here_group * group
        start, end = here_group == 0, here_group == groups - 1
        row = lax.broadcasted_iota(jnp.int32, (y, z), 0)
        lane = lax.broadcasted_iota(jnp.int32, (y, z), 1)

        def next_z(field):
            edge = lane[: field.shape[0]] == z - 1
            return jnp.where(edge, 0.0, pltpu.roll(field, z - 1, 1))

        def prior_z(field):
            edge = lane[: field.shape[0]] == 0
            return jnp.where(edge, 0.0, pltpu.roll(field, 1, 1))

        def next_y(field, rim):
            rows = field.shape[0]
            return jnp.where(row[:rows] == rows - 1, rim, pltpu.roll(field, rows - 1, 0))

        def prior_y(field, rim):
            return jnp.where(row[: field.shape[0]] == 0, rim, pltpu.roll(field, 1, 0))

        def wide(value):
            return value.astype(f32)

        def low(which, at, refs=y_rims):
            value = refs[0][which, pl.ds(at, 1), :]
            return jnp.where(me == 1, value, 0.0) if swapped else value

        def high(which, at, refs=y_rims):
            value = refs[-1][which, pl.ds(at, 1), :]
            return jnp.where(me == 0, value, 0.0) if swapped else value

        def low_after(at):
            if not ends:
                return low(1, at)
            return jnp.where(at == x, xr[:1], low(1, jnp.minimum(at, x - 1)))

        def high_before(at):
            if not ends:
                return high(0, at)
            return jnp.where(at < 0, xl[:1], high(0, jnp.maximum(at, 0)))

        def rows_of(ref, i, span=slice(0, y)):
            start = EDGE_ROWS + i * y
            return ref[start + span.start : start + span.stop]

        def begin(value, rim):
            return jnp.where(start, rim(), value) if ends else value

        def finish(value, rim):
            return jnp.where(end, rim(), value) if ends else value

        def fresh():
            shear_rim = begin(wide(shear_prior_ref[0]), lambda: rows_of(xl_medium, 5))
            vx, vy, vz = (begin(v_prior_ref[i, 0], lambda: rows_of(xl, i)) for i in range(3))
            xy = begin(xy_prior_ref[0, 0], lambda: rows_of(xl, 3))
            xz = begin(xz_prior_ref[0, 0], lambda: rows_of(xl, 4))
            pull = time_step * shear_rim
            carried[0] = vx
            carried[1] = xy + pull * ((next_y(vx, high_before(at - 1)) - vx) + (v_ref[1, 0] - vy))
            carried[2] = xz + pull * ((next_z(vx) - vx) + (v_ref[2, 0] - vz))

        if ends:
            fresh()
        else:
            pl.when(turn == 0)(fresh)
        if not last and done:

            @pl.when(turn == 0)
            def _():
                for out, value in zip(y_outs, given[2:]):
                    out[...] = value[...]

        def after(i, rows):
            return finish(v_next_ref[i, 0, rows], lambda: rows_of(xr, i, rows))

        spans = [slice(top, top + tall) for top in range(0, y, tall)]

        def row_before(span, field, rim):
            return rim() if span.start == 0 else field[span.start - 1 : span.start]

        def row_after(span, field, rim):
            return rim() if span.stop == y else field[span.stop : span.stop + 1]

        for k in range(group):
            here = at + k
            v_here = [v_ref.at[i, k] for i in range(3)]
            for span in spans:
                vx, vy, vz = (field[span] for field in v_here)
                vx_prior = carried[0, span] if k == 0 else v_ref[0, k - 1, span]
                vy_next = after(1, span) if k == group - 1 else v_ref[1, k + 1, span]
                vz_next = after(2, span) if k == group - 1 else v_ref[2, k + 1, span]
                vy_rim = row_before(span, v_here[1], lambda: low(1, here))
                vx_rim = row_after(span, v_here[0], lambda: high(0, here))
                vz_rim = row_after(span, v_here[2], lambda: high(2, here))
                lame_value, shear_value = wide(lame_ref[k, span]), wide(shear_ref[k, span])
                ex = vx - vx_prior
                ey = vy - prior_y(vy, vy_rim)
                ez = vz - prior_z(vz)
                swell = lame_value * (ex + ey + ez)
                double = 2.0 * shear_value
                pull = time_step * shear_value
                found = (
                    s_ref[0, k, span] + time_step * (swell + double * ex),
                    s_ref[1, k, span] + time_step * (swell + double * ey),
                    s_ref[2, k, span] + time_step * (swell + double * ez),
                    s_ref[3, k, span] + pull * ((next_y(vx, vx_rim) - vx) + (vy_next - vy)),
                    s_ref[4, k, span] + pull * ((next_z(vx) - vx) + (vz_next - vz)),
                    s_ref[5, k, span] + pull * ((next_z(vy) - vy) + (next_y(vz, vz_rim) - vz)),
                )
                for i, value in enumerate(found):
                    s_new[i, k, span] = value

        for span in spans:
            vx, vy, vz = (after(i, span) for i in range(3))
            vy_rim = (
                low_after(at + group)
                if span.start == 0
                else after(1, slice(span.start - 1, span.start))
            )
            ex = vx - v_ref[0, group - 1, span]
            ey = vy - prior_y(vy, vy_rim)
            ez = vz - prior_z(vz)
            lame_value = finish(wide(lame_next_ref[0, span]), lambda: rows_of(xr_medium, 4, span))
            shear_value = finish(wide(shear_next_ref[0, span]), lambda: rows_of(xr_medium, 5, span))
            xx_after[span] = finish(xx_next_ref[0, 0, span], lambda: rows_of(xr, 3, span)) + time_step * (
                lame_value * (ex + ey + ez) + 2.0 * shear_value * ex
            )

        for k in range(group):
            here = at + k
            v_here = [v_ref.at[i, k] for i in range(3)]
            vx_edge, vy_edge, vz_edge = v_here[0][:1], v_here[1][y - 1 :], v_here[2][:1]
            pull = time_step * low(5, here, y_medium)
            vy_rim, vz_rim = low(1, here), low(2, here)
            xy_rim = low(3, here) + pull * (
                (vx_edge - low(0, here)) + (low_after(here + 1) - vy_rim)
            )
            yz_rim = low(4, here) + pull * ((next_z(vy_rim) - vy_rim) + (vz_edge - vz_rim))
            vx_rim, vz_rim = high(0, here), high(2, here)
            ex = vx_rim - high_before(here - 1)
            ey = high(1, here) - vy_edge
            ez = vz_rim - prior_z(vz_rim)
            yy_rim = high(3, here) + time_step * (
                high(4, here, y_medium) * (ex + ey + ez) + 2.0 * high(5, here, y_medium) * ey
            )
            s_here = [s_new.at[i, k] for i in range(6)]
            for span in spans:
                xx, yy, zz, xy, xz, yz = (field[span] for field in s_here)
                xx_next = xx_after[span] if k == group - 1 else s_new[0, k + 1, span]
                xy_prior = carried[1, span] if k == 0 else s_new[3, k - 1, span]
                xz_prior = carried[2, span] if k == 0 else s_new[4, k - 1, span]
                xy_before = row_before(span, s_here[3], lambda: xy_rim)
                yz_before = row_before(span, s_here[5], lambda: yz_rim)
                yy_after = row_after(span, s_here[1], lambda: yy_rim)
                push = time_step * wide(buoy_ref[k, span])
                new[0, k, span] = v_ref[0, k, span] + push * (
                    (xx_next - xx) + (xy - prior_y(xy, xy_before)) + (xz - prior_z(xz))
                )
                new[1, k, span] = v_ref[1, k, span] + push * (
                    (xy - xy_prior) + (next_y(yy, yy_after) - yy) + (yz - prior_z(yz))
                )
                new[2, k, span] = v_ref[2, k, span] + push * (
                    (xz - xz_prior) + (yz - prior_y(yz, yz_before)) + (next_z(zz) - zz)
                )
            if last:
                continue
            lasts = [new[i, k, y - 1 :] for i in range(3)]
            lasts += [s_new[3, k, y - 1 :], s_new[5, k, y - 1 :]]
            firsts = [new[i, k, :1] for i in range(3)] + [s_new[1, k, :1]] * 2
            for i in range(5):
                spot = pl.ds(here, 1)
                if swapped:
                    y_outs[0][i, spot, :] = jnp.where(me == 0, lasts[i], firsts[i])
                else:
                    y_outs[0][i, spot, :], y_outs[1][i, spot, :] = lasts[i], firsts[i]

        if ends and not last:

            def edge(out, values):
                out[:EDGE_ROWS] = jnp.zeros((EDGE_ROWS, z), f32)
                for i, value in enumerate(values):
                    out[EDGE_ROWS + i * y : EDGE_ROWS + (i + 1) * y] = value

            @pl.when(start)
            def _():
                edge(x_first, [new[0, 0], new[1, 0], new[2, 0], s_new[0, 0]])

            @pl.when(end)
            def _():
                most = group - 1
                values = [new[i, most] for i in range(3)]
                edge(x_last, values + [s_new[3, most], s_new[4, most]])

        if not ends:
            carried[0] = v_ref[0, group - 1]
            carried[1] = s_new[3, group - 1]
            carried[2] = s_new[4, group - 1]

    def next_plane(i):
        return jnp.minimum((of(i) + 1) * group, x - 1)

    def prior_plane(i):
        return jnp.maximum(of(i) * group - 1, 0) if ends else group - 1

    def planes(number):
        return pl.BlockSpec((number, group, y, z), lambda i: (0, of(i), 0, 0))

    def one(number, which, place):
        return pl.BlockSpec((number, 1, y, z), lambda i: (which, place(i), 0, 0))

    def medium_one(place):
        return pl.BlockSpec((1, y, z), lambda i: (place(i), 0, 0))

    medium_block = pl.BlockSpec((group, y, z), lambda i: (of(i), 0, 0))
    args = [place, velocity, stress, lame, shear, buoyancy, velocity, stress, lame, shear]
    args += [velocity, stress, stress, shear, *rims, *medium]
    in_specs = [scalars(), planes(3), planes(6), medium_block, medium_block, medium_block]
    in_specs += [one(3, 0, next_plane), one(1, 0, next_plane)]
    in_specs += [medium_one(next_plane), medium_one(next_plane)]
    in_specs += [one(3, 0, prior_plane), one(1, 3, prior_plane), one(1, 4, prior_plane)]
    in_specs += [medium_one(prior_plane)]
    in_specs += [whole_block(rim.shape) for rim in (*rims, *medium)]
    if ends:
        args += [*x_rims, *x_medium]
        in_specs += [whole_block(rim.shape) for rim in (*x_rims, *x_medium)]
    aliases = {}
    for i, value in enumerate(done):
        if i < 2:
            aliases[len(args)] = i
        in_specs.append(unread() if i < 2 else whole_block(value.shape))
        args.append(value)
    out_shape = [(3, x, y, z)]
    out_specs = [planes(3)]
    if not last:
        out_shape += [(6, x, y, z)] + [(5, x, z)] * len(rims)
        out_specs += [planes(6)]
        if ends:
            out_shape += [(EDGE_ROWS + 5 * y, z), (EDGE_ROWS + 4 * y, z)]
        out_specs += [whole_block(shape) for shape in out_shape[2:]]
    part = (1 if ends else WEIGHT) * count * group * y * z
    return pl.pallas_call(
        kernel,
        grid=(count,),
        in_specs=in_specs,
        out_specs=out_specs,
        out_shape=[jax.ShapeDtypeStruct(shape, f32) for shape in out_shape],
        scratch_shapes=[pltpu.VMEM((3, y, z), f32), pltpu.VMEM((y, z), f32)]
        + ([pltpu.VMEM((6, group, y, z), f32)] if last else []),
        input_output_aliases=aliases,
        compiler_params=params(STENCIL_BYTES),
        cost_estimate=pl.CostEstimate(
            flops=80 * part, bytes_accessed=(54 if last else 78) * part, transcendentals=0
        ),
        name="stencil_ends" if ends else "stencil_middle",
    )(*args)


def propagate(place, velocity, stress, lame, shear, buoyancy):
    brick = velocity.shape[1:]
    between = brick[0] // fit(brick[0], X_GROUP) > 2
    rims, x_rims = exchange(place, *first_rims(brick, place, velocity, stress, lame, shear))
    held, medium, x_medium = (rims, x_rims), (), ()
    for step_index in range(STEPS):
        last = step_index == STEPS - 1
        state = (velocity, stress, lame, shear, buoyancy)
        done = []
        if between:
            done = stencil(brick, place, state, rims, medium, None, None, done, last)
        found = stencil(brick, place, state, rims, medium, x_rims, x_medium, done, last)
        velocity = found[0]
        if not last:
            _, stress, *y_outs, x_last, x_first = found
            rims, x_rims = exchange(place, x_last, x_first, *y_outs)
            medium, x_medium = held
    return velocity


def basis(length):
    half = length // 2
    wave = np.arange(half)
    place = np.arange(length)
    angle = (wave[:, None] * place[None, :] % length) * (2.0 * np.pi / length)
    cosine, sine = np.cos(angle), np.sin(angle)
    sine[0] = 1.0 - 2.0 * (place % 2)
    return np.concatenate([cosine, sine])


def waves_of(length):
    return np.tile(np.arange(length // 2, dtype=np.float64), 2)


def inverse_basis(length):
    weight = np.where(waves_of(length) == 0, 1.0, 2.0) / length
    return basis(length) * weight[:, None]


def turned(table):
    half = table.shape[0] // 2
    return np.concatenate([table[half:], -table[:half]]) * waves_of(table.shape[0])[:, None]


def halves(table):
    high = table.astype(ml_dtypes.bfloat16)
    low = (table - high.astype(np.float64)).astype(ml_dtypes.bfloat16)
    return np.stack([high, low])


def split(value):
    high = value.astype(jnp.bfloat16)
    return high, (value - high.astype(jnp.float32)).astype(jnp.bfloat16)


def dot(left, right, dims=((1,), (0,))):
    return lax.dot_general(left, right, (dims, ((), ())), preferred_element_type=jnp.float32)


def times(left, right):
    return dot(left[0], right[0]) + (dot(left[1], right[0]) + dot(left[0], right[1]))


def joined(pieces, axis):
    return pieces[0] if len(pieces) == 1 else jnp.concatenate(pieces, axis=axis)


def fit(length, most):
    size = min(length, most)
    while length % size:
        size -= 1
    return size


def params(limit=VMEM_BYTES):
    return pltpu.CompilerParams(vmem_limit_bytes=limit)


def whole_block(shape):
    return pl.BlockSpec(shape, lambda *_: (0,) * len(shape))


def scalars():
    return pl.BlockSpec(memory_space=pltpu.SMEM)


class Plan:
    def __init__(self, brick):
        self.x, self.y, self.z = brick
        self.gx, self.gy = lax.axis_size("gx"), lax.axis_size("gy")
        self.nx, self.ny = self.x * self.gx, self.y * self.gy
        chunks = MOST_CHUNKS
        while chunks > 1 and self.z % (chunks * self.gy * self.gx):
            chunks -= 1
        self.chunks = chunks
        self.kz = self.z // (chunks * self.gy)
        self.parts = max(1, self.gx // self.kz)
        self.per = max(1, self.kz // self.gx)
        self.ky = self.ny // self.parts


def source(me, step, count):
    return lax.rem(me - step + count, count)


def z_forward(plan, place, velocity):
    x, y, z, kz = plan.x, plan.y, plan.z, plan.kz
    table = np.stack([halves(basis(z)), halves(turned(basis(z)))])
    table = table.reshape(2, 2, plan.chunks, plan.gy, kz, z)
    count = plan.chunks * plan.gy

    group = fit(x, Z_GROUP)
    deep = fit(group, 2)

    def kernel(place_ref, table_ref, v_ref, *outs):
        at = pl.program_id(0) * group
        me = place_ref[1]
        order = [(c, lax.rem(me + s, plan.gy)) for c in range(plan.chunks) for s in range(plan.gy)]
        tables = []
        for kind in range(2):
            high, low = (joined([table_ref[kind, i, c, g] for c, g in order], 0) for i in range(2))
            tables.append((jnp.concatenate([high, high], axis=1), low))
        for comp in range(3):
            twice, low = tables[1 if comp == 2 else 0]
            for plane in range(0, group, deep):
                field = split(v_ref[comp, plane : plane + deep].reshape(deep * y, z))
                value = dot(twice, jnp.concatenate(field, axis=1), ((1,), (1,)))
                value += dot(low, field[0], ((1,), (1,)))
                for i, out in enumerate(outs):
                    for k in range(deep):
                        part = value[i * kz : (i + 1) * kz, k * y : (k + 1) * y]
                        out[comp, pl.ds(at + plane + k, kz, stride=x), :] = part

    outs = pl.pallas_call(
        kernel,
        grid=(x // group,),
        in_specs=[
            scalars(),
            whole_block(table.shape),
            pl.BlockSpec((3, group, y, z), lambda i: (0, i, 0, 0)),
        ],
        out_specs=[whole_block((3, kz * x, y))] * count,
        out_shape=[jax.ShapeDtypeStruct((3, kz * x, y), jnp.float32)] * count,
        compiler_params=params(),
        cost_estimate=pl.CostEstimate(
            flops=18 * x * y * z * z, bytes_accessed=24 * x * y * z, transcendentals=0
        ),
        name="z_forward",
    )(place, jnp.asarray(table), velocity)
    outs = [out.reshape(3, kz, x, y) for out in outs]
    return [outs[c * plan.gy : (c + 1) * plan.gy] for c in range(plan.chunks)]


def swap_gy(blocks):
    count = len(blocks)
    moved = [blocks[0]]
    for step in range(1, count):
        route = [(i, (i + step) % count) for i in range(count)]
        moved.append(lax.ppermute(blocks[step], "gy", route))
    return moved


def y_forward(plan, place, blocks):
    x, y, ny, kz = plan.x, plan.y, plan.ny, plan.kz
    table = halves(basis(ny).T).reshape(2, plan.gy, y, ny)
    deep = fit(kz, 8)
    rows = deep * x
    half = ny // 2
    aligned = y % 128 == 0

    def kernel(place_ref, table_ref, *refs):
        ins, out = refs[:-1], refs[-1]
        me = place_ref[1]
        groups = [source(me, step, plan.gy) for step in range(plan.gy)]
        tables = [(table_ref[0, g], table_ref[1, g]) for g in groups]
        if aligned:
            tables = [tuple(joined([t[i] for t in tables], 0) for i in range(2))]

        def moved(comp):
            fields = [ref[comp].reshape(rows, y) for ref in ins]
            if aligned:
                fields = [joined(fields, 1)]
            return sum(times(split(f), t) for f, t in zip(fields, tables))

        wave = lax.broadcasted_iota(jnp.int32, (1, half), 1).astype(jnp.float32)
        out[:, 0] = moved(0).reshape(deep, x, ny)
        along, rest = moved(1), moved(2)
        out[:, 1, :, :half] = (rest[:, :half] + wave * along[:, half:]).reshape(deep, x, half)
        out[:, 1, :, half:] = (rest[:, half:] - wave * along[:, :half]).reshape(deep, x, half)

    return pl.pallas_call(
        kernel,
        grid=(kz // deep,),
        in_specs=[scalars(), whole_block(table.shape)]
        + [pl.BlockSpec((3, deep, x, y), lambda i: (0, i, 0, 0))] * plan.gy,
        out_specs=pl.BlockSpec((deep, 2, x, ny), lambda i: (i, 0, 0, 0)),
        out_shape=jax.ShapeDtypeStruct((kz, 2, x, ny), jnp.float32),
        compiler_params=params(),
        cost_estimate=pl.CostEstimate(
            flops=18 * kz * x * ny * ny, bytes_accessed=20 * kz * x * ny, transcendentals=0
        ),
        name="y_forward",
    )(place, jnp.asarray(table), *blocks)


def to_lines(plan, planes):
    if plan.parts > 1:
        planes = planes.reshape(plan.kz, 2, plan.x, plan.parts, plan.ky).transpose(0, 3, 1, 2, 4)
    planes = planes.reshape(plan.gx, plan.per, 2, plan.x, plan.ky)
    return lax.all_to_all(planes, "gx", 0, 0, tiled=True)


def to_planes(plan, lines):
    planes = lax.all_to_all(lines, "gx", 0, 0, tiled=True)
    if plan.parts > 1:
        planes = planes.reshape(plan.kz, plan.parts, 2, plan.x, plan.ky).transpose(0, 2, 3, 1, 4)
    return planes.reshape(plan.kz, 2, plan.x, plan.ny)


def x_lines(plan, place, lines, chunk):
    x, nx, ny, ky, gx = plan.x, plan.nx, plan.ny, plan.ky, plan.gx
    forth = halves(basis(nx))
    back = halves(-inverse_basis(nx).T)
    lanes = 128 if ky % 128 == 0 else ky
    half = nx // 2
    aligned = lanes % 128 == 0

    def kernel(place_ref, forth_ref, back_ref, in_ref, out_ref):
        me_x, me_y = place_ref[0], place_ref[1]
        which, lane = pl.program_id(0), pl.program_id(1)

        def through(table_ref, pair):
            table = (table_ref[0], table_ref[1])
            if aligned:
                both = times(table, split(jnp.concatenate(pair, axis=1)))
                return both[:, :lanes], both[:, lanes:]
            return tuple(times(table, split(value)) for value in pair)

        pair = [in_ref[:, 0, i].reshape(nx, lanes) for i in range(2)]
        along, rest = through(forth_ref, pair)
        wave_x = lax.broadcasted_iota(jnp.int32, (half, lanes), 0).astype(jnp.float32)
        slot_y = lax.broadcasted_iota(jnp.int32, (1, lanes), 1) + (
            lane * lanes + lax.rem(me_x, plan.parts) * ky
        )
        wave_y = lax.rem(slot_y, ny // 2).astype(jnp.float32)
        slot_z = (chunk * plan.gy + me_y) * plan.kz + me_x // plan.parts * plan.per + which
        wave_z = lax.rem(slot_z, plan.z // 2).astype(jnp.float32)
        scale = 1.0 / jnp.maximum(wave_x * wave_x + (wave_y * wave_y + wave_z * wave_z), 1.0)
        cosine = (rest[:half] + wave_x * along[half:]) * scale
        sine = (rest[half:] - wave_x * along[:half]) * scale
        plain = jnp.concatenate([cosine, sine], axis=0)
        slope = jnp.concatenate([wave_x * sine, -wave_x * cosine], axis=0)
        for i, value in enumerate(through(back_ref, [slope, plain])):
            out_ref[:, 0, i] = value.reshape(gx, x, lanes)

    block = pl.BlockSpec((gx, 1, 2, x, lanes), lambda i, j: (0, i, 0, 0, j))
    return pl.pallas_call(
        kernel,
        grid=(plan.per, ky // lanes),
        in_specs=[scalars(), whole_block(forth.shape), whole_block(back.shape), block],
        out_specs=block,
        out_shape=jax.ShapeDtypeStruct(lines.shape, jnp.float32),
        compiler_params=params(),
        cost_estimate=pl.CostEstimate(
            flops=24 * plan.per * ky * nx * nx,
            bytes_accessed=16 * plan.per * ky * nx,
            transcendentals=0,
        ),
        name="x_lines",
    )(place, jnp.asarray(forth), jnp.asarray(back), lines)


def y_inverse(plan, place, planes):
    x, y, ny, kz = plan.x, plan.y, plan.ny, plan.kz
    table = np.stack(np.split(inverse_basis(ny), plan.gy, axis=1))
    table = halves(table)
    deep = fit(kz, 8)
    rows = deep * x
    half = ny // 2
    aligned = y % 128 == 0

    def kernel(place_ref, table_ref, in_ref, *outs):
        me = place_ref[1]
        groups = [lax.rem(me + step, plan.gy) for step in range(plan.gy)]
        tables = [(table_ref[0, g], table_ref[1, g]) for g in groups]
        slope = in_ref[:, 0].reshape(rows, ny)
        plain = in_ref[:, 1].reshape(rows, ny)
        wave = lax.broadcasted_iota(jnp.int32, (1, half), 1).astype(jnp.float32)
        along = jnp.concatenate([wave * plain[:, half:], -wave * plain[:, :half]], axis=1)
        for comp, value in enumerate((slope, along, plain)):
            parts = split(value)
            if aligned:
                table = tuple(joined([t[i] for t in tables], 1) for i in range(2))
                found = times(parts, table)
                pieces = [found[:, s * y : (s + 1) * y] for s in range(plan.gy)]
            else:
                pieces = [times(parts, t) for t in tables]
            for out, piece in zip(outs, pieces):
                out[comp] = piece.reshape(deep, x, y)

    return pl.pallas_call(
        kernel,
        grid=(kz // deep,),
        in_specs=[
            scalars(),
            whole_block(table.shape),
            pl.BlockSpec((deep, 2, x, ny), lambda i: (i, 0, 0, 0)),
        ],
        out_specs=[pl.BlockSpec((3, deep, x, y), lambda i: (0, i, 0, 0))] * plan.gy,
        out_shape=[jax.ShapeDtypeStruct((3, kz, x, y), jnp.float32)] * plan.gy,
        compiler_params=params(),
        cost_estimate=pl.CostEstimate(
            flops=18 * kz * x * ny * ny, bytes_accessed=20 * kz * x * ny, transcendentals=0
        ),
        name="y_inverse",
    )(place, jnp.asarray(table), planes)


def images(plan, place, blocks, velocity, source_p, source_s):
    x, y, z, kz = plan.x, plan.y, plan.z, plan.kz
    table = np.stack([halves(inverse_basis(z)), halves(-turned(inverse_basis(z)))])
    table = table.reshape(2, 2, plan.chunks, plan.gy, kz, z)
    blocks = [block.reshape(3, kz * x, y) for group in blocks for block in group]

    group = fit(x, Z_GROUP)
    deep = fit(group, 2)

    def kernel(place_ref, table_ref, v_ref, p_ref, s_ref, *refs):
        ins, (image_p, image_s) = refs[:-2], refs[-2:]
        at = pl.program_id(0) * group
        me = place_ref[1]
        order = [
            (chunk, source(me, step, plan.gy))
            for chunk in range(plan.chunks)
            for step in range(plan.gy)
        ]
        tables = []
        for kind in range(2):
            high, low = (joined([table_ref[kind, i, c, g] for c, g in order], 0) for i in range(2))
            high, low = (part.astype(jnp.float32).T.astype(jnp.bfloat16) for part in (high, low))
            tables.append((jnp.concatenate([high, high], axis=1), low))
        for plane in range(0, group, deep):
            here = slice(plane, plane + deep)
            total_p = total_s = 0.0
            for comp in range(3):
                twice, low = tables[1 if comp == 2 else 0]
                columns = [
                    joined([ref[comp, pl.ds(at + plane + k, kz, stride=x), :] for ref in ins], 0)
                    for k in range(deep)
                ]
                high, rest = split(joined(columns, 1))
                field = dot(twice, jnp.concatenate([high, rest], axis=0)) + dot(low, high)
                field = field.T.reshape(deep, y, z)
                total_p += p_ref[comp, here].astype(jnp.float32) * field
                total_s += s_ref[comp, here].astype(jnp.float32) * (v_ref[comp, here] - field)
            image_p[here] = total_p
            image_s[here] = total_s

    plane = pl.BlockSpec((3, group, y, z), lambda i: (0, i, 0, 0))
    image = pl.BlockSpec((group, y, z), lambda i: (i, 0, 0))
    return pl.pallas_call(
        kernel,
        grid=(x // group,),
        in_specs=[scalars(), whole_block(table.shape), plane, plane, plane]
        + [whole_block((3, kz * x, y))] * len(blocks),
        out_specs=[image, image],
        out_shape=[jax.ShapeDtypeStruct((x, y, z), jnp.float32)] * 2,
        compiler_params=params(),
        cost_estimate=pl.CostEstimate(
            flops=18 * x * y * z * z, bytes_accessed=44 * x * y * z, transcendentals=0
        ),
        name="images",
    )(place, jnp.asarray(table), velocity, source_p, source_s, *blocks)


def doubled(table, axis):
    high, low = halves(table)
    return np.concatenate([high, high], axis=axis), low


def left_times(table, value):
    high, low = split(value)
    return dot(table[0], jnp.concatenate([high, low], axis=0)) + dot(table[1], high)


def right_times(value, table):
    high, low = split(value)
    return dot(jnp.concatenate([high, low], axis=1), table[0]) + dot(high, table[1])


def odd_basis(length):
    wave = 2 * np.arange(length // 4) + 1
    angle = (wave[:, None] * np.arange(length // 2) % length) * (2.0 * np.pi / length)
    return np.concatenate([np.cos(angle), np.sin(angle)])


def x_tables(length, inverse):
    even, odd = basis(length // 2), odd_basis(length)
    if inverse:
        even, odd = -inverse_basis(length // 2).T / 2.0, -odd.T * (2.0 / length)
    return [*doubled(even, 1), *doubled(odd, 1)]


def x_forward(tables, value):
    half = value.shape[0] // 2
    even = left_times(tables[:2], value[:half] + value[half:])
    return jnp.concatenate([even, left_times(tables[2:], value[:half] - value[half:])], axis=0)


def x_inverse(tables, value):
    half = value.shape[0] // 2
    even = left_times(tables[:2], value[:half])
    odd = left_times(tables[2:], value[half:])
    return jnp.concatenate([even + odd, even - odd], axis=0)


def x_wave(length):
    slot = lax.broadcasted_iota(jnp.int32, (length, 1), 0)
    wave = 2 * lax.rem(slot, length // 4) + slot // (length // 2)
    return wave.astype(jnp.float32)


def slope_x(value):
    part = value.shape[0] // 4
    wave = x_wave(value.shape[0])
    swapped = [value[part : 2 * part], -value[:part], value[3 * part :], -value[2 * part : 3 * part]]
    return wave * jnp.concatenate(swapped, axis=0)


def side_by_side(through, tables, values):
    width = values[0].shape[1]
    if width % 128:
        return [through(tables, value) for value in values]
    both = through(tables, joined(values, 1))
    return [both[:, i * width : (i + 1) * width] for i in range(len(values))]


def cost(flops, values):
    return pl.CostEstimate(flops=6 * flops, bytes_accessed=4 * values, transcendentals=0)


def crossed(table, plan):
    shape = (plan.gy, plan.gx, plan.per, table.shape[-1])
    return table.reshape(shape).transpose(1, 0, 2, 3).reshape(table.shape)


def unread():
    return pl.BlockSpec(memory_space=pl.ANY)


def along_z(plan, place, velocity, comps, tables, outs, ahead=()):
    x, y, z = plan.x, plan.y, plan.z
    table = np.stack([halves(table) for table in tables]).reshape(len(comps), 2, outs, z // outs, z)
    group = fit(x, LINE_GROUP)
    deep = fit(group, 2)
    rows = z // outs

    def kernel(place_ref, table_ref, *refs):
        fields, found = refs[: len(comps)], refs[len(comps) + len(ahead) :]
        found = [out.reshape(len(comps), rows * group, y) for out in found]
        me = place_ref[1]
        order = [lax.rem(me + s, outs) if outs > 1 else 0 for s in range(outs)]
        for comp, field in enumerate(fields):
            high, low = (joined([table_ref[comp, i, g] for g in order], 0) for i in range(2))
            twice = jnp.concatenate([high, high], axis=1)
            for plane in range(0, group, deep):
                parts = split(field[0, plane : plane + deep].reshape(deep * y, z))
                value = dot(twice, jnp.concatenate(parts, axis=1), ((1,), (1,)))
                value += dot(low, parts[0], ((1,), (1,)))
                for i, out in enumerate(found):
                    for k in range(deep):
                        part = value[i * rows : (i + 1) * rows, k * y : (k + 1) * y]
                        out[comp, pl.ds(plane + k, rows, stride=group), :] = part

    def block(comp):
        return pl.BlockSpec((1, group, y, z), lambda i: (comp, i, 0, 0))

    shape = (len(comps), rows, x, y)
    return pl.pallas_call(
        kernel,
        grid=(x // group,),
        in_specs=[scalars(), whole_block(table.shape)]
        + [block(comp) for comp in comps]
        + [unread()] * len(ahead),
        out_specs=[pl.BlockSpec((len(comps), rows, group, y), lambda i: (0, 0, i, 0))] * outs,
        out_shape=[jax.ShapeDtypeStruct(shape, jnp.float32)] * outs,
        compiler_params=params(STENCIL_BYTES),
        cost_estimate=cost(len(comps) * x * y * z * z, 2 * len(comps) * x * y * z),
        name="along_z",
    )(place, jnp.asarray(table), *[velocity] * len(comps), *ahead)


def y_table(plan, table_ref, groups):
    tables = [(table_ref[0, g], table_ref[1, g]) for g in groups]
    if plan.y % 128 == 0:
        high, low = (joined([table[i] for table in tables], 0) for i in range(2))
        return [(jnp.concatenate([high, high], axis=0), low)]
    return [(jnp.concatenate([high, high], axis=0), low) for high, low in tables]


def over_y(fields, tables):
    if len(tables) == 1:
        fields = [joined(fields, 1)]
    return sum(right_times(field, table) for field, table in zip(fields, tables))


def pair_y_forward(plan, place, blocks):
    x, y, ny = plan.x, plan.y, plan.ny
    count = blocks[0].shape[1]
    table = halves(basis(ny).T).reshape(2, plan.gy, y, ny)
    deep = fit(count, Y_DEEP)
    rows = deep * x
    half = ny // 2

    def kernel(place_ref, table_ref, *refs):
        ins, out = refs[:-1], refs[-1]
        me = place_ref[1]
        tables = y_table(plan, table_ref, [source(me, s, plan.gy) for s in range(plan.gy)])
        along, rest = (
            over_y([ref[comp].reshape(rows, y) for ref in ins], tables) for comp in range(2)
        )
        wave = lax.broadcasted_iota(jnp.int32, (1, half), 1).astype(jnp.float32)
        out[:, :, :half] = (rest[:, :half] + wave * along[:, half:]).reshape(deep, x, half)
        out[:, :, half:] = (rest[:, half:] - wave * along[:, :half]).reshape(deep, x, half)

    return pl.pallas_call(
        kernel,
        grid=(count // deep,),
        in_specs=[scalars(), whole_block(table.shape)]
        + [pl.BlockSpec((2, deep, x, y), lambda i: (0, i, 0, 0))] * plan.gy,
        out_specs=pl.BlockSpec((deep, x, ny), lambda i: (i, 0, 0)),
        out_shape=jax.ShapeDtypeStruct((count, x, ny), jnp.float32),
        compiler_params=params(),
        cost_estimate=cost(2 * WEIGHT * count * x * ny * ny, 3 * WEIGHT * count * x * ny),
        name="pair_y_forward",
    )(place, jnp.asarray(table), *blocks)


def first_x_forward(plan, place, lines):
    x, y, nx = plan.x, plan.y, plan.nx
    tables = x_tables(nx, False)

    def kernel(place_ref, *refs):
        table_refs, in_ref, outs = refs[:4], refs[4], refs[5:]
        me = place_ref[1]
        fields = [in_ref[:, lax.rem(me + s, plan.gy), 0].reshape(nx, y) for s in range(plan.gy)]
        found = side_by_side(x_forward, [ref[...] for ref in table_refs], fields)
        for out, value in zip(outs, found):
            out[0] = value

    return pl.pallas_call(
        kernel,
        grid=(plan.per,),
        in_specs=[scalars()]
        + [whole_block(table.shape) for table in tables]
        + [pl.BlockSpec((plan.gx, plan.gy, 1, x, y), lambda i: (0, 0, i, 0, 0))],
        out_specs=[pl.BlockSpec((1, nx, y), lambda i: (i, 0, 0))] * plan.gy,
        out_shape=[jax.ShapeDtypeStruct((plan.per, nx, y), jnp.float32)] * plan.gy,
        compiler_params=params(),
        cost_estimate=cost(plan.per * plan.ny * nx * nx, 2 * plan.per * plan.ny * nx),
        name="first_x_forward",
    )(place, *[jnp.asarray(table) for table in tables], lines)


def first_y_forward(plan, place, blocks):
    y, nx, ny = plan.y, plan.nx, plan.ny
    table = halves(basis(ny).T).reshape(2, plan.gy, y, ny)

    def kernel(place_ref, table_ref, *refs):
        ins, out = refs[:-1], refs[-1]
        me = place_ref[1]
        tables = y_table(plan, table_ref, [source(me, s, plan.gy) for s in range(plan.gy)])
        out[0] = slope_x(over_y([ref[0] for ref in ins], tables))

    return pl.pallas_call(
        kernel,
        grid=(plan.per,),
        in_specs=[scalars(), whole_block(table.shape)]
        + [pl.BlockSpec((1, nx, y), lambda i: (i, 0, 0))] * plan.gy,
        out_specs=pl.BlockSpec((1, nx, ny), lambda i: (i, 0, 0)),
        out_shape=jax.ShapeDtypeStruct((plan.per, nx, ny), jnp.float32),
        compiler_params=params(),
        cost_estimate=cost(plan.per * nx * ny * ny, 2 * plan.per * nx * ny),
        name="first_y_forward",
    )(place, jnp.asarray(table), *blocks)


def potential(plan, place, first, lines):
    x, nx, ny, gx = plan.x, plan.nx, plan.ny, plan.gx
    tables = x_tables(nx, False) + x_tables(nx, True)

    def kernel(place_ref, *refs):
        first_ref, in_ref, out_ref, slope_ref = refs[8:]
        forth, back = ([ref[...] for ref in refs[i : i + 4]] for i in (0, 4))
        me_x, me_y = place_ref[0], place_ref[1]
        total = x_forward(forth, in_ref[:, 0].reshape(nx, ny)) + first_ref[0]
        wave_x = x_wave(nx)
        slot_y = lax.broadcasted_iota(jnp.int32, (1, ny), 1)
        wave_y = lax.rem(slot_y, ny // 2).astype(jnp.float32)
        slot_z = (me_y * gx + me_x) * plan.per + pl.program_id(0)
        wave_z = lax.rem(slot_z, plan.z // 2).astype(jnp.float32)
        square = wave_x * wave_x + (wave_y * wave_y + wave_z * wave_z)
        found = total / jnp.maximum(square, 1.0)
        out_ref[:, 0] = x_inverse(back, found).reshape(gx, x, ny)
        slope_ref[0] = slope_x(found)

    spectrum = pl.BlockSpec((1, nx, ny), lambda i: (i, 0, 0))
    block = pl.BlockSpec((gx, 1, x, ny), lambda i: (0, i, 0, 0))
    return pl.pallas_call(
        kernel,
        grid=(plan.per,),
        in_specs=[scalars()] + [whole_block(t.shape) for t in tables] + [spectrum, block],
        out_specs=[block, spectrum],
        out_shape=[
            jax.ShapeDtypeStruct(lines.shape, jnp.float32),
            jax.ShapeDtypeStruct((plan.per, nx, ny), jnp.float32),
        ],
        compiler_params=params(),
        cost_estimate=cost(2 * plan.per * ny * nx * nx, 4 * plan.per * ny * nx),
        name="potential",
    )(place, *[jnp.asarray(t) for t in tables], first, lines)


def pieces_of_y(plan, table_ref, me, values):
    groups = [lax.rem(me + s, plan.gy) for s in range(plan.gy)]
    y = plan.y
    tables = [(table_ref[0, g], table_ref[1, g]) for g in groups]
    if y % 128 == 0:
        tables = [tuple(joined([table[i] for table in tables], 1) for i in range(2))]
    tables = [(jnp.concatenate([high, high], axis=0), low) for high, low in tables]
    found = []
    for value in values:
        pieces = [right_times(value, table) for table in tables]
        if y % 128 == 0:
            pieces = [pieces[0][:, s * y : (s + 1) * y] for s in range(plan.gy)]
        found.append(pieces)
    return found


def last_y_inverse(plan, place, slope):
    y, nx, ny = plan.y, plan.nx, plan.ny
    table = halves(np.stack(np.split(inverse_basis(ny), plan.gy, axis=1)))

    def kernel(place_ref, table_ref, in_ref, *outs):
        (pieces,) = pieces_of_y(plan, table_ref, place_ref[1], [in_ref[0]])
        for out, piece in zip(outs, pieces):
            out[0] = piece

    return pl.pallas_call(
        kernel,
        grid=(plan.per,),
        in_specs=[
            scalars(),
            whole_block(table.shape),
            pl.BlockSpec((1, nx, ny), lambda i: (i, 0, 0)),
        ],
        out_specs=[pl.BlockSpec((1, nx, y), lambda i: (i, 0, 0))] * plan.gy,
        out_shape=[jax.ShapeDtypeStruct((plan.per, nx, y), jnp.float32)] * plan.gy,
        compiler_params=params(),
        cost_estimate=cost(plan.per * nx * ny * ny, 2 * plan.per * nx * ny),
        name="last_y_inverse",
    )(place, jnp.asarray(table), slope)


def last_x_inverse(plan, place, blocks):
    x, y, nx, gx = plan.x, plan.y, plan.nx, plan.gx
    tables = x_tables(nx, True)

    def kernel(place_ref, *refs):
        table_refs, ins, out = refs[:4], refs[4:-1], refs[-1]
        me = place_ref[1]
        found = side_by_side(x_inverse, [ref[...] for ref in table_refs], [ref[0] for ref in ins])
        for s, value in enumerate(found):
            out[:, source(me, s, plan.gy), 0] = value.reshape(gx, x, y)

    return pl.pallas_call(
        kernel,
        grid=(plan.per,),
        in_specs=[scalars()]
        + [whole_block(table.shape) for table in tables]
        + [pl.BlockSpec((1, nx, y), lambda i: (i, 0, 0))] * plan.gy,
        out_specs=pl.BlockSpec((gx, plan.gy, 1, x, y), lambda i: (0, 0, i, 0, 0)),
        out_shape=jax.ShapeDtypeStruct((gx, plan.gy, plan.per, x, y), jnp.float32),
        compiler_params=params(),
        cost_estimate=cost(plan.per * plan.ny * nx * nx, 2 * plan.per * plan.ny * nx),
        name="last_x_inverse",
    )(place, *[jnp.asarray(table) for table in tables], *blocks)


def pair_y_inverse(plan, place, planes, behind):
    x, y, ny = plan.x, plan.y, plan.ny
    count = planes.shape[0]
    table = halves(np.stack(np.split(inverse_basis(ny), plan.gy, axis=1)))
    deep = fit(count, Y_DEEP)
    rows = deep * x
    half = ny // 2

    def kernel(place_ref, table_ref, in_ref, _, *outs):
        plain = in_ref[...].reshape(rows, ny)
        wave = lax.broadcasted_iota(jnp.int32, (1, half), 1).astype(jnp.float32)
        along = jnp.concatenate([wave * plain[:, half:], -wave * plain[:, :half]], axis=1)
        found = pieces_of_y(plan, table_ref, place_ref[1], [along, plain])
        for comp, pieces in enumerate(found):
            for out, piece in zip(outs[:-1], pieces):
                out[comp] = piece.reshape(deep, x, y)

    return pl.pallas_call(
        kernel,
        grid=(count // deep,),
        in_specs=[
            scalars(),
            whole_block(table.shape),
            pl.BlockSpec((deep, x, ny), lambda i: (i, 0, 0)),
            unread(),
        ],
        out_specs=[pl.BlockSpec((2, deep, x, y), lambda i: (0, i, 0, 0))] * plan.gy + [unread()],
        out_shape=[jax.ShapeDtypeStruct((2, count, x, y), jnp.float32)] * plan.gy
        + [jax.ShapeDtypeStruct(behind.shape, behind.dtype)],
        input_output_aliases={3: plan.gy},
        compiler_params=params(),
        cost_estimate=cost(2 * count * x * ny * ny, 3 * count * x * ny),
        name="pair_y_inverse",
    )(place, jnp.asarray(table), planes, behind)


def image_part(plan, place, comps, tables, blocks, fields, before, weight):
    x, y, z = plan.x, plan.y, plan.z
    outs = len(blocks)
    rows = z // outs
    table = np.stack([halves(table) for table in tables]).reshape(len(comps), 2, outs, rows, z)
    group = fit(x, LINE_GROUP)
    deep = fit(group, 2)

    def kernel(place_ref, table_ref, *refs):
        refs = list(refs)
        inputs = [[refs.pop(0) for _ in comps] for _ in range(3)]
        started = [refs.pop(0) for _ in before]
        *ins, image_p, image_s = refs
        ins = [ref.reshape(len(comps), rows * group, y) for ref in ins]
        order = [source(place_ref[1], s, outs) if outs > 1 else 0 for s in range(outs)]
        turned_tables = []
        for comp in range(len(comps)):
            parts = [joined([table_ref[comp, i, g] for g in order], 0) for i in range(2)]
            high, low = (part.astype(jnp.float32).T.astype(jnp.bfloat16) for part in parts)
            turned_tables.append((jnp.concatenate([high, high], axis=1), low))
        for plane in range(0, group, deep):
            here = slice(plane, plane + deep)
            total_p, total_s = (ref[here] for ref in started) if before else (0.0, 0.0)
            for comp, table in enumerate(turned_tables):
                v_ref, p_ref, s_ref = (each[comp] for each in inputs)
                columns = []
                for k in range(deep):
                    cut = pl.ds(plane + k, rows, stride=group)
                    columns.append(joined([ref[comp, cut, :] for ref in ins], 0))
                field = left_times(table, joined(columns, 1)).T.reshape(deep, y, z)
                total_p += p_ref[0, here].astype(jnp.float32) * field
                total_s += s_ref[0, here].astype(jnp.float32) * (v_ref[0, here] - field)
            image_p[here] = total_p
            image_s[here] = total_s

    def block(comp):
        return pl.BlockSpec((1, group, y, z), lambda i: (comp, i, 0, 0))

    blocks = [part.reshape(len(comps), rows, x, y) for part in blocks]
    image = pl.BlockSpec((group, y, z), lambda i: (i, 0, 0))
    return pl.pallas_call(
        kernel,
        grid=(x // group,),
        in_specs=[scalars(), whole_block(table.shape)]
        + [block(comp) for _ in fields for comp in comps]
        + [image] * len(before)
        + [pl.BlockSpec((len(comps), rows, group, y), lambda i: (0, 0, i, 0))] * outs,
        out_specs=[image, image],
        out_shape=[jax.ShapeDtypeStruct((x, y, z), jnp.float32)] * 2,
        compiler_params=params(),
        cost_estimate=cost(
            weight * len(comps) * x * y * z * z, weight * (2 + 3 * len(comps)) * x * y * z
        ),
        name="image_part",
    )(
        place,
        jnp.asarray(table),
        *[field for field in fields for _ in comps],
        *before,
        *blocks,
    )


def over_gx(blocks):
    return lax.all_to_all(blocks, "gx", 0, 0, tiled=True)


def separated(plan, place, velocity, source_p, source_s):
    x, y, z, gx, gy, per = plan.x, plan.y, plan.z, plan.gx, plan.gy, plan.per
    plain = basis(z)
    pair = along_z(plan, place, velocity, (1, 2), (plain, turned(plain)), gy)
    (first,) = along_z(plan, place, velocity, (0,), (crossed(plain, plan),), 1, pair[:1])
    first = over_gx(first.reshape(gx, gy, per, x, y))
    pair = pair_y_forward(plan, place, swap_gy(pair))
    pair = over_gx(pair.reshape(gx, per, x, plan.ny))
    first = first_y_forward(plan, place, swap_gy(first_x_forward(plan, place, first)))
    lines, slope = potential(plan, place, first, pair)
    pair = over_gx(lines)
    last = last_x_inverse(plan, place, swap_gy(last_y_inverse(plan, place, slope)))
    *pair, last = pair_y_inverse(plan, place, pair.reshape(gx * per, x, plan.ny), last)
    pair = swap_gy(pair)
    last = over_gx(last)
    back = inverse_basis(z)
    fields = (velocity, source_p, source_s)
    found = image_part(plan, place, (1, 2), (back, -turned(back)), pair, fields, (), WEIGHT)
    return image_part(plan, place, (0,), (crossed(back, plan),), [last], fields, found, 1)


def shards(velocity, stress, lame_lambda, shear_modulus, buoyancy, source_p, source_s):
    place = jnp.stack([lax.axis_index("gx"), lax.axis_index("gy")]).astype(jnp.int32)
    velocity = propagate(place, velocity, stress, lame_lambda, shear_modulus, buoyancy)
    plan = Plan(velocity.shape[1:])
    if plan.z % (plan.gx * plan.gy) == 0:
        return tuple(separated(plan, place, velocity, source_p, source_s))
    blocks = z_forward(plan, place, velocity)
    lines = [to_lines(plan, y_forward(plan, place, swap_gy(group))) for group in blocks]
    lines = [x_lines(plan, place, part, chunk) for chunk, part in enumerate(lines)]
    blocks = [swap_gy(y_inverse(plan, place, to_planes(plan, part))) for part in lines]
    return tuple(images(plan, place, blocks, velocity, source_p, source_s))


def solution(mesh):
    in_specs = (
        P(None, "gx", "gy", None),
        P(None, "gx", "gy", None),
        P("gx", "gy", None),
        P("gx", "gy", None),
        P("gx", "gy", None),
        P(None, "gx", "gy", None),
        P(None, "gx", "gy", None),
    )
    out_specs = (P("gx", "gy", None), P("gx", "gy", None))
    return jax.shard_map(shards, mesh=mesh, in_specs=in_specs, out_specs=out_specs, check_vma=False)
```

```python
import numpy as np
import ml_dtypes
import jax
import jax.numpy as jnp
from jax import lax
from jax.experimental import pallas as pl
from jax.experimental.pallas import tpu as pltpu
from jax.sharding import PartitionSpec as P

STEPS = 2
MOST_CHUNKS = 1
VMEM_BYTES = 63 * 2**20
STENCIL_BYTES = 22 * 2**20
Y_DEEP = 32
Z_GROUP = 16
X_GROUP = 4
LINE_GROUP = 16
Y_TILE = 32
WEIGHT = 1000

time_step = 0.2


def passed_along(block, axis, distance):
    devices = range(lax.axis_size(axis))
    route = [(i - distance, i) for i in devices if i - distance in devices]
    return lax.ppermute(block, axis, route)


EDGE_ROWS = 8


def with_edges(place, rims, x_last, x_first):
    high, low = rims[-1], rims[0]
    count, z = high.shape[1:]
    some = fit(count, 8)
    lone = len(rims) == 1

    def kernel(place_ref, high_ref, low_ref, _, __, last_ref, first_ref):
        row = lax.broadcasted_iota(jnp.int32, (EDGE_ROWS, z), 0)
        me = place_ref[1]
        keep_high, keep_low = (me == 0, me == 1) if lone else (True, True)
        above = jnp.where(keep_high, high_ref[0, some - 1 :], 0.0)
        below = jnp.where(keep_low, low_ref[0, :1], 0.0)
        last_ref[...] = jnp.where(row == 0, above, 0.0)
        first_ref[...] = jnp.where(row == 0, below, 0.0)

    return pl.pallas_call(
        kernel,
        grid=(1,),
        in_specs=[
            scalars(),
            pl.BlockSpec((1, some, z), lambda i: (0, count // some - 1, 0)),
            pl.BlockSpec((1, some, z), lambda i: (1, 0, 0)),
            unread(),
            unread(),
        ],
        out_specs=[pl.BlockSpec((EDGE_ROWS, z), lambda i: (0, 0))] * 2,
        out_shape=[jax.ShapeDtypeStruct(edge.shape, jnp.float32) for edge in (x_last, x_first)],
        input_output_aliases={3: 0, 4: 1},
        compiler_params=params(4 * 2**20),
        name="with_edges",
    )(place, high, low, x_last, x_first)


def exchange(place, x_last, x_first, *y_outs):
    if len(y_outs) == 1:
        rims = (lax.ppermute(y_outs[0], "gy", [(0, 1), (1, 0)]),)
    else:
        rims = (passed_along(y_outs[0], "gy", 1), passed_along(y_outs[1], "gy", -1))
    x_last, x_first = with_edges(place, rims, x_last, x_first)
    return rims, (passed_along(x_last, "gx", 1), passed_along(x_first, "gx", -1))


def first_rims(brick, place, velocity, stress, lame, shear):
    x, y, z = brick
    some = fit(y, 8)
    many = fit(y, 16)
    swapped = lax.axis_size("gy") == 2

    def kernel(place_ref, *refs):
        (v_first, v_last, s_first, s_last, lame_first, shear_first, shear_last) = refs[:7]
        (v_low, v_high, s_low, s_high, lame_low, shear_low, shear_high) = refs[7:14]
        x_last, x_first, *y_outs = refs[14:]

        def wide(value):
            return value.astype(jnp.float32)

        lasts = [v_last[0, 0], v_last[1, 0], v_last[2, 0], s_last[3, 0], s_last[4, 0]]
        firsts = [v_first[0, 0], v_first[1, 0], v_first[2, 0], s_first[0, 0]]
        lasts += [wide(shear_last[0])]
        firsts += [wide(lame_first[0]), wide(shear_first[0])]
        for ref, values in ((x_last, lasts), (x_first, firsts)):
            ref[:EDGE_ROWS] = jnp.zeros((EDGE_ROWS, z), jnp.float32)
            for i, value in enumerate(values):
                ref[EDGE_ROWS + i * y : EDGE_ROWS + (i + 1) * y] = value
        lasts = [v_high[i, :, some - 1] for i in range(3)]
        firsts = [v_low[i, :, 0] for i in range(3)]
        lasts += [s_high[3, :, some - 1], s_high[5, :, some - 1], wide(shear_high[...])[:, many - 1]]
        firsts += [s_low[1, :, 0], wide(lame_low[...])[:, 0], wide(shear_low[...])[:, 0]]
        for i, (low, high) in enumerate(zip(lasts, firsts)):
            if swapped:
                y_outs[0][i] = jnp.where(place_ref[1] == 0, low, high)
            else:
                y_outs[0][i], y_outs[1][i] = low, high

    def plane(count, at):
        return pl.BlockSpec((count, 1, y, z), lambda i: (0, at, 0, 0))

    def medium_plane(at):
        return pl.BlockSpec((1, y, z), lambda i: (at, 0, 0))

    def rows(count, at):
        return pl.BlockSpec((count, x, some, z), lambda i: (0, 0, at, 0))

    def medium_rows(at):
        return pl.BlockSpec((x, many, z), lambda i: (0, at, 0))

    shapes = [(EDGE_ROWS + 6 * y, z)] * 2 + [(6, x, z)] * (1 if swapped else 2)
    ends, highs, most = x - 1, y // some - 1, y // many - 1
    return pl.pallas_call(
        kernel,
        grid=(1,),
        in_specs=[scalars(), plane(3, 0), plane(3, ends), plane(6, 0), plane(6, ends)]
        + [medium_plane(0), medium_plane(0), medium_plane(ends)]
        + [rows(3, 0), rows(3, highs), rows(6, 0), rows(6, highs)]
        + [medium_rows(0), medium_rows(0), medium_rows(most)],
        out_specs=[whole_block(shape) for shape in shapes],
        out_shape=[jax.ShapeDtypeStruct(shape, jnp.float32) for shape in shapes],
        compiler_params=params(),
        cost_estimate=pl.CostEstimate(
            flops=0, bytes_accessed=80 * (y + 8 * x) * z, transcendentals=0
        ),
        name="first_rims",
    )(
        place,
        *(velocity, velocity, stress, stress, lame, shear, shear),
        *(velocity, velocity, stress, stress, lame, shear, shear),
    )


def stencil(brick, place, state, rims, medium, x_rims, x_medium, done, last):
    x, y, z = brick
    velocity, stress, lame, shear, buoyancy = state
    group = fit(x, X_GROUP)
    groups = x // group
    tall = fit(y, Y_TILE)
    ends = x_rims is not None
    if ends:
        count, of = min(groups, 2), lambda i: i * (groups - 1)
    else:
        count, of = groups - 2, lambda i: i + 1
    f32 = jnp.float32
    swapped = len(rims) == 1

    def kernel(place_ref, *refs):
        refs = list(refs)
        me = place_ref[1]

        def take(number):
            taken = refs[:number]
            del refs[:number]
            return taken

        v_ref, s_ref, lame_ref, shear_ref, buoy_ref = take(5)
        v_next_ref, xx_next_ref, lame_next_ref, shear_next_ref = take(4)
        v_prior_ref, xy_prior_ref, xz_prior_ref, shear_prior_ref = take(4)
        y_rims = take(len(rims))
        y_medium = take(len(rims)) if medium else y_rims
        if ends:
            xl, xr = take(2)
            xl_medium, xr_medium = take(2) if medium else (xl, xr)
        given = take(len(done))
        new = take(1)[0]
        if not last:
            s_out = take(1)[0]
            y_outs = take(len(rims))
            if ends:
                x_last, x_first = take(2)
        carried, xx_after = take(2)
        s_new = take(1)[0] if last else s_out
        turn = pl.program_id(0)
        here_group = of(turn)
        at = here_group * group
        start, end = here_group == 0, here_group == groups - 1
        row = lax.broadcasted_iota(jnp.int32, (y, z), 0)
        lane = lax.broadcasted_iota(jnp.int32, (y, z), 1)

        def next_z(field):
            edge = lane[: field.shape[0]] == z - 1
            return jnp.where(edge, 0.0, pltpu.roll(field, z - 1, 1))

        def prior_z(field):
            edge = lane[: field.shape[0]] == 0
            return jnp.where(edge, 0.0, pltpu.roll(field, 1, 1))

        def next_y(field, rim):
            rows = field.shape[0]
            return jnp.where(row[:rows] == rows - 1, rim, pltpu.roll(field, rows - 1, 0))

        def prior_y(field, rim):
            return jnp.where(row[: field.shape[0]] == 0, rim, pltpu.roll(field, 1, 0))

        def wide(value):
            return value.astype(f32)

        def low(which, at, refs=y_rims):
            value = refs[0][which, pl.ds(at, 1), :]
            return jnp.where(me == 1, value, 0.0) if swapped else value

        def high(which, at, refs=y_rims):
            value = refs[-1][which, pl.ds(at, 1), :]
            return jnp.where(me == 0, value, 0.0) if swapped else value

        def low_after(at):
            if not ends:
                return low(1, at)
            return jnp.where(at == x, xr[:1], low(1, jnp.minimum(at, x - 1)))

        def high_before(at):
            if not ends:
                return high(0, at)
            return jnp.where(at < 0, xl[:1], high(0, jnp.maximum(at, 0)))

        def rows_of(ref, i, span=slice(0, y)):
            start = EDGE_ROWS + i * y
            return ref[start + span.start : start + span.stop]

        def begin(value, rim):
            return jnp.where(start, rim(), value) if ends else value

        def finish(value, rim):
            return jnp.where(end, rim(), value) if ends else value

        def fresh():
            shear_rim = begin(wide(shear_prior_ref[0]), lambda: rows_of(xl_medium, 5))
            vx, vy, vz = (begin(v_prior_ref[i, 0], lambda: rows_of(xl, i)) for i in range(3))
            xy = begin(xy_prior_ref[0, 0], lambda: rows_of(xl, 3))
            xz = begin(xz_prior_ref[0, 0], lambda: rows_of(xl, 4))
            pull = time_step * shear_rim
            carried[0] = vx
            carried[1] = xy + pull * ((next_y(vx, high_before(at - 1)) - vx) + (v_ref[1, 0] - vy))
            carried[2] = xz + pull * ((next_z(vx) - vx) + (v_ref[2, 0] - vz))

        if ends:
            fresh()
        else:
            pl.when(turn == 0)(fresh)
        if not last and done:

            @pl.when(turn == 0)
            def _():
                for out, value in zip(y_outs, given[2:]):
                    out[...] = value[...]

        def after(i, rows):
            return finish(v_next_ref[i, 0, rows], lambda: rows_of(xr, i, rows))

        spans = [slice(top, top + tall) for top in range(0, y, tall)]

        def row_before(span, field, rim):
            return rim() if span.start == 0 else field[span.start - 1 : span.start]

        def row_after(span, field, rim):
            return rim() if span.stop == y else field[span.stop : span.stop + 1]

        for k in range(group):
            here = at + k
            v_here = [v_ref.at[i, k] for i in range(3)]
            for span in spans:
                vx, vy, vz = (field[span] for field in v_here)
                vx_prior = carried[0, span] if k == 0 else v_ref[0, k - 1, span]
                vy_next = after(1, span) if k == group - 1 else v_ref[1, k + 1, span]
                vz_next = after(2, span) if k == group - 1 else v_ref[2, k + 1, span]
                vy_rim = row_before(span, v_here[1], lambda: low(1, here))
                vx_rim = row_after(span, v_here[0], lambda: high(0, here))
                vz_rim = row_after(span, v_here[2], lambda: high(2, here))
                lame_value, shear_value = wide(lame_ref[k, span]), wide(shear_ref[k, span])
                ex = vx - vx_prior
                ey = vy - prior_y(vy, vy_rim)
                ez = vz - prior_z(vz)
                swell = lame_value * (ex + ey + ez)
                double = 2.0 * shear_value
                pull = time_step * shear_value
                found = (
                    s_ref[0, k, span] + time_step * (swell + double * ex),
                    s_ref[1, k, span] + time_step * (swell + double * ey),
                    s_ref[2, k, span] + time_step * (swell + double * ez),
                    s_ref[3, k, span] + pull * ((next_y(vx, vx_rim) - vx) + (vy_next - vy)),
                    s_ref[4, k, span] + pull * ((next_z(vx) - vx) + (vz_next - vz)),
                    s_ref[5, k, span] + pull * ((next_z(vy) - vy) + (next_y(vz, vz_rim) - vz)),
                )
                for i, value in enumerate(found):
                    s_new[i, k, span] = value

        for span in spans:
            vx, vy, vz = (after(i, span) for i in range(3))
            vy_rim = (
                low_after(at + group)
                if span.start == 0
                else after(1, slice(span.start - 1, span.start))
            )
            ex = vx - v_ref[0, group - 1, span]
            ey = vy - prior_y(vy, vy_rim)
            ez = vz - prior_z(vz)
            lame_value = finish(wide(lame_next_ref[0, span]), lambda: rows_of(xr_medium, 4, span))
            shear_value = finish(wide(shear_next_ref[0, span]), lambda: rows_of(xr_medium, 5, span))
            xx_after[span] = finish(xx_next_ref[0, 0, span], lambda: rows_of(xr, 3, span)) + time_step * (
                lame_value * (ex + ey + ez) + 2.0 * shear_value * ex
            )

        for k in range(group):
            here = at + k
            v_here = [v_ref.at[i, k] for i in range(3)]
            vx_edge, vy_edge, vz_edge = v_here[0][:1], v_here[1][y - 1 :], v_here[2][:1]
            pull = time_step * low(5, here, y_medium)
            vy_rim, vz_rim = low(1, here), low(2, here)
            xy_rim = low(3, here) + pull * (
                (vx_edge - low(0, here)) + (low_after(here + 1) - vy_rim)
            )
            yz_rim = low(4, here) + pull * ((next_z(vy_rim) - vy_rim) + (vz_edge - vz_rim))
            vx_rim, vz_rim = high(0, here), high(2, here)
            ex = vx_rim - high_before(here - 1)
            ey = high(1, here) - vy_edge
            ez = vz_rim - prior_z(vz_rim)
            yy_rim = high(3, here) + time_step * (
                high(4, here, y_medium) * (ex + ey + ez) + 2.0 * high(5, here, y_medium) * ey
            )
            s_here = [s_new.at[i, k] for i in range(6)]
            for span in spans:
                xx, yy, zz, xy, xz, yz = (field[span] for field in s_here)
                xx_next = xx_after[span] if k == group - 1 else s_new[0, k + 1, span]
                xy_prior = carried[1, span] if k == 0 else s_new[3, k - 1, span]
                xz_prior = carried[2, span] if k == 0 else s_new[4, k - 1, span]
                xy_before = row_before(span, s_here[3], lambda: xy_rim)
                yz_before = row_before(span, s_here[5], lambda: yz_rim)
                yy_after = row_after(span, s_here[1], lambda: yy_rim)
                push = time_step * wide(buoy_ref[k, span])
                new[0, k, span] = v_ref[0, k, span] + push * (
                    (xx_next - xx) + (xy - prior_y(xy, xy_before)) + (xz - prior_z(xz))
                )
                new[1, k, span] = v_ref[1, k, span] + push * (
                    (xy - xy_prior) + (next_y(yy, yy_after) - yy) + (yz - prior_z(yz))
                )
                new[2, k, span] = v_ref[2, k, span] + push * (
                    (xz - xz_prior) + (yz - prior_y(yz, yz_before)) + (next_z(zz) - zz)
                )
            if last:
                continue
            lasts = [new[i, k, y - 1 :] for i in range(3)]
            lasts += [s_new[3, k, y - 1 :], s_new[5, k, y - 1 :]]
            firsts = [new[i, k, :1] for i in range(3)] + [s_new[1, k, :1]] * 2
            for i in range(5):
                spot = pl.ds(here, 1)
                if swapped:
                    y_outs[0][i, spot, :] = jnp.where(me == 0, lasts[i], firsts[i])
                else:
                    y_outs[0][i, spot, :], y_outs[1][i, spot, :] = lasts[i], firsts[i]

        if ends and not last:

            def edge(out, values):
                out[:EDGE_ROWS] = jnp.zeros((EDGE_ROWS, z), f32)
                for i, value in enumerate(values):
                    out[EDGE_ROWS + i * y : EDGE_ROWS + (i + 1) * y] = value

            @pl.when(start)
            def _():
                edge(x_first, [new[0, 0], new[1, 0], new[2, 0], s_new[0, 0]])

            @pl.when(end)
            def _():
                most = group - 1
                values = [new[i, most] for i in range(3)]
                edge(x_last, values + [s_new[3, most], s_new[4, most]])

        if not ends:
            carried[0] = v_ref[0, group - 1]
            carried[1] = s_new[3, group - 1]
            carried[2] = s_new[4, group - 1]

    def next_plane(i):
        return jnp.minimum((of(i) + 1) * group, x - 1)

    def prior_plane(i):
        return jnp.maximum(of(i) * group - 1, 0) if ends else group - 1

    def planes(number):
        return pl.BlockSpec((number, group, y, z), lambda i: (0, of(i), 0, 0))

    def one(number, which, place):
        return pl.BlockSpec((number, 1, y, z), lambda i: (which, place(i), 0, 0))

    def medium_one(place):
        return pl.BlockSpec((1, y, z), lambda i: (place(i), 0, 0))

    medium_block = pl.BlockSpec((group, y, z), lambda i: (of(i), 0, 0))
    args = [place, velocity, stress, lame, shear, buoyancy, velocity, stress, lame, shear]
    args += [velocity, stress, stress, shear, *rims, *medium]
    in_specs = [scalars(), planes(3), planes(6), medium_block, medium_block, medium_block]
    in_specs += [one(3, 0, next_plane), one(1, 0, next_plane)]
    in_specs += [medium_one(next_plane), medium_one(next_plane)]
    in_specs += [one(3, 0, prior_plane), one(1, 3, prior_plane), one(1, 4, prior_plane)]
    in_specs += [medium_one(prior_plane)]
    in_specs += [whole_block(rim.shape) for rim in (*rims, *medium)]
    if ends:
        args += [*x_rims, *x_medium]
        in_specs += [whole_block(rim.shape) for rim in (*x_rims, *x_medium)]
    aliases = {}
    for i, value in enumerate(done):
        if i < 2:
            aliases[len(args)] = i
        in_specs.append(unread() if i < 2 else whole_block(value.shape))
        args.append(value)
    out_shape = [(3, x, y, z)]
    out_specs = [planes(3)]
    if not last:
        out_shape += [(6, x, y, z)] + [(5, x, z)] * len(rims)
        out_specs += [planes(6)]
        if ends:
            out_shape += [(EDGE_ROWS + 5 * y, z), (EDGE_ROWS + 4 * y, z)]
        out_specs += [whole_block(shape) for shape in out_shape[2:]]
    part = (1 if ends else WEIGHT) * count * group * y * z
    return pl.pallas_call(
        kernel,
        grid=(count,),
        in_specs=in_specs,
        out_specs=out_specs,
        out_shape=[jax.ShapeDtypeStruct(shape, f32) for shape in out_shape],
        scratch_shapes=[pltpu.VMEM((3, y, z), f32), pltpu.VMEM((y, z), f32)]
        + ([pltpu.VMEM((6, group, y, z), f32)] if last else []),
        input_output_aliases=aliases,
        compiler_params=params(STENCIL_BYTES),
        cost_estimate=pl.CostEstimate(
            flops=80 * part, bytes_accessed=(54 if last else 78) * part, transcendentals=0
        ),
        name="stencil_ends" if ends else "stencil_middle",
    )(*args)


def propagate(place, velocity, stress, lame, shear, buoyancy):
    brick = velocity.shape[1:]
    between = brick[0] // fit(brick[0], X_GROUP) > 2
    rims, x_rims = exchange(place, *first_rims(brick, place, velocity, stress, lame, shear))
    held, medium, x_medium = (rims, x_rims), (), ()
    for step_index in range(STEPS):
        last = step_index == STEPS - 1
        state = (velocity, stress, lame, shear, buoyancy)
        done = []
        if between:
            done = stencil(brick, place, state, rims, medium, None, None, done, last)
        found = stencil(brick, place, state, rims, medium, x_rims, x_medium, done, last)
        velocity = found[0]
        if not last:
            _, stress, *y_outs, x_last, x_first = found
            rims, x_rims = exchange(place, x_last, x_first, *y_outs)
            medium, x_medium = held
    return velocity


def basis(length):
    half = length // 2
    wave = np.arange(half)
    place = np.arange(length)
    angle = (wave[:, None] * place[None, :] % length) * (2.0 * np.pi / length)
    cosine, sine = np.cos(angle), np.sin(angle)
    sine[0] = 1.0 - 2.0 * (place % 2)
    return np.concatenate([cosine, sine])


def waves_of(length):
    return np.tile(np.arange(length // 2, dtype=np.float64), 2)


def inverse_basis(length):
    weight = np.where(waves_of(length) == 0, 1.0, 2.0) / length
    return basis(length) * weight[:, None]


def turned(table):
    half = table.shape[0] // 2
    return np.concatenate([table[half:], -table[:half]]) * waves_of(table.shape[0])[:, None]


def halves(table):
    high = table.astype(ml_dtypes.bfloat16)
    low = (table - high.astype(np.float64)).astype(ml_dtypes.bfloat16)
    return np.stack([high, low])


def split(value):
    high = value.astype(jnp.bfloat16)
    return high, (value - high.astype(jnp.float32)).astype(jnp.bfloat16)


def dot(left, right, dims=((1,), (0,))):
    return lax.dot_general(left, right, (dims, ((), ())), preferred_element_type=jnp.float32)


def times(left, right):
    return dot(left[0], right[0]) + (dot(left[1], right[0]) + dot(left[0], right[1]))


def joined(pieces, axis):
    return pieces[0] if len(pieces) == 1 else jnp.concatenate(pieces, axis=axis)


def fit(length, most):
    size = min(length, most)
    while length % size:
        size -= 1
    return size


def params(limit=VMEM_BYTES):
    return pltpu.CompilerParams(vmem_limit_bytes=limit)


def whole_block(shape):
    return pl.BlockSpec(shape, lambda *_: (0,) * len(shape))


def scalars():
    return pl.BlockSpec(memory_space=pltpu.SMEM)


class Plan:
    def __init__(self, brick):
        self.x, self.y, self.z = brick
        self.gx, self.gy = lax.axis_size("gx"), lax.axis_size("gy")
        self.nx, self.ny = self.x * self.gx, self.y * self.gy
        chunks = MOST_CHUNKS
        while chunks > 1 and self.z % (chunks * self.gy * self.gx):
            chunks -= 1
        self.chunks = chunks
        self.kz = self.z // (chunks * self.gy)
        self.parts = max(1, self.gx // self.kz)
        self.per = max(1, self.kz // self.gx)
        self.ky = self.ny // self.parts


def source(me, step, count):
    return lax.rem(me - step + count, count)


def z_forward(plan, place, velocity):
    x, y, z, kz = plan.x, plan.y, plan.z, plan.kz
    table = np.stack([halves(basis(z)), halves(turned(basis(z)))])
    table = table.reshape(2, 2, plan.chunks, plan.gy, kz, z)
    count = plan.chunks * plan.gy

    group = fit(x, Z_GROUP)
    deep = fit(group, 2)

    def kernel(place_ref, table_ref, v_ref, *outs):
        at = pl.program_id(0) * group
        me = place_ref[1]
        order = [(c, lax.rem(me + s, plan.gy)) for c in range(plan.chunks) for s in range(plan.gy)]
        tables = []
        for kind in range(2):
            high, low = (joined([table_ref[kind, i, c, g] for c, g in order], 0) for i in range(2))
            tables.append((jnp.concatenate([high, high], axis=1), low))
        for comp in range(3):
            twice, low = tables[1 if comp == 2 else 0]
            for plane in range(0, group, deep):
                field = split(v_ref[comp, plane : plane + deep].reshape(deep * y, z))
                value = dot(twice, jnp.concatenate(field, axis=1), ((1,), (1,)))
                value += dot(low, field[0], ((1,), (1,)))
                for i, out in enumerate(outs):
                    for k in range(deep):
                        part = value[i * kz : (i + 1) * kz, k * y : (k + 1) * y]
                        out[comp, pl.ds(at + plane + k, kz, stride=x), :] = part

    outs = pl.pallas_call(
        kernel,
        grid=(x // group,),
        in_specs=[
            scalars(),
            whole_block(table.shape),
            pl.BlockSpec((3, group, y, z), lambda i: (0, i, 0, 0)),
        ],
        out_specs=[whole_block((3, kz * x, y))] * count,
        out_shape=[jax.ShapeDtypeStruct((3, kz * x, y), jnp.float32)] * count,
        compiler_params=params(),
        cost_estimate=pl.CostEstimate(
            flops=18 * x * y * z * z, bytes_accessed=24 * x * y * z, transcendentals=0
        ),
        name="z_forward",
    )(place, jnp.asarray(table), velocity)
    outs = [out.reshape(3, kz, x, y) for out in outs]
    return [outs[c * plan.gy : (c + 1) * plan.gy] for c in range(plan.chunks)]


def swap_gy(blocks):
    count = len(blocks)
    moved = [blocks[0]]
    for step in range(1, count):
        route = [(i, (i + step) % count) for i in range(count)]
        moved.append(lax.ppermute(blocks[step], "gy", route))
    return moved


def y_forward(plan, place, blocks):
    x, y, ny, kz = plan.x, plan.y, plan.ny, plan.kz
    table = halves(basis(ny).T).reshape(2, plan.gy, y, ny)
    deep = fit(kz, 8)
    rows = deep * x
    half = ny // 2
    aligned = y % 128 == 0

    def kernel(place_ref, table_ref, *refs):
        ins, out = refs[:-1], refs[-1]
        me = place_ref[1]
        groups = [source(me, step, plan.gy) for step in range(plan.gy)]
        tables = [(table_ref[0, g], table_ref[1, g]) for g in groups]
        if aligned:
            tables = [tuple(joined([t[i] for t in tables], 0) for i in range(2))]

        def moved(comp):
            fields = [ref[comp].reshape(rows, y) for ref in ins]
            if aligned:
                fields = [joined(fields, 1)]
            return sum(times(split(f), t) for f, t in zip(fields, tables))

        wave = lax.broadcasted_iota(jnp.int32, (1, half), 1).astype(jnp.float32)
        out[:, 0] = moved(0).reshape(deep, x, ny)
        along, rest = moved(1), moved(2)
        out[:, 1, :, :half] = (rest[:, :half] + wave * along[:, half:]).reshape(deep, x, half)
        out[:, 1, :, half:] = (rest[:, half:] - wave * along[:, :half]).reshape(deep, x, half)

    return pl.pallas_call(
        kernel,
        grid=(kz // deep,),
        in_specs=[scalars(), whole_block(table.shape)]
        + [pl.BlockSpec((3, deep, x, y), lambda i: (0, i, 0, 0))] * plan.gy,
        out_specs=pl.BlockSpec((deep, 2, x, ny), lambda i: (i, 0, 0, 0)),
        out_shape=jax.ShapeDtypeStruct((kz, 2, x, ny), jnp.float32),
        compiler_params=params(),
        cost_estimate=pl.CostEstimate(
            flops=18 * kz * x * ny * ny, bytes_accessed=20 * kz * x * ny, transcendentals=0
        ),
        name="y_forward",
    )(place, jnp.asarray(table), *blocks)


def to_lines(plan, planes):
    if plan.parts > 1:
        planes = planes.reshape(plan.kz, 2, plan.x, plan.parts, plan.ky).transpose(0, 3, 1, 2, 4)
    planes = planes.reshape(plan.gx, plan.per, 2, plan.x, plan.ky)
    return lax.all_to_all(planes, "gx", 0, 0, tiled=True)


def to_planes(plan, lines):
    planes = lax.all_to_all(lines, "gx", 0, 0, tiled=True)
    if plan.parts > 1:
        planes = planes.reshape(plan.kz, plan.parts, 2, plan.x, plan.ky).transpose(0, 2, 3, 1, 4)
    return planes.reshape(plan.kz, 2, plan.x, plan.ny)


def x_lines(plan, place, lines, chunk):
    x, nx, ny, ky, gx = plan.x, plan.nx, plan.ny, plan.ky, plan.gx
    forth = halves(basis(nx))
    back = halves(-inverse_basis(nx).T)
    lanes = 128 if ky % 128 == 0 else ky
    half = nx // 2
    aligned = lanes % 128 == 0

    def kernel(place_ref, forth_ref, back_ref, in_ref, out_ref):
        me_x, me_y = place_ref[0], place_ref[1]
        which, lane = pl.program_id(0), pl.program_id(1)

        def through(table_ref, pair):
            table = (table_ref[0], table_ref[1])
            if aligned:
                both = times(table, split(jnp.concatenate(pair, axis=1)))
                return both[:, :lanes], both[:, lanes:]
            return tuple(times(table, split(value)) for value in pair)

        pair = [in_ref[:, 0, i].reshape(nx, lanes) for i in range(2)]
        along, rest = through(forth_ref, pair)
        wave_x = lax.broadcasted_iota(jnp.int32, (half, lanes), 0).astype(jnp.float32)
        slot_y = lax.broadcasted_iota(jnp.int32, (1, lanes), 1) + (
            lane * lanes + lax.rem(me_x, plan.parts) * ky
        )
        wave_y = lax.rem(slot_y, ny // 2).astype(jnp.float32)
        slot_z = (chunk * plan.gy + me_y) * plan.kz + me_x // plan.parts * plan.per + which
        wave_z = lax.rem(slot_z, plan.z // 2).astype(jnp.float32)
        scale = 1.0 / jnp.maximum(wave_x * wave_x + (wave_y * wave_y + wave_z * wave_z), 1.0)
        cosine = (rest[:half] + wave_x * along[half:]) * scale
        sine = (rest[half:] - wave_x * along[:half]) * scale
        plain = jnp.concatenate([cosine, sine], axis=0)
        slope = jnp.concatenate([wave_x * sine, -wave_x * cosine], axis=0)
        for i, value in enumerate(through(back_ref, [slope, plain])):
            out_ref[:, 0, i] = value.reshape(gx, x, lanes)

    block = pl.BlockSpec((gx, 1, 2, x, lanes), lambda i, j: (0, i, 0, 0, j))
    return pl.pallas_call(
        kernel,
        grid=(plan.per, ky // lanes),
        in_specs=[scalars(), whole_block(forth.shape), whole_block(back.shape), block],
        out_specs=block,
        out_shape=jax.ShapeDtypeStruct(lines.shape, jnp.float32),
        compiler_params=params(),
        cost_estimate=pl.CostEstimate(
            flops=24 * plan.per * ky * nx * nx,
            bytes_accessed=16 * plan.per * ky * nx,
            transcendentals=0,
        ),
        name="x_lines",
    )(place, jnp.asarray(forth), jnp.asarray(back), lines)


def y_inverse(plan, place, planes):
    x, y, ny, kz = plan.x, plan.y, plan.ny, plan.kz
    table = np.stack(np.split(inverse_basis(ny), plan.gy, axis=1))
    table = halves(table)
    deep = fit(kz, 8)
    rows = deep * x
    half = ny // 2
    aligned = y % 128 == 0

    def kernel(place_ref, table_ref, in_ref, *outs):
        me = place_ref[1]
        groups = [lax.rem(me + step, plan.gy) for step in range(plan.gy)]
        tables = [(table_ref[0, g], table_ref[1, g]) for g in groups]
        slope = in_ref[:, 0].reshape(rows, ny)
        plain = in_ref[:, 1].reshape(rows, ny)
        wave = lax.broadcasted_iota(jnp.int32, (1, half), 1).astype(jnp.float32)
        along = jnp.concatenate([wave * plain[:, half:], -wave * plain[:, :half]], axis=1)
        for comp, value in enumerate((slope, along, plain)):
            parts = split(value)
            if aligned:
                table = tuple(joined([t[i] for t in tables], 1) for i in range(2))
                found = times(parts, table)
                pieces = [found[:, s * y : (s + 1) * y] for s in range(plan.gy)]
            else:
                pieces = [times(parts, t) for t in tables]
            for out, piece in zip(outs, pieces):
                out[comp] = piece.reshape(deep, x, y)

    return pl.pallas_call(
        kernel,
        grid=(kz // deep,),
        in_specs=[
            scalars(),
            whole_block(table.shape),
            pl.BlockSpec((deep, 2, x, ny), lambda i: (i, 0, 0, 0)),
        ],
        out_specs=[pl.BlockSpec((3, deep, x, y), lambda i: (0, i, 0, 0))] * plan.gy,
        out_shape=[jax.ShapeDtypeStruct((3, kz, x, y), jnp.float32)] * plan.gy,
        compiler_params=params(),
        cost_estimate=pl.CostEstimate(
            flops=18 * kz * x * ny * ny, bytes_accessed=20 * kz * x * ny, transcendentals=0
        ),
        name="y_inverse",
    )(place, jnp.asarray(table), planes)


def images(plan, place, blocks, velocity, source_p, source_s):
    x, y, z, kz = plan.x, plan.y, plan.z, plan.kz
    table = np.stack([halves(inverse_basis(z)), halves(-turned(inverse_basis(z)))])
    table = table.reshape(2, 2, plan.chunks, plan.gy, kz, z)
    blocks = [block.reshape(3, kz * x, y) for group in blocks for block in group]

    group = fit(x, Z_GROUP)
    deep = fit(group, 2)

    def kernel(place_ref, table_ref, v_ref, p_ref, s_ref, *refs):
        ins, (image_p, image_s) = refs[:-2], refs[-2:]
        at = pl.program_id(0) * group
        me = place_ref[1]
        order = [
            (chunk, source(me, step, plan.gy))
            for chunk in range(plan.chunks)
            for step in range(plan.gy)
        ]
        tables = []
        for kind in range(2):
            high, low = (joined([table_ref[kind, i, c, g] for c, g in order], 0) for i in range(2))
            high, low = (part.astype(jnp.float32).T.astype(jnp.bfloat16) for part in (high, low))
            tables.append((jnp.concatenate([high, high], axis=1), low))
        for plane in range(0, group, deep):
            here = slice(plane, plane + deep)
            total_p = total_s = 0.0
            for comp in range(3):
                twice, low = tables[1 if comp == 2 else 0]
                columns = [
                    joined([ref[comp, pl.ds(at + plane + k, kz, stride=x), :] for ref in ins], 0)
                    for k in range(deep)
                ]
                high, rest = split(joined(columns, 1))
                field = dot(twice, jnp.concatenate([high, rest], axis=0)) + dot(low, high)
                field = field.T.reshape(deep, y, z)
                total_p += p_ref[comp, here].astype(jnp.float32) * field
                total_s += s_ref[comp, here].astype(jnp.float32) * (v_ref[comp, here] - field)
            image_p[here] = total_p
            image_s[here] = total_s

    plane = pl.BlockSpec((3, group, y, z), lambda i: (0, i, 0, 0))
    image = pl.BlockSpec((group, y, z), lambda i: (i, 0, 0))
    return pl.pallas_call(
        kernel,
        grid=(x // group,),
        in_specs=[scalars(), whole_block(table.shape), plane, plane, plane]
        + [whole_block((3, kz * x, y))] * len(blocks),
        out_specs=[image, image],
        out_shape=[jax.ShapeDtypeStruct((x, y, z), jnp.float32)] * 2,
        compiler_params=params(),
        cost_estimate=pl.CostEstimate(
            flops=18 * x * y * z * z, bytes_accessed=44 * x * y * z, transcendentals=0
        ),
        name="images",
    )(place, jnp.asarray(table), velocity, source_p, source_s, *blocks)


def doubled(table, axis):
    high, low = halves(table)
    return np.concatenate([high, high], axis=axis), low


def left_times(table, value):
    high, low = split(value)
    return dot(table[0], jnp.concatenate([high, low], axis=0)) + dot(table[1], high)


def right_times(value, table):
    high, low = split(value)
    return dot(jnp.concatenate([high, low], axis=1), table[0]) + dot(high, table[1])


def odd_basis(length):
    wave = 2 * np.arange(length // 4) + 1
    angle = (wave[:, None] * np.arange(length // 2) % length) * (2.0 * np.pi / length)
    return np.concatenate([np.cos(angle), np.sin(angle)])


def x_tables(length, inverse):
    even, odd = basis(length // 2), odd_basis(length)
    if inverse:
        even, odd = -inverse_basis(length // 2).T / 2.0, -odd.T * (2.0 / length)
    return [*doubled(even, 1), *doubled(odd, 1)]


def x_forward(tables, value):
    half = value.shape[0] // 2
    even = left_times(tables[:2], value[:half] + value[half:])
    return jnp.concatenate([even, left_times(tables[2:], value[:half] - value[half:])], axis=0)


def x_inverse(tables, value):
    half = value.shape[0] // 2
    even = left_times(tables[:2], value[:half])
    odd = left_times(tables[2:], value[half:])
    return jnp.concatenate([even + odd, even - odd], axis=0)


def x_wave(length):
    slot = lax.broadcasted_iota(jnp.int32, (length, 1), 0)
    wave = 2 * lax.rem(slot, length // 4) + slot // (length // 2)
    return wave.astype(jnp.float32)


def slope_x(value):
    part = value.shape[0] // 4
    wave = x_wave(value.shape[0])
    swapped = [value[part : 2 * part], -value[:part], value[3 * part :], -value[2 * part : 3 * part]]
    return wave * jnp.concatenate(swapped, axis=0)


def side_by_side(through, tables, values):
    width = values[0].shape[1]
    if width % 128:
        return [through(tables, value) for value in values]
    both = through(tables, joined(values, 1))
    return [both[:, i * width : (i + 1) * width] for i in range(len(values))]


def cost(flops, values):
    return pl.CostEstimate(flops=6 * flops, bytes_accessed=4 * values, transcendentals=0)


def crossed(table, plan):
    shape = (plan.gy, plan.gx, plan.per, table.shape[-1])
    return table.reshape(shape).transpose(1, 0, 2, 3).reshape(table.shape)


def unread():
    return pl.BlockSpec(memory_space=pl.ANY)


def along_z(plan, place, velocity, comps, tables, outs, ahead=()):
    x, y, z = plan.x, plan.y, plan.z
    table = np.stack([halves(table) for table in tables]).reshape(len(comps), 2, outs, z // outs, z)
    group = fit(x, LINE_GROUP)
    deep = fit(group, 2)
    rows = z // outs

    def kernel(place_ref, table_ref, *refs):
        fields, found = refs[: len(comps)], refs[len(comps) + len(ahead) :]
        found = [out.reshape(len(comps), rows * group, y) for out in found]
        me = place_ref[1]
        order = [lax.rem(me + s, outs) if outs > 1 else 0 for s in range(outs)]
        for comp, field in enumerate(fields):
            high, low = (joined([table_ref[comp, i, g] for g in order], 0) for i in range(2))
            twice = jnp.concatenate([high, high], axis=1)
            for plane in range(0, group, deep):
                parts = split(field[0, plane : plane + deep].reshape(deep * y, z))
                value = dot(twice, jnp.concatenate(parts, axis=1), ((1,), (1,)))
                value += dot(low, parts[0], ((1,), (1,)))
                for i, out in enumerate(found):
                    for k in range(deep):
                        part = value[i * rows : (i + 1) * rows, k * y : (k + 1) * y]
                        out[comp, pl.ds(plane + k, rows, stride=group), :] = part

    def block(comp):
        return pl.BlockSpec((1, group, y, z), lambda i: (comp, i, 0, 0))

    shape = (len(comps), rows, x, y)
    return pl.pallas_call(
        kernel,
        grid=(x // group,),
        in_specs=[scalars(), whole_block(table.shape)]
        + [block(comp) for comp in comps]
        + [unread()] * len(ahead),
        out_specs=[pl.BlockSpec((len(comps), rows, group, y), lambda i: (0, 0, i, 0))] * outs,
        out_shape=[jax.ShapeDtypeStruct(shape, jnp.float32)] * outs,
        compiler_params=params(STENCIL_BYTES),
        cost_estimate=cost(len(comps) * x * y * z * z, 2 * len(comps) * x * y * z),
        name="along_z",
    )(place, jnp.asarray(table), *[velocity] * len(comps), *ahead)


def y_table(plan, table_ref, groups):
    tables = [(table_ref[0, g], table_ref[1, g]) for g in groups]
    if plan.y % 128 == 0:
        high, low = (joined([table[i] for table in tables], 0) for i in range(2))
        return [(jnp.concatenate([high, high], axis=0), low)]
    return [(jnp.concatenate([high, high], axis=0), low) for high, low in tables]


def over_y(fields, tables):
    if len(tables) == 1:
        fields = [joined(fields, 1)]
    return sum(right_times(field, table) for field, table in zip(fields, tables))


def pair_y_forward(plan, place, blocks):
    x, y, ny = plan.x, plan.y, plan.ny
    count = blocks[0].shape[1]
    table = halves(basis(ny).T).reshape(2, plan.gy, y, ny)
    deep = fit(count, Y_DEEP)
    rows = deep * x
    half = ny // 2

    def kernel(place_ref, table_ref, *refs):
        ins, out = refs[:-1], refs[-1]
        me = place_ref[1]
        tables = y_table(plan, table_ref, [source(me, s, plan.gy) for s in range(plan.gy)])
        along, rest = (
            over_y([ref[comp].reshape(rows, y) for ref in ins], tables) for comp in range(2)
        )
        wave = lax.broadcasted_iota(jnp.int32, (1, half), 1).astype(jnp.float32)
        out[:, :, :half] = (rest[:, :half] + wave * along[:, half:]).reshape(deep, x, half)
        out[:, :, half:] = (rest[:, half:] - wave * along[:, :half]).reshape(deep, x, half)

    return pl.pallas_call(
        kernel,
        grid=(count // deep,),
        in_specs=[scalars(), whole_block(table.shape)]
        + [pl.BlockSpec((2, deep, x, y), lambda i: (0, i, 0, 0))] * plan.gy,
        out_specs=pl.BlockSpec((deep, x, ny), lambda i: (i, 0, 0)),
        out_shape=jax.ShapeDtypeStruct((count, x, ny), jnp.float32),
        compiler_params=params(),
        cost_estimate=cost(2 * WEIGHT * count * x * ny * ny, 3 * WEIGHT * count * x * ny),
        name="pair_y_forward",
    )(place, jnp.asarray(table), *blocks)


def first_x_forward(plan, place, lines):
    x, y, nx = plan.x, plan.y, plan.nx
    tables = x_tables(nx, False)

    def kernel(place_ref, *refs):
        table_refs, in_ref, outs = refs[:4], refs[4], refs[5:]
        me = place_ref[1]
        fields = [in_ref[:, lax.rem(me + s, plan.gy), 0].reshape(nx, y) for s in range(plan.gy)]
        found = side_by_side(x_forward, [ref[...] for ref in table_refs], fields)
        for out, value in zip(outs, found):
            out[0] = value

    return pl.pallas_call(
        kernel,
        grid=(plan.per,),
        in_specs=[scalars()]
        + [whole_block(table.shape) for table in tables]
        + [pl.BlockSpec((plan.gx, plan.gy, 1, x, y), lambda i: (0, 0, i, 0, 0))],
        out_specs=[pl.BlockSpec((1, nx, y), lambda i: (i, 0, 0))] * plan.gy,
        out_shape=[jax.ShapeDtypeStruct((plan.per, nx, y), jnp.float32)] * plan.gy,
        compiler_params=params(),
        cost_estimate=cost(plan.per * plan.ny * nx * nx, 2 * plan.per * plan.ny * nx),
        name="first_x_forward",
    )(place, *[jnp.asarray(table) for table in tables], lines)


def first_y_forward(plan, place, blocks):
    y, nx, ny = plan.y, plan.nx, plan.ny
    table = halves(basis(ny).T).reshape(2, plan.gy, y, ny)

    def kernel(place_ref, table_ref, *refs):
        ins, out = refs[:-1], refs[-1]
        me = place_ref[1]
        tables = y_table(plan, table_ref, [source(me, s, plan.gy) for s in range(plan.gy)])
        out[0] = slope_x(over_y([ref[0] for ref in ins], tables))

    return pl.pallas_call(
        kernel,
        grid=(plan.per,),
        in_specs=[scalars(), whole_block(table.shape)]
        + [pl.BlockSpec((1, nx, y), lambda i: (i, 0, 0))] * plan.gy,
        out_specs=pl.BlockSpec((1, nx, ny), lambda i: (i, 0, 0)),
        out_shape=jax.ShapeDtypeStruct((plan.per, nx, ny), jnp.float32),
        compiler_params=params(),
        cost_estimate=cost(plan.per * nx * ny * ny, 2 * plan.per * nx * ny),
        name="first_y_forward",
    )(place, jnp.asarray(table), *blocks)


def potential(plan, place, first, lines):
    x, nx, ny, gx = plan.x, plan.nx, plan.ny, plan.gx
    tables = x_tables(nx, False) + x_tables(nx, True)

    def kernel(place_ref, *refs):
        first_ref, in_ref, out_ref, slope_ref = refs[8:]
        forth, back = ([ref[...] for ref in refs[i : i + 4]] for i in (0, 4))
        me_x, me_y = place_ref[0], place_ref[1]
        total = x_forward(forth, in_ref[:, 0].reshape(nx, ny)) + first_ref[0]
        wave_x = x_wave(nx)
        slot_y = lax.broadcasted_iota(jnp.int32, (1, ny), 1)
        wave_y = lax.rem(slot_y, ny // 2).astype(jnp.float32)
        slot_z = (me_y * gx + me_x) * plan.per + pl.program_id(0)
        wave_z = lax.rem(slot_z, plan.z // 2).astype(jnp.float32)
        square = wave_x * wave_x + (wave_y * wave_y + wave_z * wave_z)
        found = total / jnp.maximum(square, 1.0)
        out_ref[:, 0] = x_inverse(back, found).reshape(gx, x, ny)
        slope_ref[0] = slope_x(found)

    spectrum = pl.BlockSpec((1, nx, ny), lambda i: (i, 0, 0))
    block = pl.BlockSpec((gx, 1, x, ny), lambda i: (0, i, 0, 0))
    return pl.pallas_call(
        kernel,
        grid=(plan.per,),
        in_specs=[scalars()] + [whole_block(t.shape) for t in tables] + [spectrum, block],
        out_specs=[block, spectrum],
        out_shape=[
            jax.ShapeDtypeStruct(lines.shape, jnp.float32),
            jax.ShapeDtypeStruct((plan.per, nx, ny), jnp.float32),
        ],
        compiler_params=params(),
        cost_estimate=cost(2 * plan.per * ny * nx * nx, 4 * plan.per * ny * nx),
        name="potential",
    )(place, *[jnp.asarray(t) for t in tables], first, lines)


def pieces_of_y(plan, table_ref, me, values):
    groups = [lax.rem(me + s, plan.gy) for s in range(plan.gy)]
    y = plan.y
    tables = [(table_ref[0, g], table_ref[1, g]) for g in groups]
    if y % 128 == 0:
        tables = [tuple(joined([table[i] for table in tables], 1) for i in range(2))]
    tables = [(jnp.concatenate([high, high], axis=0), low) for high, low in tables]
    found = []
    for value in values:
        pieces = [right_times(value, table) for table in tables]
        if y % 128 == 0:
            pieces = [pieces[0][:, s * y : (s + 1) * y] for s in range(plan.gy)]
        found.append(pieces)
    return found


def last_y_inverse(plan, place, slope):
    y, nx, ny = plan.y, plan.nx, plan.ny
    table = halves(np.stack(np.split(inverse_basis(ny), plan.gy, axis=1)))

    def kernel(place_ref, table_ref, in_ref, *outs):
        (pieces,) = pieces_of_y(plan, table_ref, place_ref[1], [in_ref[0]])
        for out, piece in zip(outs, pieces):
            out[0] = piece

    return pl.pallas_call(
        kernel,
        grid=(plan.per,),
        in_specs=[
            scalars(),
            whole_block(table.shape),
            pl.BlockSpec((1, nx, ny), lambda i: (i, 0, 0)),
        ],
        out_specs=[pl.BlockSpec((1, nx, y), lambda i: (i, 0, 0))] * plan.gy,
        out_shape=[jax.ShapeDtypeStruct((plan.per, nx, y), jnp.float32)] * plan.gy,
        compiler_params=params(),
        cost_estimate=cost(plan.per * nx * ny * ny, 2 * plan.per * nx * ny),
        name="last_y_inverse",
    )(place, jnp.asarray(table), slope)


def last_x_inverse(plan, place, blocks, ahead):
    x, y, nx, gx = plan.x, plan.y, plan.nx, plan.gx
    tables = x_tables(nx, True)

    def kernel(place_ref, *refs):
        table_refs, ins, out = refs[:4], refs[4:-2], refs[-1]
        me = place_ref[1]
        found = side_by_side(x_inverse, [ref[...] for ref in table_refs], [ref[0] for ref in ins])
        for s, value in enumerate(found):
            out[:, source(me, s, plan.gy), 0] = value.reshape(gx, x, y)

    return pl.pallas_call(
        kernel,
        grid=(plan.per,),
        in_specs=[scalars()]
        + [whole_block(table.shape) for table in tables]
        + [pl.BlockSpec((1, nx, y), lambda i: (i, 0, 0))] * plan.gy
        + [unread()],
        out_specs=pl.BlockSpec((gx, plan.gy, 1, x, y), lambda i: (0, 0, i, 0, 0)),
        out_shape=jax.ShapeDtypeStruct((gx, plan.gy, plan.per, x, y), jnp.float32),
        compiler_params=params(),
        cost_estimate=cost(plan.per * plan.ny * nx * nx, 2 * plan.per * plan.ny * nx),
        name="last_x_inverse",
    )(place, *[jnp.asarray(table) for table in tables], *blocks, ahead)


def pair_y_inverse(plan, place, planes, behind):
    x, y, ny = plan.x, plan.y, plan.ny
    count = planes.shape[0]
    table = halves(np.stack(np.split(inverse_basis(ny), plan.gy, axis=1)))
    deep = fit(count, Y_DEEP)
    rows = deep * x
    half = ny // 2

    def kernel(place_ref, table_ref, in_ref, _, *outs):
        plain = in_ref[...].reshape(rows, ny)
        wave = lax.broadcasted_iota(jnp.int32, (1, half), 1).astype(jnp.float32)
        along = jnp.concatenate([wave * plain[:, half:], -wave * plain[:, :half]], axis=1)
        found = pieces_of_y(plan, table_ref, place_ref[1], [along, plain])
        for comp, pieces in enumerate(found):
            for out, piece in zip(outs[:-1], pieces):
                out[comp] = piece.reshape(deep, x, y)

    return pl.pallas_call(
        kernel,
        grid=(count // deep,),
        in_specs=[
            scalars(),
            whole_block(table.shape),
            pl.BlockSpec((deep, x, ny), lambda i: (i, 0, 0)),
            unread(),
        ],
        out_specs=[pl.BlockSpec((2, deep, x, y), lambda i: (0, i, 0, 0))] * plan.gy + [unread()],
        out_shape=[jax.ShapeDtypeStruct((2, count, x, y), jnp.float32)] * plan.gy
        + [jax.ShapeDtypeStruct(behind.shape, behind.dtype)],
        input_output_aliases={3: plan.gy},
        compiler_params=params(),
        cost_estimate=cost(2 * count * x * ny * ny, 3 * count * x * ny),
        name="pair_y_inverse",
    )(place, jnp.asarray(table), planes, behind)


def source_sum(plan, velocity, source_s, ahead):
    x, y, z = plan.x, plan.y, plan.z
    group = fit(x, X_GROUP)

    def kernel(v_ref, s_ref, _, out):
        out[...] = sum(s_ref[i].astype(jnp.float32) * v_ref[i] for i in range(3))

    block = pl.BlockSpec((3, group, y, z), lambda i: (0, i, 0, 0))
    return pl.pallas_call(
        kernel,
        grid=(x // group,),
        in_specs=[block, block, unread()],
        out_specs=pl.BlockSpec((group, y, z), lambda i: (i, 0, 0)),
        out_shape=jax.ShapeDtypeStruct((x, y, z), jnp.float32),
        compiler_params=params(),
        cost_estimate=cost(x * y * z, 6 * x * y * z),
        name="source_sum",
    )(velocity, source_s, ahead)


def image_part(plan, place, comps, tables, blocks, fields, before, weight):
    x, y, z = plan.x, plan.y, plan.z
    outs = len(blocks)
    rows = z // outs
    table = np.stack([halves(table) for table in tables]).reshape(len(comps), 2, outs, rows, z)
    group = fit(x, LINE_GROUP)
    deep = fit(group, 2)

    def kernel(place_ref, table_ref, *refs):
        refs = list(refs)
        inputs = [[refs.pop(0) for _ in comps] for _ in fields]
        started = [refs.pop(0) for _ in before]
        *ins, image_s, image_p = refs
        ins = [ref.reshape(len(comps), rows * group, y) for ref in ins]
        order = [source(place_ref[1], s, outs) if outs > 1 else 0 for s in range(outs)]
        turned_tables = []
        for comp in range(len(comps)):
            parts = [joined([table_ref[comp, i, g] for g in order], 0) for i in range(2)]
            high, low = (part.astype(jnp.float32).T.astype(jnp.bfloat16) for part in parts)
            turned_tables.append((jnp.concatenate([high, high], axis=1), low))
        for plane in range(0, group, deep):
            here = slice(plane, plane + deep)
            total_s, total_p = ([ref[here] for ref in started] + [0.0])[:2]
            for comp, table in enumerate(turned_tables):
                p_ref, s_ref = (each[comp] for each in inputs)
                columns = []
                for k in range(deep):
                    cut = pl.ds(plane + k, rows, stride=group)
                    columns.append(joined([ref[comp, cut, :] for ref in ins], 0))
                field = left_times(table, joined(columns, 1)).T.reshape(deep, y, z)
                total_p += p_ref[0, here].astype(jnp.float32) * field
                total_s -= s_ref[0, here].astype(jnp.float32) * field
            image_s[here] = total_s
            image_p[here] = total_p

    def block(comp):
        return pl.BlockSpec((1, group, y, z), lambda i: (comp, i, 0, 0))

    blocks = [part.reshape(len(comps), rows, x, y) for part in blocks]
    image = pl.BlockSpec((group, y, z), lambda i: (i, 0, 0))
    return pl.pallas_call(
        kernel,
        grid=(x // group,),
        in_specs=[scalars(), whole_block(table.shape)]
        + [block(comp) for _ in fields for comp in comps]
        + [image] * len(before)
        + [pl.BlockSpec((len(comps), rows, group, y), lambda i: (0, 0, i, 0))] * outs,
        out_specs=[image, image],
        out_shape=[jax.ShapeDtypeStruct((x, y, z), jnp.float32)] * 2,
        compiler_params=params(),
        cost_estimate=cost(
            weight * len(comps) * x * y * z * z, weight * (2 + 3 * len(comps)) * x * y * z
        ),
        name="image_part",
    )(
        place,
        jnp.asarray(table),
        *[field for field in fields for _ in comps],
        *before,
        *blocks,
    )


def over_gx(blocks):
    return lax.all_to_all(blocks, "gx", 0, 0, tiled=True)


def separated(plan, place, velocity, source_p, source_s):
    x, y, z, gx, gy, per = plan.x, plan.y, plan.z, plan.gx, plan.gy, plan.per
    plain = basis(z)
    pair = along_z(plan, place, velocity, (1, 2), (plain, turned(plain)), gy)
    (first,) = along_z(plan, place, velocity, (0,), (crossed(plain, plan),), 1, pair[:1])
    first = over_gx(first.reshape(gx, gy, per, x, y))
    pair = pair_y_forward(plan, place, swap_gy(pair))
    pair = over_gx(pair.reshape(gx, per, x, plan.ny))
    first = first_y_forward(plan, place, swap_gy(first_x_forward(plan, place, first)))
    lines, slope = potential(plan, place, first, pair)
    pair = over_gx(lines)
    last = last_y_inverse(plan, place, slope)
    whole = source_sum(plan, velocity, source_s, last[0])
    last = last_x_inverse(plan, place, swap_gy(last), whole)
    *pair, last = pair_y_inverse(plan, place, pair.reshape(gx * per, x, plan.ny), last)
    pair = swap_gy(pair)
    last = over_gx(last)
    back = inverse_basis(z)
    fields = (source_p, source_s)
    found = image_part(plan, place, (1, 2), (back, -turned(back)), pair, fields, (whole,), WEIGHT)
    return image_part(plan, place, (0,), (crossed(back, plan),), [last], fields, found, 1)[::-1]


def shards(velocity, stress, lame_lambda, shear_modulus, buoyancy, source_p, source_s):
    place = jnp.stack([lax.axis_index("gx"), lax.axis_index("gy")]).astype(jnp.int32)
    velocity = propagate(place, velocity, stress, lame_lambda, shear_modulus, buoyancy)
    plan = Plan(velocity.shape[1:])
    if plan.z % (plan.gx * plan.gy) == 0:
        return tuple(separated(plan, place, velocity, source_p, source_s))
    blocks = z_forward(plan, place, velocity)
    lines = [to_lines(plan, y_forward(plan, place, swap_gy(group))) for group in blocks]
    lines = [x_lines(plan, place, part, chunk) for chunk, part in enumerate(lines)]
    blocks = [swap_gy(y_inverse(plan, place, to_planes(plan, part))) for part in lines]
    return tuple(images(plan, place, blocks, velocity, source_p, source_s))


def solution(mesh):
    in_specs = (
        P(None, "gx", "gy", None),
        P(None, "gx", "gy", None),
        P("gx", "gy", None),
        P("gx", "gy", None),
        P("gx", "gy", None),
        P(None, "gx", "gy", None),
        P(None, "gx", "gy", None),
    )
    out_specs = (P("gx", "gy", None), P("gx", "gy", None))
    return jax.shard_map(shards, mesh=mesh, in_specs=in_specs, out_specs=out_specs, check_vma=False)
```

```python
import numpy as np
import ml_dtypes
import jax
import jax.numpy as jnp
from jax import lax
from jax.experimental import pallas as pl
from jax.experimental.pallas import tpu as pltpu
from jax.sharding import PartitionSpec as P

STEPS = 2
MOST_CHUNKS = 1
VMEM_BYTES = 63 * 2**20
STENCIL_BYTES = 22 * 2**20
Y_DEEP = 32
Z_GROUP = 16
X_GROUP = 4
LINE_GROUP = 16
Y_TILE = 32
WEIGHT = 1000

time_step = 0.2


def passed_along(block, axis, distance):
    devices = range(lax.axis_size(axis))
    route = [(i - distance, i) for i in devices if i - distance in devices]
    return lax.ppermute(block, axis, route)


EDGE_ROWS = 8


def with_edges(place, rims, x_last, x_first):
    high, low = rims[-1], rims[0]
    count, z = high.shape[1:]
    some = fit(count, 8)
    lone = len(rims) == 1

    def kernel(place_ref, high_ref, low_ref, _, __, last_ref, first_ref):
        row = lax.broadcasted_iota(jnp.int32, (EDGE_ROWS, z), 0)
        me = place_ref[1]
        keep_high, keep_low = (me == 0, me == 1) if lone else (True, True)
        above = jnp.where(keep_high, high_ref[0, some - 1 :], 0.0)
        below = jnp.where(keep_low, low_ref[0, :1], 0.0)
        last_ref[...] = jnp.where(row == 0, above, 0.0)
        first_ref[...] = jnp.where(row == 0, below, 0.0)

    return pl.pallas_call(
        kernel,
        grid=(1,),
        in_specs=[
            scalars(),
            pl.BlockSpec((1, some, z), lambda i: (0, count // some - 1, 0)),
            pl.BlockSpec((1, some, z), lambda i: (1, 0, 0)),
            unread(),
            unread(),
        ],
        out_specs=[pl.BlockSpec((EDGE_ROWS, z), lambda i: (0, 0))] * 2,
        out_shape=[jax.ShapeDtypeStruct(edge.shape, jnp.float32) for edge in (x_last, x_first)],
        input_output_aliases={3: 0, 4: 1},
        compiler_params=params(4 * 2**20),
        name="with_edges",
    )(place, high, low, x_last, x_first)


def exchange(place, x_last, x_first, *y_outs):
    if len(y_outs) == 1:
        rims = (lax.ppermute(y_outs[0], "gy", [(0, 1), (1, 0)]),)
    else:
        rims = (passed_along(y_outs[0], "gy", 1), passed_along(y_outs[1], "gy", -1))
    x_last, x_first = with_edges(place, rims, x_last, x_first)
    return rims, (passed_along(x_last, "gx", 1), passed_along(x_first, "gx", -1))


def first_rims(brick, place, velocity, stress, lame, shear):
    x, y, z = brick
    some = fit(y, 8)
    many = fit(y, 16)
    swapped = lax.axis_size("gy") == 2

    def kernel(place_ref, *refs):
        (v_first, v_last, s_first, s_last, lame_first, shear_first, shear_last) = refs[:7]
        (v_low, v_high, s_low, s_high, lame_low, shear_low, shear_high) = refs[7:14]
        x_last, x_first, *y_outs = refs[14:]

        def wide(value):
            return value.astype(jnp.float32)

        lasts = [v_last[0, 0], v_last[1, 0], v_last[2, 0], s_last[3, 0], s_last[4, 0]]
        firsts = [v_first[0, 0], v_first[1, 0], v_first[2, 0], s_first[0, 0]]
        lasts += [wide(shear_last[0])]
        firsts += [wide(lame_first[0]), wide(shear_first[0])]
        for ref, values in ((x_last, lasts), (x_first, firsts)):
            ref[:EDGE_ROWS] = jnp.zeros((EDGE_ROWS, z), jnp.float32)
            for i, value in enumerate(values):
                ref[EDGE_ROWS + i * y : EDGE_ROWS + (i + 1) * y] = value
        lasts = [v_high[i, :, some - 1] for i in range(3)]
        firsts = [v_low[i, :, 0] for i in range(3)]
        lasts += [s_high[3, :, some - 1], s_high[5, :, some - 1], wide(shear_high[...])[:, many - 1]]
        firsts += [s_low[1, :, 0], wide(lame_low[...])[:, 0], wide(shear_low[...])[:, 0]]
        for i, (low, high) in enumerate(zip(lasts, firsts)):
            if swapped:
                y_outs[0][i] = jnp.where(place_ref[1] == 0, low, high)
            else:
                y_outs[0][i], y_outs[1][i] = low, high

    def plane(count, at):
        return pl.BlockSpec((count, 1, y, z), lambda i: (0, at, 0, 0))

    def medium_plane(at):
        return pl.BlockSpec((1, y, z), lambda i: (at, 0, 0))

    def rows(count, at):
        return pl.BlockSpec((count, x, some, z), lambda i: (0, 0, at, 0))

    def medium_rows(at):
        return pl.BlockSpec((x, many, z), lambda i: (0, at, 0))

    shapes = [(EDGE_ROWS + 6 * y, z)] * 2 + [(6, x, z)] * (1 if swapped else 2)
    ends, highs, most = x - 1, y // some - 1, y // many - 1
    return pl.pallas_call(
        kernel,
        grid=(1,),
        in_specs=[scalars(), plane(3, 0), plane(3, ends), plane(6, 0), plane(6, ends)]
        + [medium_plane(0), medium_plane(0), medium_plane(ends)]
        + [rows(3, 0), rows(3, highs), rows(6, 0), rows(6, highs)]
        + [medium_rows(0), medium_rows(0), medium_rows(most)],
        out_specs=[whole_block(shape) for shape in shapes],
        out_shape=[jax.ShapeDtypeStruct(shape, jnp.float32) for shape in shapes],
        compiler_params=params(40 * 2**20),
        cost_estimate=pl.CostEstimate(
            flops=0, bytes_accessed=80 * (y + 8 * x) * z, transcendentals=0
        ),
        name="first_rims",
    )(
        place,
        *(velocity, velocity, stress, stress, lame, shear, shear),
        *(velocity, velocity, stress, stress, lame, shear, shear),
    )


def stencil(brick, place, state, rims, medium, x_rims, x_medium, done, last):
    x, y, z = brick
    velocity, stress, lame, shear, buoyancy = state
    group = fit(x, X_GROUP)
    groups = x // group
    tall = fit(y, Y_TILE)
    ends = x_rims is not None
    if ends:
        count, of = min(groups, 2), lambda i: i * (groups - 1)
    else:
        count, of = groups - 2, lambda i: i + 1
    f32 = jnp.float32
    swapped = len(rims) == 1

    def kernel(place_ref, *refs):
        refs = list(refs)
        me = place_ref[1]

        def take(number):
            taken = refs[:number]
            del refs[:number]
            return taken

        v_ref, s_ref, lame_ref, shear_ref, buoy_ref = take(5)
        v_next_ref, xx_next_ref, lame_next_ref, shear_next_ref = take(4)
        v_prior_ref, xy_prior_ref, xz_prior_ref, shear_prior_ref = take(4)
        y_rims = take(len(rims))
        y_medium = take(len(rims)) if medium else y_rims
        if ends:
            xl, xr = take(2)
            xl_medium, xr_medium = take(2) if medium else (xl, xr)
        given = take(len(done))
        new = take(1)[0]
        if not last:
            s_out = take(1)[0]
            y_outs = take(len(rims))
            if ends:
                x_last, x_first = take(2)
        carried, xx_after = take(2)
        s_new = take(1)[0] if last else s_out
        turn = pl.program_id(0)
        here_group = of(turn)
        at = here_group * group
        start, end = here_group == 0, here_group == groups - 1
        row = lax.broadcasted_iota(jnp.int32, (y, z), 0)
        lane = lax.broadcasted_iota(jnp.int32, (y, z), 1)

        def next_z(field):
            edge = lane[: field.shape[0]] == z - 1
            return jnp.where(edge, 0.0, pltpu.roll(field, z - 1, 1))

        def prior_z(field):
            edge = lane[: field.shape[0]] == 0
            return jnp.where(edge, 0.0, pltpu.roll(field, 1, 1))

        def next_y(field, rim):
            rows = field.shape[0]
            return jnp.where(row[:rows] == rows - 1, rim, pltpu.roll(field, rows - 1, 0))

        def prior_y(field, rim):
            return jnp.where(row[: field.shape[0]] == 0, rim, pltpu.roll(field, 1, 0))

        def wide(value):
            return value.astype(f32)

        def low(which, at, refs=y_rims):
            value = refs[0][which, pl.ds(at, 1), :]
            return jnp.where(me == 1, value, 0.0) if swapped else value

        def high(which, at, refs=y_rims):
            value = refs[-1][which, pl.ds(at, 1), :]
            return jnp.where(me == 0, value, 0.0) if swapped else value

        def low_after(at):
            if not ends:
                return low(1, at)
            return jnp.where(at == x, xr[:1], low(1, jnp.minimum(at, x - 1)))

        def high_before(at):
            if not ends:
                return high(0, at)
            return jnp.where(at < 0, xl[:1], high(0, jnp.maximum(at, 0)))

        def rows_of(ref, i, span=slice(0, y)):
            start = EDGE_ROWS + i * y
            return ref[start + span.start : start + span.stop]

        def begin(value, rim):
            return jnp.where(start, rim(), value) if ends else value

        def finish(value, rim):
            return jnp.where(end, rim(), value) if ends else value

        def fresh():
            shear_rim = begin(wide(shear_prior_ref[0]), lambda: rows_of(xl_medium, 5))
            vx, vy, vz = (begin(v_prior_ref[i, 0], lambda: rows_of(xl, i)) for i in range(3))
            xy = begin(xy_prior_ref[0, 0], lambda: rows_of(xl, 3))
            xz = begin(xz_prior_ref[0, 0], lambda: rows_of(xl, 4))
            pull = time_step * shear_rim
            carried[0] = vx
            carried[1] = xy + pull * ((next_y(vx, high_before(at - 1)) - vx) + (v_ref[1, 0] - vy))
            carried[2] = xz + pull * ((next_z(vx) - vx) + (v_ref[2, 0] - vz))

        if ends:
            fresh()
        else:
            pl.when(turn == 0)(fresh)
        if not last and done:

            @pl.when(turn == 0)
            def _():
                for out, value in zip(y_outs, given[2:]):
                    out[...] = value[...]

        def after(i, rows):
            return finish(v_next_ref[i, 0, rows], lambda: rows_of(xr, i, rows))

        spans = [slice(top, top + tall) for top in range(0, y, tall)]

        def row_before(span, field, rim):
            return rim() if span.start == 0 else field[span.start - 1 : span.start]

        def row_after(span, field, rim):
            return rim() if span.stop == y else field[span.stop : span.stop + 1]

        for k in range(group):
            here = at + k
            v_here = [v_ref.at[i, k] for i in range(3)]
            for span in spans:
                vx, vy, vz = (field[span] for field in v_here)
                vx_prior = carried[0, span] if k == 0 else v_ref[0, k - 1, span]
                vy_next = after(1, span) if k == group - 1 else v_ref[1, k + 1, span]
                vz_next = after(2, span) if k == group - 1 else v_ref[2, k + 1, span]
                vy_rim = row_before(span, v_here[1], lambda: low(1, here))
                vx_rim = row_after(span, v_here[0], lambda: high(0, here))
                vz_rim = row_after(span, v_here[2], lambda: high(2, here))
                lame_value, shear_value = wide(lame_ref[k, span]), wide(shear_ref[k, span])
                ex = vx - vx_prior
                ey = vy - prior_y(vy, vy_rim)
                ez = vz - prior_z(vz)
                swell = lame_value * (ex + ey + ez)
                double = 2.0 * shear_value
                pull = time_step * shear_value
                found = (
                    s_ref[0, k, span] + time_step * (swell + double * ex),
                    s_ref[1, k, span] + time_step * (swell + double * ey),
                    s_ref[2, k, span] + time_step * (swell + double * ez),
                    s_ref[3, k, span] + pull * ((next_y(vx, vx_rim) - vx) + (vy_next - vy)),
                    s_ref[4, k, span] + pull * ((next_z(vx) - vx) + (vz_next - vz)),
                    s_ref[5, k, span] + pull * ((next_z(vy) - vy) + (next_y(vz, vz_rim) - vz)),
                )
                for i, value in enumerate(found):
                    s_new[i, k, span] = value

        for span in spans:
            vx, vy, vz = (after(i, span) for i in range(3))
            vy_rim = (
                low_after(at + group)
                if span.start == 0
                else after(1, slice(span.start - 1, span.start))
            )
            ex = vx - v_ref[0, group - 1, span]
            ey = vy - prior_y(vy, vy_rim)
            ez = vz - prior_z(vz)
            lame_value = finish(wide(lame_next_ref[0, span]), lambda: rows_of(xr_medium, 4, span))
            shear_value = finish(wide(shear_next_ref[0, span]), lambda: rows_of(xr_medium, 5, span))
            xx_after[span] = finish(xx_next_ref[0, 0, span], lambda: rows_of(xr, 3, span)) + time_step * (
                lame_value * (ex + ey + ez) + 2.0 * shear_value * ex
            )

        for k in range(group):
            here = at + k
            v_here = [v_ref.at[i, k] for i in range(3)]
            vx_edge, vy_edge, vz_edge = v_here[0][:1], v_here[1][y - 1 :], v_here[2][:1]
            pull = time_step * low(5, here, y_medium)
            vy_rim, vz_rim = low(1, here), low(2, here)
            xy_rim = low(3, here) + pull * (
                (vx_edge - low(0, here)) + (low_after(here + 1) - vy_rim)
            )
            yz_rim = low(4, here) + pull * ((next_z(vy_rim) - vy_rim) + (vz_edge - vz_rim))
            vx_rim, vz_rim = high(0, here), high(2, here)
            ex = vx_rim - high_before(here - 1)
            ey = high(1, here) - vy_edge
            ez = vz_rim - prior_z(vz_rim)
            yy_rim = high(3, here) + time_step * (
                high(4, here, y_medium) * (ex + ey + ez) + 2.0 * high(5, here, y_medium) * ey
            )
            s_here = [s_new.at[i, k] for i in range(6)]
            for span in spans:
                xx, yy, zz, xy, xz, yz = (field[span] for field in s_here)
                xx_next = xx_after[span] if k == group - 1 else s_new[0, k + 1, span]
                xy_prior = carried[1, span] if k == 0 else s_new[3, k - 1, span]
                xz_prior = carried[2, span] if k == 0 else s_new[4, k - 1, span]
                xy_before = row_before(span, s_here[3], lambda: xy_rim)
                yz_before = row_before(span, s_here[5], lambda: yz_rim)
                yy_after = row_after(span, s_here[1], lambda: yy_rim)
                push = time_step * wide(buoy_ref[k, span])
                new[0, k, span] = v_ref[0, k, span] + push * (
                    (xx_next - xx) + (xy - prior_y(xy, xy_before)) + (xz - prior_z(xz))
                )
                new[1, k, span] = v_ref[1, k, span] + push * (
                    (xy - xy_prior) + (next_y(yy, yy_after) - yy) + (yz - prior_z(yz))
                )
                new[2, k, span] = v_ref[2, k, span] + push * (
                    (xz - xz_prior) + (yz - prior_y(yz, yz_before)) + (next_z(zz) - zz)
                )
            if last:
                continue
            lasts = [new[i, k, y - 1 :] for i in range(3)]
            lasts += [s_new[3, k, y - 1 :], s_new[5, k, y - 1 :]]
            firsts = [new[i, k, :1] for i in range(3)] + [s_new[1, k, :1]] * 2
            for i in range(5):
                spot = pl.ds(here, 1)
                if swapped:
                    y_outs[0][i, spot, :] = jnp.where(me == 0, lasts[i], firsts[i])
                else:
                    y_outs[0][i, spot, :], y_outs[1][i, spot, :] = lasts[i], firsts[i]

        if ends and not last:

            def edge(out, values):
                out[:EDGE_ROWS] = jnp.zeros((EDGE_ROWS, z), f32)
                for i, value in enumerate(values):
                    out[EDGE_ROWS + i * y : EDGE_ROWS + (i + 1) * y] = value

            @pl.when(start)
            def _():
                edge(x_first, [new[0, 0], new[1, 0], new[2, 0], s_new[0, 0]])

            @pl.when(end)
            def _():
                most = group - 1
                values = [new[i, most] for i in range(3)]
                edge(x_last, values + [s_new[3, most], s_new[4, most]])

        if not ends:
            carried[0] = v_ref[0, group - 1]
            carried[1] = s_new[3, group - 1]
            carried[2] = s_new[4, group - 1]

    def next_plane(i):
        return jnp.minimum((of(i) + 1) * group, x - 1)

    def prior_plane(i):
        return jnp.maximum(of(i) * group - 1, 0) if ends else group - 1

    def planes(number):
        return pl.BlockSpec((number, group, y, z), lambda i: (0, of(i), 0, 0))

    def one(number, which, place):
        return pl.BlockSpec((number, 1, y, z), lambda i: (which, place(i), 0, 0))

    def medium_one(place):
        return pl.BlockSpec((1, y, z), lambda i: (place(i), 0, 0))

    medium_block = pl.BlockSpec((group, y, z), lambda i: (of(i), 0, 0))
    args = [place, velocity, stress, lame, shear, buoyancy, velocity, stress, lame, shear]
    args += [velocity, stress, stress, shear, *rims, *medium]
    in_specs = [scalars(), planes(3), planes(6), medium_block, medium_block, medium_block]
    in_specs += [one(3, 0, next_plane), one(1, 0, next_plane)]
    in_specs += [medium_one(next_plane), medium_one(next_plane)]
    in_specs += [one(3, 0, prior_plane), one(1, 3, prior_plane), one(1, 4, prior_plane)]
    in_specs += [medium_one(prior_plane)]
    in_specs += [whole_block(rim.shape) for rim in (*rims, *medium)]
    if ends:
        args += [*x_rims, *x_medium]
        in_specs += [whole_block(rim.shape) for rim in (*x_rims, *x_medium)]
    aliases = {}
    for i, value in enumerate(done):
        if i < 2:
            aliases[len(args)] = i
        in_specs.append(unread() if i < 2 else whole_block(value.shape))
        args.append(value)
    out_shape = [(3, x, y, z)]
    out_specs = [planes(3)]
    if not last:
        out_shape += [(6, x, y, z)] + [(5, x, z)] * len(rims)
        out_specs += [planes(6)]
        if ends:
            out_shape += [(EDGE_ROWS + 5 * y, z), (EDGE_ROWS + 4 * y, z)]
        out_specs += [whole_block(shape) for shape in out_shape[2:]]
    part = (1 if ends else WEIGHT) * count * group * y * z
    return pl.pallas_call(
        kernel,
        grid=(count,),
        in_specs=in_specs,
        out_specs=out_specs,
        out_shape=[jax.ShapeDtypeStruct(shape, f32) for shape in out_shape],
        scratch_shapes=[pltpu.VMEM((3, y, z), f32), pltpu.VMEM((y, z), f32)]
        + ([pltpu.VMEM((6, group, y, z), f32)] if last else []),
        input_output_aliases=aliases,
        compiler_params=params(STENCIL_BYTES),
        cost_estimate=pl.CostEstimate(
            flops=80 * part, bytes_accessed=(54 if last else 78) * part, transcendentals=0
        ),
        name="stencil_ends" if ends else "stencil_middle",
    )(*args)


def propagate(place, velocity, stress, lame, shear, buoyancy):
    brick = velocity.shape[1:]
    between = brick[0] // fit(brick[0], X_GROUP) > 2
    rims, x_rims = exchange(place, *first_rims(brick, place, velocity, stress, lame, shear))
    held, medium, x_medium = (rims, x_rims), (), ()
    for step_index in range(STEPS):
        last = step_index == STEPS - 1
        state = (velocity, stress, lame, shear, buoyancy)
        done = []
        if between:
            done = stencil(brick, place, state, rims, medium, None, None, done, last)
        found = stencil(brick, place, state, rims, medium, x_rims, x_medium, done, last)
        velocity = found[0]
        if not last:
            _, stress, *y_outs, x_last, x_first = found
            rims, x_rims = exchange(place, x_last, x_first, *y_outs)
            medium, x_medium = held
    return velocity


def basis(length):
    half = length // 2
    wave = np.arange(half)
    place = np.arange(length)
    angle = (wave[:, None] * place[None, :] % length) * (2.0 * np.pi / length)
    cosine, sine = np.cos(angle), np.sin(angle)
    sine[0] = 1.0 - 2.0 * (place % 2)
    return np.concatenate([cosine, sine])


def waves_of(length):
    return np.tile(np.arange(length // 2, dtype=np.float64), 2)


def inverse_basis(length):
    weight = np.where(waves_of(length) == 0, 1.0, 2.0) / length
    return basis(length) * weight[:, None]


def turned(table):
    half = table.shape[0] // 2
    return np.concatenate([table[half:], -table[:half]]) * waves_of(table.shape[0])[:, None]


def halves(table):
    high = table.astype(ml_dtypes.bfloat16)
    low = (table - high.astype(np.float64)).astype(ml_dtypes.bfloat16)
    return np.stack([high, low])


def split(value):
    high = value.astype(jnp.bfloat16)
    return high, (value - high.astype(jnp.float32)).astype(jnp.bfloat16)


def dot(left, right, dims=((1,), (0,))):
    return lax.dot_general(left, right, (dims, ((), ())), preferred_element_type=jnp.float32)


def times(left, right):
    return dot(left[0], right[0]) + (dot(left[1], right[0]) + dot(left[0], right[1]))


def joined(pieces, axis):
    return pieces[0] if len(pieces) == 1 else jnp.concatenate(pieces, axis=axis)


def fit(length, most):
    size = min(length, most)
    while length % size:
        size -= 1
    return size


def params(limit=VMEM_BYTES):
    return pltpu.CompilerParams(vmem_limit_bytes=limit)


def whole_block(shape):
    return pl.BlockSpec(shape, lambda *_: (0,) * len(shape))


def scalars():
    return pl.BlockSpec(memory_space=pltpu.SMEM)


class Plan:
    def __init__(self, brick):
        self.x, self.y, self.z = brick
        self.gx, self.gy = lax.axis_size("gx"), lax.axis_size("gy")
        self.nx, self.ny = self.x * self.gx, self.y * self.gy
        chunks = MOST_CHUNKS
        while chunks > 1 and self.z % (chunks * self.gy * self.gx):
            chunks -= 1
        self.chunks = chunks
        self.kz = self.z // (chunks * self.gy)
        self.parts = max(1, self.gx // self.kz)
        self.per = max(1, self.kz // self.gx)
        self.ky = self.ny // self.parts


def source(me, step, count):
    return lax.rem(me - step + count, count)


def z_forward(plan, place, velocity):
    x, y, z, kz = plan.x, plan.y, plan.z, plan.kz
    table = np.stack([halves(basis(z)), halves(turned(basis(z)))])
    table = table.reshape(2, 2, plan.chunks, plan.gy, kz, z)
    count = plan.chunks * plan.gy

    group = fit(x, Z_GROUP)
    deep = fit(group, 2)

    def kernel(place_ref, table_ref, v_ref, *outs):
        at = pl.program_id(0) * group
        me = place_ref[1]
        order = [(c, lax.rem(me + s, plan.gy)) for c in range(plan.chunks) for s in range(plan.gy)]
        tables = []
        for kind in range(2):
            high, low = (joined([table_ref[kind, i, c, g] for c, g in order], 0) for i in range(2))
            tables.append((jnp.concatenate([high, high], axis=1), low))
        for comp in range(3):
            twice, low = tables[1 if comp == 2 else 0]
            for plane in range(0, group, deep):
                field = split(v_ref[comp, plane : plane + deep].reshape(deep * y, z))
                value = dot(twice, jnp.concatenate(field, axis=1), ((1,), (1,)))
                value += dot(low, field[0], ((1,), (1,)))
                for i, out in enumerate(outs):
                    for k in range(deep):
                        part = value[i * kz : (i + 1) * kz, k * y : (k + 1) * y]
                        out[comp, pl.ds(at + plane + k, kz, stride=x), :] = part

    outs = pl.pallas_call(
        kernel,
        grid=(x // group,),
        in_specs=[
            scalars(),
            whole_block(table.shape),
            pl.BlockSpec((3, group, y, z), lambda i: (0, i, 0, 0)),
        ],
        out_specs=[whole_block((3, kz * x, y))] * count,
        out_shape=[jax.ShapeDtypeStruct((3, kz * x, y), jnp.float32)] * count,
        compiler_params=params(),
        cost_estimate=pl.CostEstimate(
            flops=18 * x * y * z * z, bytes_accessed=24 * x * y * z, transcendentals=0
        ),
        name="z_forward",
    )(place, jnp.asarray(table), velocity)
    outs = [out.reshape(3, kz, x, y) for out in outs]
    return [outs[c * plan.gy : (c + 1) * plan.gy] for c in range(plan.chunks)]


def swap_gy(blocks):
    count = len(blocks)
    moved = [blocks[0]]
    for step in range(1, count):
        route = [(i, (i + step) % count) for i in range(count)]
        moved.append(lax.ppermute(blocks[step], "gy", route))
    return moved


def y_forward(plan, place, blocks):
    x, y, ny, kz = plan.x, plan.y, plan.ny, plan.kz
    table = halves(basis(ny).T).reshape(2, plan.gy, y, ny)
    deep = fit(kz, 8)
    rows = deep * x
    half = ny // 2
    aligned = y % 128 == 0

    def kernel(place_ref, table_ref, *refs):
        ins, out = refs[:-1], refs[-1]
        me = place_ref[1]
        groups = [source(me, step, plan.gy) for step in range(plan.gy)]
        tables = [(table_ref[0, g], table_ref[1, g]) for g in groups]
        if aligned:
            tables = [tuple(joined([t[i] for t in tables], 0) for i in range(2))]

        def moved(comp):
            fields = [ref[comp].reshape(rows, y) for ref in ins]
            if aligned:
                fields = [joined(fields, 1)]
            return sum(times(split(f), t) for f, t in zip(fields, tables))

        wave = lax.broadcasted_iota(jnp.int32, (1, half), 1).astype(jnp.float32)
        out[:, 0] = moved(0).reshape(deep, x, ny)
        along, rest = moved(1), moved(2)
        out[:, 1, :, :half] = (rest[:, :half] + wave * along[:, half:]).reshape(deep, x, half)
        out[:, 1, :, half:] = (rest[:, half:] - wave * along[:, :half]).reshape(deep, x, half)

    return pl.pallas_call(
        kernel,
        grid=(kz // deep,),
        in_specs=[scalars(), whole_block(table.shape)]
        + [pl.BlockSpec((3, deep, x, y), lambda i: (0, i, 0, 0))] * plan.gy,
        out_specs=pl.BlockSpec((deep, 2, x, ny), lambda i: (i, 0, 0, 0)),
        out_shape=jax.ShapeDtypeStruct((kz, 2, x, ny), jnp.float32),
        compiler_params=params(),
        cost_estimate=pl.CostEstimate(
            flops=18 * kz * x * ny * ny, bytes_accessed=20 * kz * x * ny, transcendentals=0
        ),
        name="y_forward",
    )(place, jnp.asarray(table), *blocks)


def to_lines(plan, planes):
    if plan.parts > 1:
        planes = planes.reshape(plan.kz, 2, plan.x, plan.parts, plan.ky).transpose(0, 3, 1, 2, 4)
    planes = planes.reshape(plan.gx, plan.per, 2, plan.x, plan.ky)
    return lax.all_to_all(planes, "gx", 0, 0, tiled=True)


def to_planes(plan, lines):
    planes = lax.all_to_all(lines, "gx", 0, 0, tiled=True)
    if plan.parts > 1:
        planes = planes.reshape(plan.kz, plan.parts, 2, plan.x, plan.ky).transpose(0, 2, 3, 1, 4)
    return planes.reshape(plan.kz, 2, plan.x, plan.ny)


def x_lines(plan, place, lines, chunk):
    x, nx, ny, ky, gx = plan.x, plan.nx, plan.ny, plan.ky, plan.gx
    forth = halves(basis(nx))
    back = halves(-inverse_basis(nx).T)
    lanes = 128 if ky % 128 == 0 else ky
    half = nx // 2
    aligned = lanes % 128 == 0

    def kernel(place_ref, forth_ref, back_ref, in_ref, out_ref):
        me_x, me_y = place_ref[0], place_ref[1]
        which, lane = pl.program_id(0), pl.program_id(1)

        def through(table_ref, pair):
            table = (table_ref[0], table_ref[1])
            if aligned:
                both = times(table, split(jnp.concatenate(pair, axis=1)))
                return both[:, :lanes], both[:, lanes:]
            return tuple(times(table, split(value)) for value in pair)

        pair = [in_ref[:, 0, i].reshape(nx, lanes) for i in range(2)]
        along, rest = through(forth_ref, pair)
        wave_x = lax.broadcasted_iota(jnp.int32, (half, lanes), 0).astype(jnp.float32)
        slot_y = lax.broadcasted_iota(jnp.int32, (1, lanes), 1) + (
            lane * lanes + lax.rem(me_x, plan.parts) * ky
        )
        wave_y = lax.rem(slot_y, ny // 2).astype(jnp.float32)
        slot_z = (chunk * plan.gy + me_y) * plan.kz + me_x // plan.parts * plan.per + which
        wave_z = lax.rem(slot_z, plan.z // 2).astype(jnp.float32)
        scale = 1.0 / jnp.maximum(wave_x * wave_x + (wave_y * wave_y + wave_z * wave_z), 1.0)
        cosine = (rest[:half] + wave_x * along[half:]) * scale
        sine = (rest[half:] - wave_x * along[:half]) * scale
        plain = jnp.concatenate([cosine, sine], axis=0)
        slope = jnp.concatenate([wave_x * sine, -wave_x * cosine], axis=0)
        for i, value in enumerate(through(back_ref, [slope, plain])):
            out_ref[:, 0, i] = value.reshape(gx, x, lanes)

    block = pl.BlockSpec((gx, 1, 2, x, lanes), lambda i, j: (0, i, 0, 0, j))
    return pl.pallas_call(
        kernel,
        grid=(plan.per, ky // lanes),
        in_specs=[scalars(), whole_block(forth.shape), whole_block(back.shape), block],
        out_specs=block,
        out_shape=jax.ShapeDtypeStruct(lines.shape, jnp.float32),
        compiler_params=params(),
        cost_estimate=pl.CostEstimate(
            flops=24 * plan.per * ky * nx * nx,
            bytes_accessed=16 * plan.per * ky * nx,
            transcendentals=0,
        ),
        name="x_lines",
    )(place, jnp.asarray(forth), jnp.asarray(back), lines)


def y_inverse(plan, place, planes):
    x, y, ny, kz = plan.x, plan.y, plan.ny, plan.kz
    table = np.stack(np.split(inverse_basis(ny), plan.gy, axis=1))
    table = halves(table)
    deep = fit(kz, 8)
    rows = deep * x
    half = ny // 2
    aligned = y % 128 == 0

    def kernel(place_ref, table_ref, in_ref, *outs):
        me = place_ref[1]
        groups = [lax.rem(me + step, plan.gy) for step in range(plan.gy)]
        tables = [(table_ref[0, g], table_ref[1, g]) for g in groups]
        slope = in_ref[:, 0].reshape(rows, ny)
        plain = in_ref[:, 1].reshape(rows, ny)
        wave = lax.broadcasted_iota(jnp.int32, (1, half), 1).astype(jnp.float32)
        along = jnp.concatenate([wave * plain[:, half:], -wave * plain[:, :half]], axis=1)
        for comp, value in enumerate((slope, along, plain)):
            parts = split(value)
            if aligned:
                table = tuple(joined([t[i] for t in tables], 1) for i in range(2))
                found = times(parts, table)
                pieces = [found[:, s * y : (s + 1) * y] for s in range(plan.gy)]
            else:
                pieces = [times(parts, t) for t in tables]
            for out, piece in zip(outs, pieces):
                out[comp] = piece.reshape(deep, x, y)

    return pl.pallas_call(
        kernel,
        grid=(kz // deep,),
        in_specs=[
            scalars(),
            whole_block(table.shape),
            pl.BlockSpec((deep, 2, x, ny), lambda i: (i, 0, 0, 0)),
        ],
        out_specs=[pl.BlockSpec((3, deep, x, y), lambda i: (0, i, 0, 0))] * plan.gy,
        out_shape=[jax.ShapeDtypeStruct((3, kz, x, y), jnp.float32)] * plan.gy,
        compiler_params=params(),
        cost_estimate=pl.CostEstimate(
            flops=18 * kz * x * ny * ny, bytes_accessed=20 * kz * x * ny, transcendentals=0
        ),
        name="y_inverse",
    )(place, jnp.asarray(table), planes)


def images(plan, place, blocks, velocity, source_p, source_s):
    x, y, z, kz = plan.x, plan.y, plan.z, plan.kz
    table = np.stack([halves(inverse_basis(z)), halves(-turned(inverse_basis(z)))])
    table = table.reshape(2, 2, plan.chunks, plan.gy, kz, z)
    blocks = [block.reshape(3, kz * x, y) for group in blocks for block in group]

    group = fit(x, Z_GROUP)
    deep = fit(group, 2)

    def kernel(place_ref, table_ref, v_ref, p_ref, s_ref, *refs):
        ins, (image_p, image_s) = refs[:-2], refs[-2:]
        at = pl.program_id(0) * group
        me = place_ref[1]
        order = [
            (chunk, source(me, step, plan.gy))
            for chunk in range(plan.chunks)
            for step in range(plan.gy)
        ]
        tables = []
        for kind in range(2):
            high, low = (joined([table_ref[kind, i, c, g] for c, g in order], 0) for i in range(2))
            high, low = (part.astype(jnp.float32).T.astype(jnp.bfloat16) for part in (high, low))
            tables.append((jnp.concatenate([high, high], axis=1), low))
        for plane in range(0, group, deep):
            here = slice(plane, plane + deep)
            total_p = total_s = 0.0
            for comp in range(3):
                twice, low = tables[1 if comp == 2 else 0]
                columns = [
                    joined([ref[comp, pl.ds(at + plane + k, kz, stride=x), :] for ref in ins], 0)
                    for k in range(deep)
                ]
                high, rest = split(joined(columns, 1))
                field = dot(twice, jnp.concatenate([high, rest], axis=0)) + dot(low, high)
                field = field.T.reshape(deep, y, z)
                total_p += p_ref[comp, here].astype(jnp.float32) * field
                total_s += s_ref[comp, here].astype(jnp.float32) * (v_ref[comp, here] - field)
            image_p[here] = total_p
            image_s[here] = total_s

    plane = pl.BlockSpec((3, group, y, z), lambda i: (0, i, 0, 0))
    image = pl.BlockSpec((group, y, z), lambda i: (i, 0, 0))
    return pl.pallas_call(
        kernel,
        grid=(x // group,),
        in_specs=[scalars(), whole_block(table.shape), plane, plane, plane]
        + [whole_block((3, kz * x, y))] * len(blocks),
        out_specs=[image, image],
        out_shape=[jax.ShapeDtypeStruct((x, y, z), jnp.float32)] * 2,
        compiler_params=params(),
        cost_estimate=pl.CostEstimate(
            flops=18 * x * y * z * z, bytes_accessed=44 * x * y * z, transcendentals=0
        ),
        name="images",
    )(place, jnp.asarray(table), velocity, source_p, source_s, *blocks)


def doubled(table, axis):
    high, low = halves(table)
    return np.concatenate([high, high], axis=axis), low


def left_times(table, value):
    high, low = split(value)
    return dot(table[0], jnp.concatenate([high, low], axis=0)) + dot(table[1], high)


def right_times(value, table):
    high, low = split(value)
    return dot(jnp.concatenate([high, low], axis=1), table[0]) + dot(high, table[1])


def odd_basis(length):
    wave = 2 * np.arange(length // 4) + 1
    angle = (wave[:, None] * np.arange(length // 2) % length) * (2.0 * np.pi / length)
    return np.concatenate([np.cos(angle), np.sin(angle)])


def x_tables(length, inverse):
    even, odd = basis(length // 2), odd_basis(length)
    if inverse:
        even, odd = -inverse_basis(length // 2).T / 2.0, -odd.T * (2.0 / length)
    return [*doubled(even, 1), *doubled(odd, 1)]


def x_forward(tables, value):
    half = value.shape[0] // 2
    even = left_times(tables[:2], value[:half] + value[half:])
    return jnp.concatenate([even, left_times(tables[2:], value[:half] - value[half:])], axis=0)


def x_inverse(tables, value):
    half = value.shape[0] // 2
    even = left_times(tables[:2], value[:half])
    odd = left_times(tables[2:], value[half:])
    return jnp.concatenate([even + odd, even - odd], axis=0)


def x_wave(length):
    slot = lax.broadcasted_iota(jnp.int32, (length, 1), 0)
    wave = 2 * lax.rem(slot, length // 4) + slot // (length // 2)
    return wave.astype(jnp.float32)


def slope_x(value):
    part = value.shape[0] // 4
    wave = x_wave(value.shape[0])
    swapped = [value[part : 2 * part], -value[:part], value[3 * part :], -value[2 * part : 3 * part]]
    return wave * jnp.concatenate(swapped, axis=0)


def side_by_side(through, tables, values):
    width = values[0].shape[1]
    if width % 128:
        return [through(tables, value) for value in values]
    both = through(tables, joined(values, 1))
    return [both[:, i * width : (i + 1) * width] for i in range(len(values))]


def cost(flops, values):
    return pl.CostEstimate(flops=6 * flops, bytes_accessed=4 * values, transcendentals=0)


def crossed(table, plan):
    shape = (plan.gy, plan.gx, plan.per, table.shape[-1])
    return table.reshape(shape).transpose(1, 0, 2, 3).reshape(table.shape)


def unread():
    return pl.BlockSpec(memory_space=pl.ANY)


def along_z(plan, place, velocity, comps, tables, outs, ahead=()):
    x, y, z = plan.x, plan.y, plan.z
    table = np.stack([halves(table) for table in tables]).reshape(len(comps), 2, outs, z // outs, z)
    group = fit(x, LINE_GROUP)
    deep = fit(group, 2)
    rows = z // outs

    def kernel(place_ref, table_ref, *refs):
        fields, found = refs[: len(comps)], refs[len(comps) + len(ahead) :]
        found = [out.reshape(len(comps), rows * group, y) for out in found]
        me = place_ref[1]
        order = [lax.rem(me + s, outs) if outs > 1 else 0 for s in range(outs)]
        for comp, field in enumerate(fields):
            high, low = (joined([table_ref[comp, i, g] for g in order], 0) for i in range(2))
            twice = jnp.concatenate([high, high], axis=1)
            for plane in range(0, group, deep):
                parts = split(field[0, plane : plane + deep].reshape(deep * y, z))
                value = dot(twice, jnp.concatenate(parts, axis=1), ((1,), (1,)))
                value += dot(low, parts[0], ((1,), (1,)))
                for i, out in enumerate(found):
                    for k in range(deep):
                        part = value[i * rows : (i + 1) * rows, k * y : (k + 1) * y]
                        out[comp, pl.ds(plane + k, rows, stride=group), :] = part

    def block(comp):
        return pl.BlockSpec((1, group, y, z), lambda i: (comp, i, 0, 0))

    shape = (len(comps), rows, x, y)
    return pl.pallas_call(
        kernel,
        grid=(x // group,),
        in_specs=[scalars(), whole_block(table.shape)]
        + [block(comp) for comp in comps]
        + [unread()] * len(ahead),
        out_specs=[pl.BlockSpec((len(comps), rows, group, y), lambda i: (0, 0, i, 0))] * outs,
        out_shape=[jax.ShapeDtypeStruct(shape, jnp.float32)] * outs,
        compiler_params=params(STENCIL_BYTES),
        cost_estimate=cost(len(comps) * x * y * z * z, 2 * len(comps) * x * y * z),
        name="along_z",
    )(place, jnp.asarray(table), *[velocity] * len(comps), *ahead)


def y_table(plan, table_ref, groups):
    tables = [(table_ref[0, g], table_ref[1, g]) for g in groups]
    if plan.y % 128 == 0:
        high, low = (joined([table[i] for table in tables], 0) for i in range(2))
        return [(jnp.concatenate([high, high], axis=0), low)]
    return [(jnp.concatenate([high, high], axis=0), low) for high, low in tables]


def over_y(fields, tables):
    if len(tables) == 1:
        fields = [joined(fields, 1)]
    return sum(right_times(field, table) for field, table in zip(fields, tables))


def pair_y_forward(plan, place, blocks):
    x, y, ny = plan.x, plan.y, plan.ny
    count = blocks[0].shape[1]
    table = halves(basis(ny).T).reshape(2, plan.gy, y, ny)
    deep = fit(count, Y_DEEP)
    rows = deep * x
    half = ny // 2

    def kernel(place_ref, table_ref, *refs):
        ins, out = refs[:-1], refs[-1]
        me = place_ref[1]
        tables = y_table(plan, table_ref, [source(me, s, plan.gy) for s in range(plan.gy)])
        along, rest = (
            over_y([ref[comp].reshape(rows, y) for ref in ins], tables) for comp in range(2)
        )
        wave = lax.broadcasted_iota(jnp.int32, (1, half), 1).astype(jnp.float32)
        out[:, :, :half] = (rest[:, :half] + wave * along[:, half:]).reshape(deep, x, half)
        out[:, :, half:] = (rest[:, half:] - wave * along[:, :half]).reshape(deep, x, half)

    return pl.pallas_call(
        kernel,
        grid=(count // deep,),
        in_specs=[scalars(), whole_block(table.shape)]
        + [pl.BlockSpec((2, deep, x, y), lambda i: (0, i, 0, 0))] * plan.gy,
        out_specs=pl.BlockSpec((deep, x, ny), lambda i: (i, 0, 0)),
        out_shape=jax.ShapeDtypeStruct((count, x, ny), jnp.float32),
        compiler_params=params(),
        cost_estimate=cost(2 * WEIGHT * count * x * ny * ny, 3 * WEIGHT * count * x * ny),
        name="pair_y_forward",
    )(place, jnp.asarray(table), *blocks)


def first_x_forward(plan, place, lines):
    x, y, nx = plan.x, plan.y, plan.nx
    tables = x_tables(nx, False)

    def kernel(place_ref, *refs):
        table_refs, in_ref, outs = refs[:4], refs[4], refs[5:]
        me = place_ref[1]
        fields = [in_ref[:, lax.rem(me + s, plan.gy), 0].reshape(nx, y) for s in range(plan.gy)]
        found = side_by_side(x_forward, [ref[...] for ref in table_refs], fields)
        for out, value in zip(outs, found):
            out[0] = value

    return pl.pallas_call(
        kernel,
        grid=(plan.per,),
        in_specs=[scalars()]
        + [whole_block(table.shape) for table in tables]
        + [pl.BlockSpec((plan.gx, plan.gy, 1, x, y), lambda i: (0, 0, i, 0, 0))],
        out_specs=[pl.BlockSpec((1, nx, y), lambda i: (i, 0, 0))] * plan.gy,
        out_shape=[jax.ShapeDtypeStruct((plan.per, nx, y), jnp.float32)] * plan.gy,
        compiler_params=params(),
        cost_estimate=cost(plan.per * plan.ny * nx * nx, 2 * plan.per * plan.ny * nx),
        name="first_x_forward",
    )(place, *[jnp.asarray(table) for table in tables], lines)


def first_y_forward(plan, place, blocks):
    y, nx, ny = plan.y, plan.nx, plan.ny
    table = halves(basis(ny).T).reshape(2, plan.gy, y, ny)

    def kernel(place_ref, table_ref, *refs):
        ins, out = refs[:-1], refs[-1]
        me = place_ref[1]
        tables = y_table(plan, table_ref, [source(me, s, plan.gy) for s in range(plan.gy)])
        out[0] = slope_x(over_y([ref[0] for ref in ins], tables))

    return pl.pallas_call(
        kernel,
        grid=(plan.per,),
        in_specs=[scalars(), whole_block(table.shape)]
        + [pl.BlockSpec((1, nx, y), lambda i: (i, 0, 0))] * plan.gy,
        out_specs=pl.BlockSpec((1, nx, ny), lambda i: (i, 0, 0)),
        out_shape=jax.ShapeDtypeStruct((plan.per, nx, ny), jnp.float32),
        compiler_params=params(),
        cost_estimate=cost(plan.per * nx * ny * ny, 2 * plan.per * nx * ny),
        name="first_y_forward",
    )(place, jnp.asarray(table), *blocks)


def potential(plan, place, first, lines):
    x, nx, ny, gx = plan.x, plan.nx, plan.ny, plan.gx
    tables = x_tables(nx, False) + x_tables(nx, True)

    def kernel(place_ref, *refs):
        first_ref, in_ref, out_ref, slope_ref = refs[8:]
        forth, back = ([ref[...] for ref in refs[i : i + 4]] for i in (0, 4))
        me_x, me_y = place_ref[0], place_ref[1]
        total = x_forward(forth, in_ref[:, 0].reshape(nx, ny)) + first_ref[0]
        wave_x = x_wave(nx)
        slot_y = lax.broadcasted_iota(jnp.int32, (1, ny), 1)
        wave_y = lax.rem(slot_y, ny // 2).astype(jnp.float32)
        slot_z = (me_y * gx + me_x) * plan.per + pl.program_id(0)
        wave_z = lax.rem(slot_z, plan.z // 2).astype(jnp.float32)
        square = wave_x * wave_x + (wave_y * wave_y + wave_z * wave_z)
        found = total / jnp.maximum(square, 1.0)
        out_ref[:, 0] = x_inverse(back, found).reshape(gx, x, ny)
        slope_ref[0] = slope_x(found)

    spectrum = pl.BlockSpec((1, nx, ny), lambda i: (i, 0, 0))
    block = pl.BlockSpec((gx, 1, x, ny), lambda i: (0, i, 0, 0))
    return pl.pallas_call(
        kernel,
        grid=(plan.per,),
        in_specs=[scalars()] + [whole_block(t.shape) for t in tables] + [spectrum, block],
        out_specs=[block, spectrum],
        out_shape=[
            jax.ShapeDtypeStruct(lines.shape, jnp.float32),
            jax.ShapeDtypeStruct((plan.per, nx, ny), jnp.float32),
        ],
        compiler_params=params(),
        cost_estimate=cost(2 * plan.per * ny * nx * nx, 4 * plan.per * ny * nx),
        name="potential",
    )(place, *[jnp.asarray(t) for t in tables], first, lines)


def pieces_of_y(plan, table_ref, me, values):
    groups = [lax.rem(me + s, plan.gy) for s in range(plan.gy)]
    y = plan.y
    tables = [(table_ref[0, g], table_ref[1, g]) for g in groups]
    if y % 128 == 0:
        tables = [tuple(joined([table[i] for table in tables], 1) for i in range(2))]
    tables = [(jnp.concatenate([high, high], axis=0), low) for high, low in tables]
    found = []
    for value in values:
        pieces = [right_times(value, table) for table in tables]
        if y % 128 == 0:
            pieces = [pieces[0][:, s * y : (s + 1) * y] for s in range(plan.gy)]
        found.append(pieces)
    return found


def last_y_inverse(plan, place, slope):
    y, nx, ny = plan.y, plan.nx, plan.ny
    table = halves(np.stack(np.split(inverse_basis(ny), plan.gy, axis=1)))

    def kernel(place_ref, table_ref, in_ref, *outs):
        (pieces,) = pieces_of_y(plan, table_ref, place_ref[1], [in_ref[0]])
        for out, piece in zip(outs, pieces):
            out[0] = piece

    return pl.pallas_call(
        kernel,
        grid=(plan.per,),
        in_specs=[
            scalars(),
            whole_block(table.shape),
            pl.BlockSpec((1, nx, ny), lambda i: (i, 0, 0)),
        ],
        out_specs=[pl.BlockSpec((1, nx, y), lambda i: (i, 0, 0))] * plan.gy,
        out_shape=[jax.ShapeDtypeStruct((plan.per, nx, y), jnp.float32)] * plan.gy,
        compiler_params=params(),
        cost_estimate=cost(plan.per * nx * ny * ny, 2 * plan.per * nx * ny),
        name="last_y_inverse",
    )(place, jnp.asarray(table), slope)


def last_x_inverse(plan, place, blocks, ahead):
    x, y, nx, gx = plan.x, plan.y, plan.nx, plan.gx
    tables = x_tables(nx, True)

    def kernel(place_ref, *refs):
        table_refs, ins, out = refs[:4], refs[4:-2], refs[-1]
        me = place_ref[1]
        found = side_by_side(x_inverse, [ref[...] for ref in table_refs], [ref[0] for ref in ins])
        for s, value in enumerate(found):
            out[:, source(me, s, plan.gy), 0] = value.reshape(gx, x, y)

    return pl.pallas_call(
        kernel,
        grid=(plan.per,),
        in_specs=[scalars()]
        + [whole_block(table.shape) for table in tables]
        + [pl.BlockSpec((1, nx, y), lambda i: (i, 0, 0))] * plan.gy
        + [unread()],
        out_specs=pl.BlockSpec((gx, plan.gy, 1, x, y), lambda i: (0, 0, i, 0, 0)),
        out_shape=jax.ShapeDtypeStruct((gx, plan.gy, plan.per, x, y), jnp.float32),
        compiler_params=params(),
        cost_estimate=cost(plan.per * plan.ny * nx * nx, 2 * plan.per * plan.ny * nx),
        name="last_x_inverse",
    )(place, *[jnp.asarray(table) for table in tables], *blocks, ahead)


def pair_y_inverse(plan, place, planes, behind):
    x, y, ny = plan.x, plan.y, plan.ny
    count = planes.shape[0]
    table = halves(np.stack(np.split(inverse_basis(ny), plan.gy, axis=1)))
    deep = fit(count, Y_DEEP)
    rows = deep * x
    half = ny // 2

    def kernel(place_ref, table_ref, in_ref, _, *outs):
        plain = in_ref[...].reshape(rows, ny)
        wave = lax.broadcasted_iota(jnp.int32, (1, half), 1).astype(jnp.float32)
        along = jnp.concatenate([wave * plain[:, half:], -wave * plain[:, :half]], axis=1)
        found = pieces_of_y(plan, table_ref, place_ref[1], [along, plain])
        for comp, pieces in enumerate(found):
            for out, piece in zip(outs[:-1], pieces):
                out[comp] = piece.reshape(deep, x, y)

    return pl.pallas_call(
        kernel,
        grid=(count // deep,),
        in_specs=[
            scalars(),
            whole_block(table.shape),
            pl.BlockSpec((deep, x, ny), lambda i: (i, 0, 0)),
            unread(),
        ],
        out_specs=[pl.BlockSpec((2, deep, x, y), lambda i: (0, i, 0, 0))] * plan.gy + [unread()],
        out_shape=[jax.ShapeDtypeStruct((2, count, x, y), jnp.float32)] * plan.gy
        + [jax.ShapeDtypeStruct(behind.shape, behind.dtype)],
        input_output_aliases={3: plan.gy},
        compiler_params=params(),
        cost_estimate=cost(2 * count * x * ny * ny, 3 * count * x * ny),
        name="pair_y_inverse",
    )(place, jnp.asarray(table), planes, behind)


def source_sum(plan, velocity, source_s, ahead):
    x, y, z = plan.x, plan.y, plan.z
    group = fit(x, X_GROUP)

    def kernel(v_ref, s_ref, _, out):
        out[...] = sum(s_ref[i].astype(jnp.float32) * v_ref[i] for i in range(3))

    block = pl.BlockSpec((3, group, y, z), lambda i: (0, i, 0, 0))
    return pl.pallas_call(
        kernel,
        grid=(x // group,),
        in_specs=[block, block, unread()],
        out_specs=pl.BlockSpec((group, y, z), lambda i: (i, 0, 0)),
        out_shape=jax.ShapeDtypeStruct((x, y, z), jnp.float32),
        compiler_params=params(),
        cost_estimate=cost(x * y * z, 6 * x * y * z),
        name="source_sum",
    )(velocity, source_s, ahead)


def image_part(plan, place, comps, tables, blocks, fields, before, weight):
    x, y, z = plan.x, plan.y, plan.z
    outs = len(blocks)
    rows = z // outs
    table = np.stack([halves(table) for table in tables]).reshape(len(comps), 2, outs, rows, z)
    group = fit(x, LINE_GROUP)
    deep = fit(group, 2)

    def kernel(place_ref, table_ref, *refs):
        refs = list(refs)
        inputs = [[refs.pop(0) for _ in comps] for _ in fields]
        started = [refs.pop(0) for _ in before]
        *ins, image_s, image_p = refs
        ins = [ref.reshape(len(comps), rows * group, y) for ref in ins]
        order = [source(place_ref[1], s, outs) if outs > 1 else 0 for s in range(outs)]
        turned_tables = []
        for comp in range(len(comps)):
            parts = [joined([table_ref[comp, i, g] for g in order], 0) for i in range(2)]
            high, low = (part.astype(jnp.float32).T.astype(jnp.bfloat16) for part in parts)
            turned_tables.append((jnp.concatenate([high, high], axis=1), low))
        for plane in range(0, group, deep):
            here = slice(plane, plane + deep)
            total_s, total_p = ([ref[here] for ref in started] + [0.0])[:2]
            for comp, table in enumerate(turned_tables):
                p_ref, s_ref = (each[comp] for each in inputs)
                columns = []
                for k in range(deep):
                    cut = pl.ds(plane + k, rows, stride=group)
                    columns.append(joined([ref[comp, cut, :] for ref in ins], 0))
                field = left_times(table, joined(columns, 1)).T.reshape(deep, y, z)
                total_p += p_ref[0, here].astype(jnp.float32) * field
                total_s -= s_ref[0, here].astype(jnp.float32) * field
            image_s[here] = total_s
            image_p[here] = total_p

    def block(comp):
        return pl.BlockSpec((1, group, y, z), lambda i: (comp, i, 0, 0))

    blocks = [part.reshape(len(comps), rows, x, y) for part in blocks]
    image = pl.BlockSpec((group, y, z), lambda i: (i, 0, 0))
    return pl.pallas_call(
        kernel,
        grid=(x // group,),
        in_specs=[scalars(), whole_block(table.shape)]
        + [block(comp) for _ in fields for comp in comps]
        + [image] * len(before)
        + [pl.BlockSpec((len(comps), rows, group, y), lambda i: (0, 0, i, 0))] * outs,
        out_specs=[image, image],
        out_shape=[jax.ShapeDtypeStruct((x, y, z), jnp.float32)] * 2,
        compiler_params=params(),
        cost_estimate=cost(
            weight * len(comps) * x * y * z * z, weight * (2 + 3 * len(comps)) * x * y * z
        ),
        name="image_part",
    )(
        place,
        jnp.asarray(table),
        *[field for field in fields for _ in comps],
        *before,
        *blocks,
    )


def over_gx(blocks):
    return lax.all_to_all(blocks, "gx", 0, 0, tiled=True)


def separated(plan, place, velocity, source_p, source_s):
    x, y, z, gx, gy, per = plan.x, plan.y, plan.z, plan.gx, plan.gy, plan.per
    plain = basis(z)
    pair = along_z(plan, place, velocity, (1, 2), (plain, turned(plain)), gy)
    (first,) = along_z(plan, place, velocity, (0,), (crossed(plain, plan),), 1, pair[:1])
    first = over_gx(first.reshape(gx, gy, per, x, y))
    pair = pair_y_forward(plan, place, swap_gy(pair))
    pair = over_gx(pair.reshape(gx, per, x, plan.ny))
    first = first_y_forward(plan, place, swap_gy(first_x_forward(plan, place, first)))
    lines, slope = potential(plan, place, first, pair)
    pair = over_gx(lines)
    last = last_y_inverse(plan, place, slope)
    whole = source_sum(plan, velocity, source_s, last[0])
    last = last_x_inverse(plan, place, swap_gy(last), whole)
    *pair, last = pair_y_inverse(plan, place, pair.reshape(gx * per, x, plan.ny), last)
    pair = swap_gy(pair)
    last = over_gx(last)
    back = inverse_basis(z)
    fields = (source_p, source_s)
    found = image_part(plan, place, (1, 2), (back, -turned(back)), pair, fields, (whole,), WEIGHT)
    return image_part(plan, place, (0,), (crossed(back, plan),), [last], fields, found, 1)[::-1]


def shards(velocity, stress, lame_lambda, shear_modulus, buoyancy, source_p, source_s):
    place = jnp.stack([lax.axis_index("gx"), lax.axis_index("gy")]).astype(jnp.int32)
    velocity = propagate(place, velocity, stress, lame_lambda, shear_modulus, buoyancy)
    plan = Plan(velocity.shape[1:])
    if plan.z % (plan.gx * plan.gy) == 0:
        return tuple(separated(plan, place, velocity, source_p, source_s))
    blocks = z_forward(plan, place, velocity)
    lines = [to_lines(plan, y_forward(plan, place, swap_gy(group))) for group in blocks]
    lines = [x_lines(plan, place, part, chunk) for chunk, part in enumerate(lines)]
    blocks = [swap_gy(y_inverse(plan, place, to_planes(plan, part))) for part in lines]
    return tuple(images(plan, place, blocks, velocity, source_p, source_s))


def solution(mesh):
    in_specs = (
        P(None, "gx", "gy", None),
        P(None, "gx", "gy", None),
        P("gx", "gy", None),
        P("gx", "gy", None),
        P("gx", "gy", None),
        P(None, "gx", "gy", None),
        P(None, "gx", "gy", None),
    )
    out_specs = (P("gx", "gy", None), P("gx", "gy", None))
    return jax.shard_map(shards, mesh=mesh, in_specs=in_specs, out_specs=out_specs, check_vma=False)
```
